32 devices in a mesh: ulys: 4 (over z), blk: 8 (over y, x, core).
Axes of the slice: x: 2, y: 2, z: 4, core: 2. Of those that a mesh axis runs over, the one named last changes fastest.
Arguments:
- target: bfloat16 [4, 1024, 1024], P('ulys', 'blk'), may hold values from -6 to 6
- source: bfloat16 [4, 1024, 1024], P('ulys', 'blk'), may hold values from -6 to 6
- cotangent: bfloat16 [4, 1024, 1024], P('ulys', 'blk'), may hold values from -6 to 6
- target_lengths: int32 [4, 3], replicated, may hold values from 16 to 992, as said below
- source_lengths: int32 [4, 3], replicated, may hold values from 16 to 992, as said below
- self_in: bfloat16 [1024, 3072], P(('ulys', 'blk')), may hold values from -0.1875 to 0.1875
- self_out: bfloat16 [1024, 1024], P(('ulys', 'blk')), may hold values from -0.75 to 0.75
- cross_query: bfloat16 [1024, 1024], P(('ulys', 'blk')), may hold values from -0.1875 to 0.1875
- cross_kv: bfloat16 [1024, 2048], P(('ulys', 'blk')), may hold values from -0.1875 to 0.1875
- cross_out: bfloat16 [1024, 1024], P(('ulys', 'blk')), may hold values from -0.75 to 0.75
- mlp_in: bfloat16 [1024, 8192], P(('ulys', 'blk')), may hold values from -0.1875 to 0.1875
- mlp_out: bfloat16 [8192, 1024], P(('ulys', 'blk')), may hold values from -0.0625 to 0.0625
- vectors: bfloat16 [13, 1024], P(None, ('ulys', 'blk')), may hold values from -1.5 to 1.5, as said below
- hidden_bias: bfloat16 [8192], P(('ulys', 'blk')), may hold values from -2.5 to 2.5
Outputs:
- layer_out: bfloat16 [4, 1024, 1024], P('ulys', 'blk')
- target_grad: bfloat16 [4, 1024, 1024], P('ulys', 'blk')
- source_grad: bfloat16 [4, 1024, 1024], P('ulys', 'blk')
- self_in_grad: float32 [1024, 3072], P(('ulys', 'blk'))
- self_out_grad: float32 [1024, 1024], P(('ulys', 'blk'))
- cross_query_grad: float32 [1024, 1024], P(('ulys', 'blk'))
- cross_kv_grad: float32 [1024, 2048], P(('ulys', 'blk'))
- cross_out_grad: float32 [1024, 1024], P(('ulys', 'blk'))
- mlp_in_grad: float32 [1024, 8192], P(('ulys', 'blk'))
- mlp_out_grad: float32 [8192, 1024], P(('ulys', 'blk'))
- vectors_grad: float32 [13, 1024], P(None, ('ulys', 'blk'))
- hidden_bias_grad: float32 [8192], P(('ulys', 'blk'))
The draws below stay inside these ranges and needn't reach their ends.
Inputs may be any that keep to these rules, and one draw needn't show every extreme that they name: `target_lengths`: each row sums to 1024; its first and last documents have 16 to 127 positions each, the middle one the rest; in one stream both ends have exactly 16, in another the first has exactly 127. `source_lengths`: each row sums to 1024; its first and last documents have 16 to 127 positions each, the middle one the rest; in one stream both ends have exactly 16, in another the first has exactly 127. `vectors`: rows 0, 2 and 4 lie between 0.5 and 1.5.
All inputs are finite; a program needn't handle non-finite values.
Results may differ from the reference program's by a relative error of at most 0.019.
Values may be sent and summed in bfloat16 or wider, within the bound.
No kernel may reach another device: no remote copies, remote signals or barrier semaphores. Data moves between devices by JAX's collectives and lax.ppermute only.
A program may use at most 448 MiB of HBM per device.

```python
import jax
import jax.numpy as jnp
from jax import lax

D = 1024
HEADS = 16
FF = 8192
TOK_DEV = 128
EDGE = 16
HD = 64
STREAMS = 4
SPAN = 1024
N_BLK = 8


def chosen_stream(key):
    return jax.random.randint(key, (), 0, STREAMS).astype(jnp.int32)


def edge_table(key, chosen):
    first_key, last_key = jax.random.split(key)
    firsts = jax.random.randint(first_key, (STREAMS,), EDGE, TOK_DEV).astype(jnp.int32)
    lasts = jax.random.randint(last_key, (STREAMS,), EDGE, TOK_DEV).astype(jnp.int32)
    streams = jnp.arange(STREAMS, dtype=jnp.int32)
    firsts = jnp.where(streams == chosen, EDGE, firsts)
    lasts = jnp.where(streams == chosen, EDGE, lasts)
    firsts = jnp.where(streams == (chosen + 1) % STREAMS, TOK_DEV - 1, firsts)
    middle = SPAN - firsts - lasts
    return jnp.stack([firsts, middle, lasts], axis=1).astype(jnp.int32)


def draw_target_lengths(key, part):
    chosen = chosen_stream(key)
    key = jax.random.fold_in(key, 21)
    return edge_table(key, chosen)


def draw_source_lengths(key, part):
    chosen = chosen_stream(key)
    key = jax.random.fold_in(key, 22)
    return edge_table(key, chosen)


def draw_vectors(key, part):
    key = jax.random.fold_in(key, 13)
    gain_key, shift_key = jax.random.split(key)
    row_index = jnp.arange(13)[:, None]
    is_gain = (row_index == 0) | (row_index == 2) | (row_index == 4)
    gains = jax.random.uniform(gain_key, (13, D), jnp.float32, 0.5, 1.5)
    shifts = jnp.clip(0.5 * jax.random.normal(shift_key, (13, D), jnp.float32), -1.5, 1.5)
    return jnp.where(is_gain, gains, shifts).astype(jnp.bfloat16)


def block_scale(key, shape, cuts, low, top_value):
    def one(axis_at, parts):
        steps = jax.random.uniform(jax.random.fold_in(jax.random.fold_in(key, 6), axis_at), (parts,), jnp.float32, low / len(cuts), top_value / len(cuts))
        return jnp.repeat(jnp.exp(steps), shape[axis_at] // parts).reshape((-1,) + (1,) * (len(shape) - axis_at - 1))

    level = one(*cuts[0])
    for cut in cuts[1:]:
        level = level * one(*cut)
    return level


def bell_draw(own_key, dims, deviation, reach, pieces=(), kind=jnp.bfloat16):
    factor_of = block_scale(own_key, dims, pieces, -0.22, 0.18) if pieces else 1.0
    drawn = jax.random.normal(own_key, dims, jnp.float32) * deviation * factor_of
    return jnp.minimum(jnp.maximum(drawn, -reach), reach).astype(kind)


def setup_inputs(seed: int = 0) -> dict:
    key_of = jax.random.split(jax.random.key(seed), 15)
    target = bell_draw(key_of[0], (STREAMS, SPAN, D), 1.0, 6.0, ((0, 4), (1, 8)))
    source = bell_draw(key_of[1], (STREAMS, SPAN, D), 1.0, 6.0, ((0, 4), (1, 8)))
    cotangent = bell_draw(key_of[2], (STREAMS, SPAN, D), 1.0, 6.0, ((0, 4), (1, 8)))
    target_lengths = draw_target_lengths(jax.random.fold_in(key_of[14], 71), 0)
    source_lengths = draw_source_lengths(jax.random.fold_in(key_of[14], 71), 0)
    self_in = bell_draw(key_of[5], (D, 3 * D), D ** -0.5, 0.1875, ((0, 32),))
    self_out = bell_draw(key_of[6], (D, D), (D // 16) ** -0.5, 0.75, ((0, 32),))
    cross_query = bell_draw(key_of[7], (D, D), D ** -0.5, 0.1875, ((0, 32),))
    cross_kv = bell_draw(key_of[8], (D, 2 * D), D ** -0.5, 0.1875, ((0, 32),))
    cross_out = bell_draw(key_of[9], (D, D), (D // 16) ** -0.5, 0.75, ((0, 32),))
    mlp_in = bell_draw(key_of[10], (D, FF), D ** -0.5, 0.1875, ((0, 32),))
    mlp_out = bell_draw(key_of[11], (FF, D), FF ** -0.5, 0.0625, ((0, 32),))
    vectors = draw_vectors(jax.random.fold_in(key_of[14], 71), 0)
    hidden_bias = bell_draw(key_of[13], (FF,), 0.5, 2.5, ((0, 32),))
    return dict(target=target, source=source, cotangent=cotangent, target_lengths=target_lengths, source_lengths=source_lengths, self_in=self_in, self_out=self_out, cross_query=cross_query, cross_kv=cross_kv, cross_out=cross_out, mlp_in=mlp_in, mlp_out=mlp_out, vectors=vectors, hidden_bias=hidden_bias)


@jax.custom_vjp
def low(v):
    return lax.optimization_barrier(v.astype(jnp.bfloat16)).astype(jnp.float32)

@jax.custom_vjp
def low_back(v):
    return v

def low_keep(v):
    return (low(v), None)

def low_pass(kept, grad):
    return (grad,)

def back_keep(v):
    return (v, None)

def back_low(kept, grad):
    return (low(grad),)
low.defvjp(low_keep, low_pass)
low_back.defvjp(back_keep, back_low)

def layer_norm(value, gain, shift):
    center = lax.optimization_barrier(jnp.mean(value, axis=-1, keepdims=True))
    centred = value - center
    spread = lax.optimization_barrier(jnp.mean(centred * centred, axis=-1, keepdims=True))
    return centred * lax.rsqrt(spread + 1e-05) * gain + shift

def linear(value, weight):
    return jnp.einsum('std,de->ste', value, weight, precision=lax.Precision.HIGHEST)

def rounded(value):
    return low(low_back(value))

def smooth(value):
    return jax.nn.gelu(value, approximate=True)

def segment_table(lengths, positions):
    ends = jnp.cumsum(lengths, axis=1).astype(jnp.int32)
    counts = lax.optimization_barrier(jnp.sum((ends[:, None, :] <= positions[None, :, None]).astype(jnp.int32), axis=-1))
    return counts.astype(jnp.int32)

def attend(queries, key_rows, value_rows, query_seg, key_seg, causal):
    key_all = key_rows.reshape(STREAMS, SPAN, HEADS, HD)
    value_all = value_rows.reshape(STREAMS, SPAN, HEADS, HD)
    scale = HD ** (-0.5)
    key_place = jnp.arange(SPAN, dtype=jnp.int32)[None, :]

    def one_block(block_index):
        first_row = (block_index * TOK_DEV).astype(jnp.int32)
        query_block = lax.dynamic_slice_in_dim(queries, first_row, TOK_DEV, 1).reshape(STREAMS, TOK_DEV, HEADS, HD)
        query_ids = lax.dynamic_slice_in_dim(query_seg, first_row, TOK_DEV, 1)
        allowed = query_ids[:, :, None] == key_seg[:, None, :]
        if causal:
            query_place = (first_row + jnp.arange(TOK_DEV, dtype=jnp.int32))[:, None]
            allowed = allowed & (key_place <= query_place)[None]
        scores = low_back(jnp.einsum('sqhd,skhd->shqk', query_block, key_all, precision=lax.Precision.HIGHEST) * scale)
        masked = jnp.where(allowed[:, None], scores, -1e+30)
        summit = lax.optimization_barrier(jnp.max(masked, axis=-1, keepdims=True))
        weights = jnp.where(allowed[:, None], jnp.exp(masked - summit), 0.0)
        probs = weights / lax.optimization_barrier(jnp.sum(weights, axis=-1, keepdims=True))
        result = jnp.einsum('shqk,skhd->sqhd', low(probs), value_all, precision=lax.Precision.HIGHEST)
        return result.reshape(STREAMS, TOK_DEV, D)
    blocks = lax.map(jax.checkpoint(one_block), jnp.arange(N_BLK, dtype=jnp.int32))
    return jnp.transpose(blocks, (1, 0, 2, 3)).reshape(STREAMS, SPAN, D)

def reference(target, source, cotangent, target_lengths, source_lengths, self_in, self_out, cross_query, cross_kv, cross_out, mlp_in, mlp_out, vectors, hidden_bias):
    positions = jnp.arange(SPAN, dtype=jnp.int32)
    query_seg = segment_table(target_lengths, positions)
    cross_keys = segment_table(source_lengths, positions)

    def forward(inputs, states, w_self, w_sout, w_query, w_pair, w_cout, w_first, w_second, params, h_bias):
        first_low = low(layer_norm(inputs, params[0], params[1]))
        projected = linear(first_low, w_self)
        queries = rounded(projected[..., :D] + params[6])
        key_rows = rounded(projected[..., D:2 * D])
        value_rows = rounded(projected[..., 2 * D:] + params[7])
        attended = rounded(attend(queries, key_rows, value_rows, query_seg, query_seg, True))
        middle = inputs + low_back(linear(attended, w_sout) + params[8])
        second_low = low(layer_norm(middle, params[2], params[3]))
        cross_q = rounded(linear(second_low, w_query) + params[9])
        pair = linear(states, w_pair)
        cross_k = rounded(pair[..., :D])
        cross_v = rounded(pair[..., D:] + params[10])
        crossed = rounded(attend(cross_q, cross_k, cross_v, query_seg, cross_keys, False))
        late = middle + low_back(linear(crossed, w_cout) + params[11])
        third_low = low(layer_norm(late, params[4], params[5]))
        before = low_back(linear(third_low, w_first) + h_bias)
        active = low(smooth(before))
        return late + low_back(linear(active, w_second) + params[12])
    floats = (target.astype(jnp.float32), source.astype(jnp.float32), self_in.astype(jnp.float32), self_out.astype(jnp.float32), cross_query.astype(jnp.float32), cross_kv.astype(jnp.float32), cross_out.astype(jnp.float32), mlp_in.astype(jnp.float32), mlp_out.astype(jnp.float32), vectors.astype(jnp.float32), hidden_bias.astype(jnp.float32))
    result, pull = jax.vjp(forward, *floats)
    grads = pull(cotangent.astype(jnp.float32))
    return (result.astype(jnp.bfloat16), grads[0].astype(jnp.bfloat16), grads[1].astype(jnp.bfloat16), grads[2], grads[3], grads[4], grads[5], grads[6], grads[7], grads[8], grads[9], grads[10])
```

```python
import functools

import jax
import jax.numpy as jnp
from jax import lax
from jax.experimental import pallas as pl
from jax.experimental.pallas import tpu as pltpu
from jax.sharding import Mesh
from jax.sharding import PartitionSpec as P

HEADS = 16
LOW = jnp.bfloat16
WIDE = jnp.float32
INNER = 8
STEP = 256


def offset_of(place):
    return ((place & 3) << 1) | (place >> 2)


def dot_t(a, b):
    return lax.dot_general(a, b, (((1,), (1,)), ((), ())), preferred_element_type=WIDE)


def dot_n(a, b):
    return lax.dot_general(a, b, (((1,), (0,)), ((), ())), preferred_element_type=WIDE)


def dot_c(a, b):
    return lax.dot_general(a, b, (((0,), (0,)), ((), ())), preferred_element_type=WIDE)


def seg_of(position, table, first):
    count = jnp.zeros_like(position)
    for n in range(3):
        count = count + (table[first + n] <= position).astype(jnp.int32)
    return count


def iota(shape, axis):
    return lax.broadcasted_iota(jnp.int32, shape, axis)


def to_order(table, source, target, rows, factor=None):
    span = rows * INNER
    for chunk in range(source.shape[0] // span):
        for place in range(INNER):
            at = pl.multiple_of((table[0] ^ offset_of(place)) * rows, rows) + chunk * span
            value = source[pl.ds(chunk * span + place * rows, rows), :]
            if factor is not None:
                value = value * factor
            target[pl.ds(at, rows), :] = value


def from_order(table, source, target, rows):
    span = rows * INNER
    for chunk in range(target.shape[0] // span):
        for place in range(INNER):
            at = pl.multiple_of((table[0] ^ offset_of(place)) * rows, rows) + chunk * span
            target[pl.ds(chunk * span + place * rows, rows), :] = source[pl.ds(at, rows), :].astype(
                target.dtype
            )


def half_lanes(value, head, size):
    lane = iota(value.shape, 1)
    keep = (lane >= head * size) & (lane < (head + 1) * size)
    return jnp.where(keep, value, jnp.zeros_like(value))


def attend_kernel(causal, rows, size, table, q, k, v, out, log_total, qs, ks, vs, ordered):
    span, keys = q.shape[0], k.shape[0]
    chunks = keys // span
    to_order(table, q, qs, rows, jnp.asarray(size**-0.5, LOW))
    to_order(table, k, ks, rows)
    to_order(table, v, vs, rows)
    for step in range(span // STEP):
        lo = step * STEP
        queries = qs[lo : lo + STEP, :]
        q_at = table[1] + lo + iota((STEP, 1), 0)
        q_seg = seg_of(q_at, table, 2)
        count = lo + STEP if causal and chunks == 1 else span

        def scores(head, start):
            k_at = start + iota((1, count), 1)
            allowed = q_seg == seg_of(k_at, table, 5)
            if causal:
                allowed = allowed & (k_at <= q_at)
            raw = dot_t(queries, half_lanes(ks[pl.ds(start, count), :], head, size))
            return jnp.where(allowed, raw, -1e30)

        parts = []
        for head in range(2):
            if chunks == 1:
                raw = scores(head, 0)
                top = jnp.max(raw, axis=1, keepdims=True)
                weight = jnp.exp(raw - top)
                total = jnp.sum(weight, axis=1, keepdims=True)
                running = dot_n(weight.astype(LOW), vs[:count, :])
            else:

                def absorb(chunk, carry, head=head):
                    top, total, running = carry
                    start = pl.multiple_of(chunk * span, span)
                    raw = scores(head, start)
                    new_top = jnp.maximum(top, jnp.max(raw, axis=1, keepdims=True))
                    weight = jnp.exp(raw - new_top)
                    fade = jnp.exp(top - new_top)
                    total = total * fade + jnp.sum(weight, axis=1, keepdims=True)
                    running = running * fade + dot_n(weight.astype(LOW), vs[pl.ds(start, span), :])
                    return new_top, total, running

                top, total, running = lax.fori_loop(
                    0,
                    chunks,
                    absorb,
                    (
                        jnp.full((STEP, 1), -1e30, WIDE),
                        jnp.zeros((STEP, 1), WIDE),
                        jnp.zeros((STEP, 2 * size), WIDE),
                    ),
                )
            parts.append(running / total)
            logs = jnp.broadcast_to(top + jnp.log(total), (STEP, 2 * size))
            log_total[head : head + 1, lo : lo + STEP] = jnp.transpose(logs)[0:1, :]
        lane = iota((STEP, 2 * size), 1)
        ordered[lo : lo + STEP, :] = jnp.where(lane < size, parts[0], parts[1])
    from_order(table, ordered, out, rows)


def attend_back_kernel(
    causal, rows, size, table, q, k, v, up, log_total, dq, dk, dv, qs, ks, vs, ups, dqs, dks, dvs
):
    span, keys = q.shape[0], k.shape[0]
    chunks = keys // span
    scale = size**-0.5
    to_order(table, q, qs, rows, jnp.asarray(scale, LOW))
    to_order(table, up, ups, rows)
    to_order(table, k, ks, rows)
    to_order(table, v, vs, rows)
    dks[...] = jnp.zeros_like(dks)
    dvs[...] = jnp.zeros_like(dvs)
    for step in range(span // STEP):
        lo = step * STEP
        queries = qs[lo : lo + STEP, :]
        upstream = ups[lo : lo + STEP, :]
        q_at = table[1] + lo + iota((1, STEP), 1)
        q_seg = seg_of(q_at, table, 2)
        count = lo + STEP if causal and chunks == 1 else span
        total_dq = jnp.zeros((STEP, 2 * size), WIDE)
        for head in range(2):
            head_q = half_lanes(queries, head, size)
            head_up = half_lanes(upstream, head, size)
            logs = log_total[head : head + 1, lo : lo + STEP]

            def pieces(start, logs=logs, head_up=head_up, head=head):
                k_at = start + iota((count, 1), 0)
                allowed = q_seg == seg_of(k_at, table, 5)
                if causal:
                    allowed = allowed & (k_at <= q_at)
                head_k = half_lanes(ks[pl.ds(start, count), :], head, size)
                raw = dot_t(head_k, queries)
                probs = jnp.exp(jnp.where(allowed, raw - logs, -1e30))
                slope = dot_t(vs[pl.ds(start, count), :], head_up)
                return head_k, probs, probs * slope

            def spread(start, delta, made, head_q=head_q, head_up=head_up):
                head_k, probs, lean = made
                push = (lean - probs * delta).astype(LOW)
                dvs[pl.ds(start, count), :] += dot_n(probs.astype(LOW), head_up)
                dks[pl.ds(start, count), :] += dot_n(push, head_q)
                return dot_c(push, head_k)

            if chunks == 1:
                made = pieces(0)
                delta = jnp.sum(made[2], axis=0, keepdims=True)
                total_dq = total_dq + spread(0, delta, made)
            else:

                def measure(chunk, delta):
                    made = pieces(pl.multiple_of(chunk * span, span))
                    return delta + jnp.sum(made[2], axis=0, keepdims=True)

                delta = lax.fori_loop(0, chunks, measure, jnp.zeros((1, STEP), WIDE))

                def absorb(chunk, running, delta=delta):
                    start = pl.multiple_of(chunk * span, span)
                    return running + spread(start, delta, pieces(start))

                total_dq = lax.fori_loop(0, chunks, absorb, total_dq)
        dqs[lo : lo + STEP, :] = total_dq * scale
    from_order(table, dqs, dq, rows)
    from_order(table, dks, dk, rows)
    from_order(table, dvs, dv, rows)


SMEM = pl.BlockSpec(memory_space=pltpu.SMEM)
VMEM = pl.BlockSpec(memory_space=pltpu.VMEM)
ROOM = pltpu.CompilerParams(vmem_limit_bytes=56 * 2**20)


def attend(table, q, k, v, rows, causal):
    span, pair = q.shape
    keys = k.shape[0]
    return pl.pallas_call(
        functools.partial(attend_kernel, causal, rows, pair // 2),
        out_shape=(
            jax.ShapeDtypeStruct((span, pair), LOW),
            jax.ShapeDtypeStruct((2, span), WIDE),
        ),
        in_specs=[SMEM, VMEM, VMEM, VMEM],
        out_specs=(VMEM, VMEM),
        scratch_shapes=[
            pltpu.VMEM((span, pair), LOW),
            pltpu.VMEM((keys, pair), LOW),
            pltpu.VMEM((keys, pair), LOW),
            pltpu.VMEM((span, pair), WIDE),
        ],
        compiler_params=ROOM,
    )(table, q, k, v)


def attend_back(table, q, k, v, up, log_total, rows, causal):
    span, pair = q.shape
    keys = k.shape[0]
    return pl.pallas_call(
        functools.partial(attend_back_kernel, causal, rows, pair // 2),
        out_shape=(
            jax.ShapeDtypeStruct((span, pair), LOW),
            jax.ShapeDtypeStruct((keys, pair), LOW),
            jax.ShapeDtypeStruct((keys, pair), LOW),
        ),
        in_specs=[SMEM] + [VMEM] * 5,
        out_specs=(VMEM, VMEM, VMEM),
        scratch_shapes=[
            pltpu.VMEM((span, pair), LOW),
            pltpu.VMEM((keys, pair), LOW),
            pltpu.VMEM((keys, pair), LOW),
            pltpu.VMEM((span, pair), LOW),
            pltpu.VMEM((span, pair), WIDE),
            pltpu.VMEM((keys, pair), WIDE),
            pltpu.VMEM((keys, pair), WIDE),
        ],
        compiler_params=ROOM,
    )(table, q, k, v, up, log_total)


OUTER = ("ulys", "outer")
ALL = ("ulys", "outer", "inner")


def hop(value, distance):
    route = [(n, n ^ distance) for n in range(INNER)]
    return lax.ppermute(value, "inner", route)


def gather_places(own):
    chips = [own] + [hop(own, offset_of(place)) for place in (1, 2, 3)]
    near = jnp.concatenate(chips, axis=0)
    return jnp.concatenate([near, hop(near, 1)], axis=0)


def scatter_places(make, rows):
    half = rows * INNER // 2
    give = make(half, 2 * half).astype(LOW)
    took = hop(give, 1)
    both = make(0, half) + took.astype(WIDE)
    result = both[:rows]
    for place in (1, 2, 3):
        part = both[place * rows : (place + 1) * rows].astype(LOW)
        result = result + hop(part, offset_of(place)).astype(WIDE)
    return result


def swap_places(piece, place, rows):
    blocks = [piece[(n ^ place) * rows : ((n ^ place) + 1) * rows] for n in range(INNER)]
    return jnp.concatenate(blocks, axis=0)


def gather_heads(own, rows):
    chips = [own] + [hop(own, offset_of(place)) for place in (1, 2, 3)]
    near = jnp.stack(chips, axis=0)
    far = hop(near, 1)
    pieces = chips + [far[n] for n in range(4)]
    return jnp.concatenate([swap_places(pieces[n], n, rows) for n in range(INNER)], axis=1)


def column_slices(weight, parts):
    rows, columns = weight.shape
    share = columns // (parts * INNER)
    cut = jnp.transpose(weight.reshape(rows, parts, INNER, share), (2, 0, 1, 3))
    return cut.reshape(INNER, rows, parts * share)


def column_home(grad, parts):
    received = lax.all_to_all(grad, "inner", 0, 0)
    count, rows, columns = received.shape
    share = columns // parts
    spread = jnp.transpose(received.reshape(count, rows, parts, share), (1, 2, 0, 3))
    return spread.reshape(rows, parts * count * share).astype(WIDE)


def layer_norm(value, gain, shift):
    center = jnp.mean(value, axis=-1, keepdims=True)
    centred = value - center
    spread = jnp.mean(centred * centred, axis=-1, keepdims=True)
    return centred * lax.rsqrt(spread + 1e-05) * gain + shift


def smooth(value):
    return jax.nn.gelu(value, approximate=True)


def dot(a, b):
    return jnp.dot(a, b, preferred_element_type=WIDE)


def across(a, b):
    return lax.dot_general(a, b, (((1,), (1,)), ((), ())), preferred_element_type=WIDE)


def under(a, b):
    return lax.dot_general(a, b, (((0,), (0,)), ((), ())), preferred_element_type=WIDE)


def per_device(
    target,
    source,
    cotangent,
    target_lengths,
    source_lengths,
    self_in,
    self_out,
    cross_query,
    cross_kv,
    cross_out,
    mlp_in,
    mlp_out,
    vectors,
    hidden_bias,
):
    rows, width = target.shape[1:]
    here = lax.axis_index("inner")
    stream = lax.axis_index("ulys")
    group = lax.axis_index("outer")
    groups = lax.axis_size("outer")
    streams = lax.axis_size("ulys")
    shares = streams * groups
    devices = shares * INNER
    span = rows * INNER
    pair = width // INNER
    share = width // devices
    count = vectors.shape[0]
    target_ends = jnp.cumsum(target_lengths[stream])
    source_ends = jnp.cumsum(source_lengths[stream])
    start = jnp.stack([here, group * span]).astype(jnp.int32)
    self_table = jnp.concatenate([start, target_ends, target_ends]).astype(jnp.int32)
    cross_table = jnp.concatenate([start, target_ends, source_ends]).astype(jnp.int32)

    def slices_of(weight, parts):
        mine = lax.all_to_all(column_slices(weight, parts), "inner", 0, 0)
        return lax.all_gather(mine, OUTER, axis=0).reshape(width, -1)

    def my_heads(vector):
        return lax.dynamic_slice_in_dim(vector, here * pair, pair)

    small = jnp.concatenate([vectors.reshape(-1), hidden_bias])
    small = lax.all_gather(small, OUTER, axis=0)
    small = lax.all_gather(small, "inner", axis=1)
    params = small[:, :, : count * share].reshape(devices, count, share)
    params = jnp.transpose(params, (1, 0, 2)).reshape(count, width).astype(WIDE)
    h_bias = lax.dynamic_index_in_dim(small[:, :, count * share :], here, 1, False)
    h_bias = h_bias.reshape(-1).astype(WIDE)

    order = here ^ jnp.array([offset_of(n) for n in range(INNER)], jnp.int32)

    def place_rows(weight):
        return jnp.take(weight.reshape(INNER, pair, width), order, axis=0).reshape(width, width)

    w_self = slices_of(self_in, 3)
    w_pair = slices_of(cross_kv, 2)
    w_query = slices_of(cross_query, 1)
    w_sout = lax.all_gather(self_out, ALL, axis=0, tiled=True)
    w_cout = lax.all_gather(cross_out, ALL, axis=0, tiled=True)
    w_first = slices_of(mlp_in, shares)
    w_second = lax.all_gather(mlp_out, OUTER, axis=0, tiled=True)

    x_low = gather_places(target[0])
    states = gather_places(source[0])
    pull_up = gather_places(cotangent[0])
    x = x_low.astype(WIDE)

    h1 = layer_norm(x, params[0], params[1]).astype(LOW)
    projected = dot(h1, w_self)
    q = (projected[:, :pair] + my_heads(params[6])).astype(LOW)
    k = projected[:, pair : 2 * pair].astype(LOW)
    v = (projected[:, 2 * pair :] + my_heads(params[7])).astype(LOW)

    def stream_keys(own):
        return lax.all_gather(own, "outer", axis=0, tiled=True) if groups > 1 else own

    def own_keys(partial):
        if groups == 1:
            return partial
        return lax.psum_scatter(partial, "outer", scatter_dimension=0, tiled=True)

    k, v = stream_keys(k), stream_keys(v)
    att, self_total = attend(self_table, q, k, v, rows, True)
    att = gather_heads(att, rows)
    y1 = x + dot(att, place_rows(w_sout)) + params[8]
    h2 = layer_norm(y1, params[2], params[3]).astype(LOW)
    cq = (dot(h2, w_query) + my_heads(params[9])).astype(LOW)
    state_proj = dot(states, w_pair)
    ck = stream_keys(state_proj[:, :pair].astype(LOW))
    cv = stream_keys((state_proj[:, pair:] + my_heads(params[10])).astype(LOW))
    catt, cross_total = attend(cross_table, cq, ck, cv, rows, False)
    catt = gather_heads(catt, rows)
    y2 = y1 + dot(catt, place_rows(w_cout)) + params[11]
    h3 = layer_norm(y2, params[4], params[5]).astype(LOW)
    before = dot(h3, w_first) + h_bias
    active, active_pull = jax.vjp(smooth, before)
    active_low = active.astype(LOW)
    fed = scatter_places(lambda lo, hi: dot(active_low[lo:hi], w_second), rows)
    layer_out = (y2[:rows] + fed + params[12]).astype(LOW)[None]

    active_grad = across(pull_up, w_second)
    before_grad = active_pull(active_grad)[0].astype(LOW)
    second_grad = under(active_low, pull_up).astype(LOW)
    second_home = lax.psum_scatter(second_grad, OUTER, scatter_dimension=0, tiled=True)
    first_grad = under(h3, before_grad).astype(LOW)
    first_home = lax.psum_scatter(first_grad, OUTER, scatter_dimension=0, tiled=True)
    h_bias_grad = jnp.sum(before_grad.astype(WIDE), axis=0)
    third_grad = scatter_places(lambda lo, hi: across(before_grad[lo:hi], w_first), rows)
    upstream = cotangent[0].astype(WIDE)
    _, third_pull = jax.vjp(layer_norm, y2[:rows], params[4], params[5])
    late_part, gain_five, shift_five = third_pull(third_grad)
    late_grad = upstream + late_part
    cross_branch = late_grad.astype(LOW)
    cross_all = gather_places(cross_branch)

    def my_rows(weight):
        return lax.dynamic_slice_in_dim(weight, here * pair, pair, axis=0)

    def shard_features(value):
        cut = []
        for n in range(shares):
            first = (n * INNER + here) * share
            block = first // pair
            mixed = block ^ here
            place = ((mixed >> 1) & 3) | ((mixed & 1) << 2)
            cut.append(
                lax.dynamic_slice_in_dim(value, place * pair + first % pair, share, axis=1)
            )
        return jnp.concatenate(cut, axis=1)

    def home_rows(value, branch):
        grad = under(shard_features(value), branch).astype(LOW)
        return lax.psum_scatter(grad, OUTER, scatter_dimension=0, tiled=True).astype(WIDE)

    def home_columns(value, branch):
        grad = under(value, branch).astype(LOW)
        return lax.psum_scatter(grad, OUTER, scatter_dimension=0, tiled=True)

    cout_home = home_rows(catt, cross_all)
    catt_grad = across(cross_all, my_rows(w_cout)).astype(LOW)
    dcq, dck, dcv = attend_back(cross_table, cq, ck, cv, catt_grad, cross_total, rows, False)
    dck, dcv = own_keys(dck), own_keys(dcv)
    pair_back = jnp.concatenate([dck, dcv], axis=1)
    second_norm_grad = scatter_places(lambda lo, hi: across(dcq[lo:hi], w_query), rows)
    _, second_pull = jax.vjp(layer_norm, y1[:rows], params[2], params[3])
    middle_part, gain_three, shift_three = second_pull(second_norm_grad)
    middle_grad = late_grad + middle_part
    self_branch = middle_grad.astype(LOW)
    self_all = gather_places(self_branch)
    att_grad = across(self_all, my_rows(w_sout)).astype(LOW)
    dq, dk, dv = attend_back(self_table, q, k, v, att_grad, self_total, rows, True)
    dk, dv = own_keys(dk), own_keys(dv)
    projected_grad = jnp.concatenate([dq, dk, dv], axis=1)
    first_norm_grad = scatter_places(lambda lo, hi: across(projected_grad[lo:hi], w_self), rows)
    source_part = scatter_places(lambda lo, hi: across(pair_back[lo:hi], w_pair), rows)
    source_grad = source_part.astype(LOW)[None]
    query_home = home_columns(h2, dcq)
    pair_home = home_columns(states, pair_back)
    sout_home = home_rows(att, self_all)
    self_home = home_columns(h1, projected_grad)
    _, first_pull = jax.vjp(layer_norm, x[:rows], params[0], params[1])
    input_part, gain_one, shift_one = first_pull(first_norm_grad)
    target_grad = (middle_grad + input_part).astype(LOW)[None]

    def spread_heads(value):
        total = jnp.sum(value.astype(WIDE), axis=0)
        return lax.dynamic_update_slice_in_dim(jnp.zeros((width,), WIDE), total, here * pair, 0)

    vector_grad = jnp.stack(
        [
            gain_one,
            shift_one,
            gain_three,
            shift_three,
            gain_five,
            shift_five,
            spread_heads(dq),
            spread_heads(dv),
            jnp.sum(self_branch.astype(WIDE), axis=0),
            spread_heads(dcq),
            spread_heads(dcv),
            jnp.sum(cross_branch.astype(WIDE), axis=0),
            jnp.sum(upstream, axis=0),
        ]
    )
    vector_part = jnp.transpose(vector_grad.reshape(count, devices, share), (1, 0, 2))
    bias_part = h_bias_grad.reshape(shares, 1, -1)
    bias_part = lax.dynamic_update_slice_in_dim(
        jnp.zeros((shares, INNER, bias_part.shape[2]), WIDE), bias_part, here, 1
    ).reshape(devices, -1)
    tiny = jnp.concatenate([vector_part.reshape(devices, -1), bias_part], axis=1)
    tiny = jnp.sum(lax.all_to_all(tiny, ALL, 0, 0, tiled=True), axis=0)

    def to_owners(grad, parts):
        return column_home(grad.reshape(INNER, -1, grad.shape[1]), parts)

    return (
        layer_out,
        target_grad,
        source_grad,
        to_owners(self_home, 3),
        sout_home,
        to_owners(query_home, 1),
        to_owners(pair_home, 2),
        cout_home,
        to_owners(first_home, shares),
        second_home.astype(WIDE),
        tiny[: count * share].reshape(count, share),
        tiny[count * share :],
    )


def solution(mesh):
    streams, blocks = mesh.devices.shape
    grid = mesh.devices.reshape(streams, blocks // INNER, INNER)
    inner_mesh = Mesh(grid, ALL)
    rows = P("ulys", ("outer", "inner"), None)
    matrix = P(ALL, None)
    row_vectors = P(None, ALL)
    in_specs = (rows,) * 3 + (P(), P()) + (matrix,) * 7 + (row_vectors, P(ALL))
    out_specs = (rows,) * 3 + (matrix,) * 7 + (row_vectors, P(ALL))
    return jax.shard_map(
        per_device, mesh=inner_mesh, in_specs=in_specs, out_specs=out_specs, check_vma=False
    )
```

```python
import functools

import jax
import jax.numpy as jnp
from jax import lax
from jax.experimental import pallas as pl
from jax.experimental.pallas import tpu as pltpu
from jax.sharding import Mesh
from jax.sharding import PartitionSpec as P

HEADS = 16
LOW = jnp.bfloat16
WIDE = jnp.float32
INNER = 8
STEP = 256
LANES = 128
OUTER = ("ulys", "outer")
ALL = ("ulys", "outer", "inner")


def offset_of(place):
    return ((place & 3) << 1) | (place >> 2)


def dot_t(a, b):
    return lax.dot_general(a, b, (((1,), (1,)), ((), ())), preferred_element_type=WIDE)


def dot_n(a, b):
    return lax.dot_general(a, b, (((1,), (0,)), ((), ())), preferred_element_type=WIDE)


def dot_c(a, b):
    return lax.dot_general(a, b, (((0,), (0,)), ((), ())), preferred_element_type=WIDE)


def seg_of(position, table, first):
    count = jnp.zeros_like(position)
    for n in range(3):
        count = count + (table[first + n] <= position).astype(jnp.int32)
    return count


def iota(shape, axis):
    return lax.broadcasted_iota(jnp.int32, shape, axis)


def to_order(table, source, target, rows, factor=None):
    span = rows * INNER
    for chunk in range(source.shape[0] // span):
        for place in range(INNER):
            at = pl.multiple_of((table[0] ^ offset_of(place)) * rows, rows) + chunk * span
            value = source[pl.ds(chunk * span + place * rows, rows), :]
            if factor is not None:
                value = value * factor
            target[pl.ds(at, rows), :] = value


def from_order(table, source, target, rows):
    span = rows * INNER
    for chunk in range(target.shape[0] // span):
        for place in range(INNER):
            at = pl.multiple_of((table[0] ^ offset_of(place)) * rows, rows) + chunk * span
            target[pl.ds(chunk * span + place * rows, rows), :] = source[pl.ds(at, rows), :].astype(
                target.dtype
            )


def half_lanes(value, head, size):
    lane = iota(value.shape, 1)
    keep = (lane >= head * size) & (lane < (head + 1) * size)
    return jnp.where(keep, value, jnp.zeros_like(value))


def attend_kernel(causal, rows, size, table, q, k, v, out, log_total, qs, ks, vs, ordered):
    span, keys = q.shape[0], k.shape[0]
    chunks = keys // span
    to_order(table, q, qs, rows, jnp.asarray(size**-0.5, LOW))
    to_order(table, k, ks, rows)
    to_order(table, v, vs, rows)
    for step in range(span // STEP):
        lo = step * STEP
        queries = qs[lo : lo + STEP, :]
        q_at = table[1] + lo + iota((STEP, 1), 0)
        q_seg = seg_of(q_at, table, 2)
        count = lo + STEP if causal and chunks == 1 else span

        def scores(head, start):
            k_at = start + iota((1, count), 1)
            allowed = q_seg == seg_of(k_at, table, 5)
            if causal:
                allowed = allowed & (k_at <= q_at)
            raw = dot_t(queries, half_lanes(ks[pl.ds(start, count), :], head, size))
            return jnp.where(allowed, raw, -1e30)

        parts = []
        for head in range(2):
            if chunks == 1:
                raw = scores(head, 0)
                top = jnp.max(raw, axis=1, keepdims=True)
                weight = jnp.exp(raw - top)
                total = jnp.sum(weight, axis=1, keepdims=True)
                running = dot_n(weight.astype(LOW), vs[:count, :])
            else:

                def absorb(chunk, carry, head=head):
                    top, total, running = carry
                    start = pl.multiple_of(chunk * span, span)
                    raw = scores(head, start)
                    new_top = jnp.maximum(top, jnp.max(raw, axis=1, keepdims=True))
                    weight = jnp.exp(raw - new_top)
                    fade = jnp.exp(top - new_top)
                    total = total * fade + jnp.sum(weight, axis=1, keepdims=True)
                    running = running * fade + dot_n(weight.astype(LOW), vs[pl.ds(start, span), :])
                    return new_top, total, running

                top, total, running = lax.fori_loop(
                    0,
                    chunks,
                    absorb,
                    (
                        jnp.full((STEP, 1), -1e30, WIDE),
                        jnp.zeros((STEP, 1), WIDE),
                        jnp.zeros((STEP, 2 * size), WIDE),
                    ),
                )
            parts.append(running / total)
            logs = jnp.broadcast_to(top + jnp.log(total), (STEP, 2 * size))
            log_total[head : head + 1, lo : lo + STEP] = jnp.transpose(logs)[0:1, :]
        lane = iota((STEP, 2 * size), 1)
        ordered[lo : lo + STEP, :] = jnp.where(lane < size, parts[0], parts[1])
    from_order(table, ordered, out, rows)


def attend_back_kernel(causal, rows, size, start, table, q, k, v, log_total, weight, own, *refs):
    pieces, refs = refs[:INNER], refs[INNER:]
    if start is not None:
        packed, give, keep, refs = refs[0], refs[1], refs[2], refs[3:]
    dq, dk, dv, sums, row_keep, row_give, refs = *refs[:6], refs[6:]
    qs, ks, vs, ups, dqs, dks, dvs, branch, row, marks = refs
    copies = pull(pieces, 0, branch, marks)
    span, keys = q.shape[0], k.shape[0]
    chunks = keys // span
    scale = size**-0.5
    to_order(table, q, qs, rows, jnp.asarray(scale, LOW))
    to_order(table, k, ks, rows)
    to_order(table, v, vs, rows)
    finish(copies)
    upstream = dot_t(branch[...], weight[...]).astype(LOW)
    for place in range(INNER):
        at = pl.multiple_of((table[0] ^ offset_of(place)) * rows, rows)
        ups[pl.ds(at, rows), :] = upstream[place * rows : (place + 1) * rows, :]
    row[...] = dot_c(own[...], branch[...]).astype(LOW)
    share = row_keep.shape[1]
    for core, out in ((table[8], row_keep), (table[9], row_give)):
        for n in range(2):
            first = pl.multiple_of((2 * n + core) * share, share)
            out[n] = row[pl.ds(first, share), :]
    dks[...] = jnp.zeros_like(dks)
    dvs[...] = jnp.zeros_like(dvs)
    for step in range(span // STEP):
        lo = step * STEP
        queries = qs[lo : lo + STEP, :]
        upstream = ups[lo : lo + STEP, :]
        q_at = table[1] + lo + iota((1, STEP), 1)
        q_seg = seg_of(q_at, table, 2)
        count = lo + STEP if causal and chunks == 1 else span
        total_dq = jnp.zeros((STEP, 2 * size), WIDE)
        for head in range(2):
            head_q = half_lanes(queries, head, size)
            head_up = half_lanes(upstream, head, size)
            logs = log_total[head : head + 1, lo : lo + STEP]

            def pieces(start, logs=logs, head_up=head_up, head=head):
                k_at = start + iota((count, 1), 0)
                allowed = q_seg == seg_of(k_at, table, 5)
                if causal:
                    allowed = allowed & (k_at <= q_at)
                head_k = half_lanes(ks[pl.ds(start, count), :], head, size)
                raw = dot_t(head_k, queries)
                probs = jnp.exp(jnp.where(allowed, raw - logs, -1e30))
                slope = dot_t(vs[pl.ds(start, count), :], head_up)
                return head_k, probs, probs * slope

            def spread(start, delta, made, head_q=head_q, head_up=head_up):
                head_k, probs, lean = made
                push = (lean - probs * delta).astype(LOW)
                dvs[pl.ds(start, count), :] += dot_n(probs.astype(LOW), head_up)
                dks[pl.ds(start, count), :] += dot_n(push, head_q)
                return dot_c(push, head_k)

            if chunks == 1:
                made = pieces(0)
                delta = jnp.sum(made[2], axis=0, keepdims=True)
                total_dq = total_dq + spread(0, delta, made)
            else:

                def measure(chunk, delta):
                    made = pieces(pl.multiple_of(chunk * span, span))
                    return delta + jnp.sum(made[2], axis=0, keepdims=True)

                delta = lax.fori_loop(0, chunks, measure, jnp.zeros((1, STEP), WIDE))

                def absorb(chunk, running, delta=delta):
                    start = pl.multiple_of(chunk * span, span)
                    return running + spread(start, delta, pieces(start))

                total_dq = lax.fori_loop(0, chunks, absorb, total_dq)
        dqs[lo : lo + STEP, :] = total_dq * scale
    from_order(table, dqs, dq, rows)
    if start is not None:
        half = span // 2
        back = packed[:, start * LANES : (start + 1) * LANES]
        give[...] = dot_t(dq[half:, :], back).astype(LOW)
        keep[...] = dot_t(dq[:half, :], back)
    from_order(table, dks, dk, rows)
    from_order(table, dvs, dv, rows)
    sums[0:1, :] = jnp.sum(dqs[...].astype(LOW).astype(WIDE), axis=0, keepdims=True)
    sums[1:2, :] = jnp.sum(dvs[...].astype(LOW).astype(WIDE), axis=0, keepdims=True)


HBM = pl.BlockSpec(memory_space=pl.ANY)


def room(megabytes):
    return pltpu.CompilerParams(vmem_limit_bytes=megabytes * 2**20)


def pull(pieces, index, target, marks):
    rows = target.shape[0] // INNER
    copies = []
    for place in range(INNER):
        source = pieces[place].at[pl.ds(index * rows, rows), :]
        aim = target.at[pl.ds(place * rows, rows), :]
        copies.append(pltpu.make_async_copy(source, aim, marks.at[place]))
    for copy in copies:
        copy.start()
    return copies


def settle(planes, table, first, target, marks):
    rows = planes[0].shape[0]
    copies = []
    for n, plane in enumerate(planes):
        at = pl.multiple_of(table[first + n], 16)
        copies.append(pltpu.make_async_copy(plane, target.at[pl.ds(at, rows), :], marks.at[n]))
    for copy in copies:
        copy.start()
    return copies


def finish(copies):
    for copy in copies:
        copy.wait()


def cost(micros):
    return pl.CostEstimate(
        flops=int(micros * 1.1e9), bytes_accessed=int(micros * 3.5e6), transcendentals=0
    )


SMEM = pl.BlockSpec(memory_space=pltpu.SMEM)
VMEM = pl.BlockSpec(memory_space=pltpu.VMEM)


def attend(table, q, k, v, rows, causal):
    span, pair = q.shape
    keys = k.shape[0]
    return pl.pallas_call(
        functools.partial(attend_kernel, causal, rows, pair // 2),
        out_shape=(
            jax.ShapeDtypeStruct((span, pair), LOW),
            jax.ShapeDtypeStruct((2, span), WIDE),
        ),
        in_specs=[SMEM, VMEM, VMEM, VMEM],
        out_specs=(VMEM, VMEM),
        scratch_shapes=[
            pltpu.VMEM((span, pair), LOW),
            pltpu.VMEM((keys, pair), LOW),
            pltpu.VMEM((keys, pair), LOW),
            pltpu.VMEM((span, pair), WIDE),
        ],
        compiler_params=room(60),
        cost_estimate=cost(6),
    )(table, q, k, v)


def attend_back(table, q, k, v, log_total, weight, own, pieces, rows, causal, back=None):
    span, pair = q.shape
    keys = k.shape[0]
    width = weight.shape[1]
    part = jax.ShapeDtypeStruct((2, pair // 4, width), LOW)
    spread_shape = (
        jax.ShapeDtypeStruct((span // 2, width), LOW),
        jax.ShapeDtypeStruct((span // 2, width), WIDE),
    )
    start, packed = back if back else (None, None)
    extra = [packed] if back else []
    return pl.pallas_call(
        functools.partial(attend_back_kernel, causal, rows, pair // 2, start),
        out_shape=(spread_shape if back else ())
        + (
            jax.ShapeDtypeStruct((span, pair), LOW),
            jax.ShapeDtypeStruct((keys, pair), LOW),
            jax.ShapeDtypeStruct((keys, pair), LOW),
            jax.ShapeDtypeStruct((2, pair), WIDE),
            part,
            part,
        ),
        in_specs=[SMEM] + [VMEM] * 6 + [HBM] * INNER + [VMEM] * len(extra),
        out_specs=(VMEM,) * (8 if back else 6),
        scratch_shapes=[
            pltpu.VMEM((span, pair), LOW),
            pltpu.VMEM((keys, pair), LOW),
            pltpu.VMEM((keys, pair), LOW),
            pltpu.VMEM((span, pair), LOW),
            pltpu.VMEM((span, pair), WIDE),
            pltpu.VMEM((keys, pair), WIDE),
            pltpu.VMEM((keys, pair), WIDE),
            pltpu.VMEM((span, width), LOW),
            pltpu.VMEM((pair, width), LOW),
            pltpu.SemaphoreType.DMA((INNER,)),
        ],
        compiler_params=room(60),
        cost_estimate=cost(10),
    )(table, q, k, v, log_total, weight, own, *pieces, *extra)


def centre(value):
    center = jnp.mean(value, axis=-1, keepdims=True)
    centred = value - center
    spread = jnp.mean(centred * centred, axis=-1, keepdims=True)
    return centred, lax.rsqrt(spread + 1e-05)


def norm_of(value, gain, shift):
    centred, inverse = centre(value)
    return (centred * inverse * gain + shift).astype(LOW)


def enter_kernel(kinds, table, *refs):
    pieces, refs = refs[:INNER], refs[INNER:]
    planes, refs = refs[:-9], refs[-9:]
    q, k, v, h, params, biases, packed, x_all, marks = refs
    copies = pull(pieces, 0, x_all, marks.at[0])
    finish(settle(planes, table, 2, packed, marks.at[1]))
    edge = kinds * LANES
    extra = packed[:, edge : edge + LANES].astype(WIDE)
    params[...] = jnp.transpose(extra)[:16, :]
    size = LANES // 2
    mine = [packed[pl.ds(pl.multiple_of(table[n], 16), size), edge : edge + LANES] for n in (0, 1)]
    biases[...] = jnp.transpose(jnp.concatenate(mine, axis=0).astype(WIDE))[:16, :]
    finish(copies)
    half = x_all.shape[0] // 2
    for part in range(2):
        at = slice(part * half, (part + 1) * half)
        low = norm_of(x_all[at, :].astype(WIDE), params[0:1, :], params[1:2, :])
        h[at, :] = low
        made = dot_n(low, packed[:, :edge])
        q[at, :] = (made[:, :LANES] + biases[6:7, :]).astype(LOW)
        k[at, :] = made[:, LANES : 2 * LANES].astype(LOW)
        v[at, :] = (made[:, 2 * LANES :] + biases[7:8, :]).astype(LOW)


def enter(table, rows, pieces, planes):
    width = pieces[0].shape[1]
    lanes = planes[0].shape[1]
    span = rows * INNER
    heads = jax.ShapeDtypeStruct((span, LANES), LOW)
    return pl.pallas_call(
        functools.partial(enter_kernel, 3),
        out_shape=(
            heads,
            heads,
            heads,
            jax.ShapeDtypeStruct((span, width), LOW),
            jax.ShapeDtypeStruct((16, width), WIDE),
            jax.ShapeDtypeStruct((16, LANES), WIDE),
            jax.ShapeDtypeStruct((width, lanes), LOW),
            jax.ShapeDtypeStruct((span, width), LOW),
        ),
        in_specs=[SMEM] + [HBM] * (INNER + len(planes)),
        out_specs=(VMEM,) * 8,
        scratch_shapes=[
            pltpu.SemaphoreType.DMA((2, INNER)),
        ],
        compiler_params=room(32),
        cost_estimate=cost(3),
    )(table, *pieces, *planes)


def join_kernel(vector, first, query, *refs):
    pieces, weights, refs = refs[:INNER], refs[INNER : 2 * INNER], refs[2 * INNER :]
    if query is None:
        base, base_own, params, y_own, h, weight, left, heads, marks = refs
    else:
        base, params, packed, biases, y_own, h, y_all, cq, weight, left, heads, marks = refs
    span = left.shape[0]
    block = span // INNER
    loads = pull(weights, 0, weight, marks.at[1])
    copies = []
    for place in range(INNER):
        copies.append(pltpu.make_async_copy(pieces[place], heads.at[place], marks.at[0, place]))
    for copy in copies:
        copy.start()
    finish(copies + loads)
    parts = INNER // 2
    for part in range(parts):
        at = slice(part * 2 * block, (part + 1) * 2 * block)
        for n in range(2 * part, 2 * part + 2):
            for place in range(INNER):
                first_row = (n ^ place) * block
                left[n * block : (n + 1) * block, place * LANES : (place + 1) * LANES] = heads[
                    place, first_row : first_row + block, :
                ]
        value = base[at, :].astype(WIDE)
        if query is None and part == 0:
            value = jnp.concatenate([base_own[...], value[block:, :]], axis=0)
        y = value + dot_n(left[at, :], weight[...]) + params[vector : vector + 1, :]
        if part == 0:
            y_own[...] = y[:block, :]
        low = norm_of(y, params[first : first + 1, :], params[first + 1 : first + 2, :])
        h[at, :] = low
        if query is not None:
            y_all[at, :] = y.astype(LOW)
            made = dot_n(low, packed[:, query * LANES : (query + 1) * LANES])
            cq[at, :] = (made + biases[9:10, :]).astype(LOW)


def join_self(pieces, weights, base, params, packed, biases):
    span, width = base.shape
    return pl.pallas_call(
        functools.partial(join_kernel, 8, 2, 2),
        out_shape=(
            jax.ShapeDtypeStruct((span // INNER, width), WIDE),
            jax.ShapeDtypeStruct((span, width), LOW),
            jax.ShapeDtypeStruct((span, width), LOW),
            jax.ShapeDtypeStruct((span, LANES), LOW),
        ),
        in_specs=[HBM] * (2 * INNER) + [VMEM] * 4,
        out_specs=(VMEM,) * 4,
        scratch_shapes=[
            pltpu.VMEM((width, width), LOW),
            pltpu.VMEM((span, width), LOW),
            pltpu.VMEM((INNER, span, LANES), LOW),
            pltpu.SemaphoreType.DMA((2, INNER)),
        ],
        compiler_params=room(60),
        cost_estimate=cost(6),
    )(*pieces, *weights, base, params, packed, biases)


def join_cross(pieces, weights, base, base_own, params):
    span, width = base.shape
    return pl.pallas_call(
        functools.partial(join_kernel, 11, 4, None),
        out_shape=(
            jax.ShapeDtypeStruct((span // INNER, width), WIDE),
            jax.ShapeDtypeStruct((span, width), LOW),
        ),
        in_specs=[HBM] * (2 * INNER) + [VMEM] * 3,
        out_specs=(VMEM,) * 2,
        scratch_shapes=[
            pltpu.VMEM((width, width), LOW),
            pltpu.VMEM((span, width), LOW),
            pltpu.VMEM((INNER, span, LANES), LOW),
            pltpu.SemaphoreType.DMA((2, INNER)),
        ],
        compiler_params=room(60),
        cost_estimate=cost(5),
    )(*pieces, *weights, base, base_own, params)


def load_rows(packed, start, target, marks):
    shares = packed.shape[0]
    rows = target.shape[0] // shares
    copies = []
    for n in range(shares):
        source = packed.at[n, pl.ds(start, rows), :]
        aim = target.at[pl.ds(n * rows, rows), :]
        copies.append(pltpu.make_async_copy(source, aim, marks.at[n]))
    for copy in copies:
        copy.start()
    return copies


def feed_kernel(h, bias, packed, *refs):
    pieces = refs[:INNER]
    act, slope, give, keep, bias_grad, up, first, second, marks, weight_marks = refs[INNER:]
    span, width = up.shape
    hidden = second.shape[0]
    loads = load_rows(packed, 0, first, weight_marks.at[0])
    copies = load_rows(packed, width // packed.shape[0], second, weight_marks.at[1])
    copies += pull(pieces, 0, up, marks)
    finish(loads)
    step = 256
    inner = (2.0 / 3.141592653589793) ** 0.5
    for n in range(hidden // step):
        at = slice(n * step, (n + 1) * step)
        pre = dot_n(h[...], first[:, at]) + bias[:, at]
        square = pre * pre
        bend = jnp.tanh(pre * (inner + (inner * 0.044715) * square))
        half = 0.5 * bend + 0.5
        act[:, at] = (pre * half).astype(LOW)
        if n == 0:
            finish(copies)
        rise = half + 0.5 * pre * (1.0 - bend * bend) * (inner + (3 * inner * 0.044715) * square)
        low = (dot_t(up[...], second[at, :]) * rise).astype(LOW)
        slope[:, at] = low
        bias_grad[:, at] = jnp.sum(low.astype(WIDE), axis=0, keepdims=True)
    give[...] = dot_t(slope[span // 2 :, :], first[...]).astype(LOW)
    keep[...] = dot_t(slope[: span // 2, :], first[...])


def feed(h, bias, packed, pieces):
    span, width = h.shape
    hidden = bias.shape[1]
    shares = packed.shape[0]
    return pl.pallas_call(
        feed_kernel,
        out_shape=(
            jax.ShapeDtypeStruct((span, hidden), LOW),
            jax.ShapeDtypeStruct((span, hidden), LOW),
            jax.ShapeDtypeStruct((span // 2, width), LOW),
            jax.ShapeDtypeStruct((span // 2, width), WIDE),
            jax.ShapeDtypeStruct((1, hidden), WIDE),
            jax.ShapeDtypeStruct((span, width), LOW),
        ),
        in_specs=[VMEM] * 2 + [HBM] * (1 + INNER),
        out_specs=(VMEM,) * 6,
        scratch_shapes=[
            pltpu.VMEM((width, hidden), LOW),
            pltpu.VMEM((hidden, width), LOW),
            pltpu.SemaphoreType.DMA((INNER,)),
            pltpu.SemaphoreType.DMA((2, shares)),
        ],
        compiler_params=room(44),
        cost_estimate=cost(13),
    )(h, bias, packed, *pieces)


def feed_out_kernel(act, packed, give, keep, second, marks):
    finish(load_rows(packed, second.shape[1] // packed.shape[0], second, marks))
    half = keep.shape[0]
    give[...] = dot_n(act[half:, :], second[...]).astype(LOW)
    keep[...] = dot_n(act[:half, :], second[...])


def feed_out(act, packed):
    span, hidden = act.shape
    shares, _, width = packed.shape
    return pl.pallas_call(
        feed_out_kernel,
        out_shape=(
            jax.ShapeDtypeStruct((span // 2, width), LOW),
            jax.ShapeDtypeStruct((span // 2, width), WIDE),
        ),
        in_specs=[VMEM, HBM],
        out_specs=(VMEM,) * 2,
        scratch_shapes=[
            pltpu.VMEM((hidden, width), LOW),
            pltpu.SemaphoreType.DMA((shares,)),
        ],
        compiler_params=room(24),
        cost_estimate=cost(3),
    )(act, packed)


def feed_grad_kernel(act, slope, h, up, out):
    width = up.shape[1]
    step = 256
    for n in range(width // step):
        at = slice(n * step, (n + 1) * step)
        out[at, width:] = dot_c(h[:, at], slope[...]).astype(LOW)
    for n in range(act.shape[1] // step):
        at = slice(n * step, (n + 1) * step)
        out[at, :width] = dot_c(act[:, at], up[...]).astype(LOW)


def feed_grad(act, slope, h, up):
    width = h.shape[1]
    hidden = act.shape[1]
    return pl.pallas_call(
        feed_grad_kernel,
        out_shape=jax.ShapeDtypeStruct((width, width + hidden), LOW),
        in_specs=[VMEM] * 4,
        out_specs=VMEM,
        compiler_params=room(40),
        cost_estimate=cost(6),
    )(act, slope, h, up)


def fold_kernel(keep, took, own, one, two, three):
    rows = own.shape[0]
    own[...] = keep[:rows, :] + took[:rows, :].astype(WIDE)
    for n, part in enumerate((one, two, three), 1):
        at = slice(n * rows, (n + 1) * rows)
        part[...] = (keep[at, :] + took[at, :].astype(WIDE)).astype(LOW)


def fold(keep, took):
    half, width = keep.shape
    part = jax.ShapeDtypeStruct((half // 4, width), LOW)
    return pl.pallas_call(
        fold_kernel,
        out_shape=(jax.ShapeDtypeStruct((half // 4, width), WIDE), part, part, part),
        in_specs=[VMEM] * 2,
        out_specs=(VMEM,) * 4,
        compiler_params=room(16),
        cost_estimate=cost(1),
    )(keep, took)


def norm_back_kernel(first, own, one, two, three, value, base, params, grad, low, sums):
    slope = own[...] + one[...].astype(WIDE) + two[...].astype(WIDE) + three[...].astype(WIDE)
    centred, inverse = centre(value[...].astype(WIDE))
    unit = centred * inverse
    lean = slope * params[first : first + 1, :]
    flat = jnp.mean(lean, axis=-1, keepdims=True)
    tilt = jnp.mean(lean * unit, axis=-1, keepdims=True)
    total = base[...].astype(WIDE) + inverse * (lean - flat - unit * tilt)
    grad[...] = total
    cut = total.astype(LOW)
    low[...] = cut
    sums[0:1, :] = jnp.sum(slope * unit, axis=0, keepdims=True)
    sums[1:2, :] = jnp.sum(slope, axis=0, keepdims=True)
    sums[2:3, :] = jnp.sum(cut.astype(WIDE), axis=0, keepdims=True)
    sums[3:4, :] = jnp.sum(base[...].astype(WIDE), axis=0, keepdims=True)


def norm_back(first, own, parts, value, base, params):
    rows, width = own.shape
    return pl.pallas_call(
        functools.partial(norm_back_kernel, first),
        out_shape=(
            jax.ShapeDtypeStruct((rows, width), WIDE),
            jax.ShapeDtypeStruct((rows, width), LOW),
            jax.ShapeDtypeStruct((4, width), WIDE),
        ),
        in_specs=[VMEM] * 7,
        out_specs=(VMEM,) * 3,
        compiler_params=room(16),
        cost_estimate=cost(2),
    )(own, *parts, value, base, params)


def spread_kernel(start, *refs):
    values, packed, give, keep = refs[:-3], refs[-3], refs[-2], refs[-1]
    half = keep.shape[0]
    weight = packed[:, start * LANES : (start + len(values)) * LANES]
    for at, out in ((half, give), (0, keep)):
        left = [value[at : at + half, :] for value in values]
        left = left[0] if len(left) == 1 else jnp.concatenate(left, axis=1)
        out[...] = dot_t(left, weight).astype(out.dtype)


def spread(start, values, packed):
    span, width = values[0].shape[0], packed.shape[0]
    return pl.pallas_call(
        functools.partial(spread_kernel, start),
        out_shape=(
            jax.ShapeDtypeStruct((span // 2, width), LOW),
            jax.ShapeDtypeStruct((span // 2, width), WIDE),
        ),
        in_specs=[VMEM] * (len(values) + 1),
        out_specs=(VMEM,) * 2,
        compiler_params=room(24),
        cost_estimate=cost(2),
    )(*values, packed)


def pair_kernel(table, biases, *refs):
    pieces, refs = refs[:INNER], refs[INNER:]
    planes, (states, k, v, packed, marks) = refs[:-5], refs[-5:]
    copies = pull(pieces, 0, states, marks.at[0])
    finish(settle(planes, table, 2, packed, marks.at[1]))
    finish(copies)
    made = dot_n(states[...], packed[:, : 2 * LANES])
    k[...] = made[:, :LANES].astype(LOW)
    v[...] = (made[:, LANES:] + biases[10:11, :]).astype(LOW)


def pair_heads(table, rows, pieces, planes, biases):
    width = pieces[0].shape[1]
    span = rows * INNER
    heads = jax.ShapeDtypeStruct((span, LANES), LOW)
    return pl.pallas_call(
        pair_kernel,
        out_shape=(
            jax.ShapeDtypeStruct((span, width), LOW),
            heads,
            heads,
            jax.ShapeDtypeStruct((width, planes[0].shape[1]), LOW),
        ),
        in_specs=[SMEM, VMEM] + [HBM] * (INNER + len(planes)),
        out_specs=(VMEM,) * 4,
        scratch_shapes=[pltpu.SemaphoreType.DMA((2, INNER))],
        compiler_params=room(24),
        cost_estimate=cost(3),
    )(table, biases, *pieces, *planes)


def spread_self_kernel(dq, dk, dv, packed, x_all, give, keep, sums):
    half = x_all.shape[0] // 2
    weight = packed[:, : 3 * LANES]
    first = second = None
    for part, out in ((1, give), (0, keep)):
        at = slice(part * half, (part + 1) * half)
        left = jnp.concatenate([dq[at, :], dk[at, :], dv[at, :]], axis=1)
        slope = dot_t(left, weight)
        out[...] = slope.astype(out.dtype)
        centred, inverse = centre(x_all[at, :].astype(WIDE))
        gain = jnp.sum(slope * (centred * inverse), axis=0, keepdims=True)
        shift = jnp.sum(slope, axis=0, keepdims=True)
        first = gain if first is None else first + gain
        second = shift if second is None else second + shift
    sums[0:1, :] = first
    sums[1:2, :] = second


def spread_self(dq, dk, dv, packed, x_all):
    span, width = x_all.shape
    return pl.pallas_call(
        spread_self_kernel,
        out_shape=(
            jax.ShapeDtypeStruct((span // 2, width), LOW),
            jax.ShapeDtypeStruct((span // 2, width), WIDE),
            jax.ShapeDtypeStruct((2, width), WIDE),
        ),
        in_specs=[VMEM] * 5,
        out_specs=(VMEM,) * 3,
        compiler_params=room(32),
        cost_estimate=cost(4),
    )(dq, dk, dv, packed, x_all)


def home_kernel(got, out):
    kinds = got.shape[2] // LANES
    groups = got.shape[0] // INNER
    size = LANES // 2
    total = []
    for place in range(INNER):
        running = got[place].astype(WIDE)
        for n in range(1, groups):
            running = running + got[n * INNER + place].astype(WIDE)
        total.append(running)
    for kind in range(kinds):
        heads = {}
        for place in range(INNER):
            for n in (0, 1):
                at = kind * LANES + n * size
                number = (2 * (place & 1) + n) * (INNER // 2) + (place >> 1)
                heads[number] = total[place][:, at : at + size]
        for number in range(0, 2 * INNER, 2):
            at = kind * INNER * LANES + number * size
            both = jnp.concatenate([heads[number], heads[number + 1]], axis=1)
            out[:, at : at + LANES] = both


def home_columns(got):
    rows, lanes = got.shape[1:]
    return pl.pallas_call(
        home_kernel,
        out_shape=jax.ShapeDtypeStruct((rows, lanes * INNER), WIDE),
        in_specs=[VMEM],
        out_specs=VMEM,
        compiler_params=room(16),
        cost_estimate=cost(2),
    )(got)


def column_part_kernel(kinds, *refs):
    count = len(kinds)
    lefts, rights, column = refs[:count], refs[count:-1], refs[-1]
    at = first = 0
    for left, kind in zip(lefts, kinds):
        right = [value[...] for value in rights[first : first + kind]]
        right = right[0] if kind == 1 else jnp.concatenate(right, axis=1)
        lanes = kind * LANES
        column[:, at : at + lanes] = dot_c(left[...], right).astype(LOW)
        at, first = at + lanes, first + kind


def column_part(*pairs):
    width = pairs[0][0].shape[1]
    kinds = tuple(len(rights) for _, rights in pairs)
    lefts = [left for left, _ in pairs]
    rights = [value for _, values in pairs for value in values]
    return pl.pallas_call(
        functools.partial(column_part_kernel, kinds),
        out_shape=jax.ShapeDtypeStruct((width, LANES * sum(kinds)), LOW),
        in_specs=[VMEM] * (len(lefts) + len(rights)),
        out_specs=VMEM,
        compiler_params=room(24),
        cost_estimate=cost(3),
    )(*lefts, *rights)


def pick_kernel(table, packed, own, give):
    share = own.shape[1]
    for first, out in ((table[0], own), (table[1], give)):
        for n in range(2):
            for place in range(INNER):
                at = pl.multiple_of(((first + n) * INNER + place) * share, share)
                out[n, :, place * LANES : (place + 1) * LANES] = packed[pl.ds(at, share), :]


def pick(table, packed):
    width = packed.shape[0]
    part = jax.ShapeDtypeStruct((2, width // (4 * INNER), width), LOW)
    return pl.pallas_call(
        pick_kernel,
        out_shape=(part, part),
        in_specs=[SMEM, VMEM],
        out_specs=(VMEM,) * 2,
        compiler_params=room(16),
        cost_estimate=cost(1),
    )(table, packed)


def merge_kernel(table, own, took, out):
    share = own.shape[1]
    for n in range(2):
        for core, value in ((table[2], own), (table[3], took)):
            first = pl.multiple_of((2 * n + core) * share, share)
            out[pl.ds(first, share), :] = value[n]


def merge(table, own, took):
    _, rows, width = own.shape
    return pl.pallas_call(
        merge_kernel,
        out_shape=jax.ShapeDtypeStruct((4 * rows, width), LOW),
        in_specs=[SMEM, VMEM, VMEM],
        out_specs=VMEM,
        compiler_params=room(16),
        cost_estimate=cost(1),
    )(table, own, took)


def stack_kernel(table, *refs):
    pairs, out = refs[:-1], refs[-1]
    rows = pairs[0].shape[1]
    for n in range(len(pairs) // 2):
        at = slice(n * rows, (n + 1) * rows)
        for first, value in ((table[0], pairs[2 * n]), (table[1], pairs[2 * n + 1])):
            out[pl.ds(first, 2), at, :] = value[...]


def stack(table, *pairs):
    _, rows, width = pairs[0].shape
    return pl.pallas_call(
        stack_kernel,
        out_shape=jax.ShapeDtypeStruct((4, rows * len(pairs) // 2, width), LOW),
        in_specs=[SMEM] + [VMEM] * len(pairs),
        out_specs=VMEM,
        compiler_params=room(16),
        cost_estimate=cost(1),
    )(table, *pairs)


def hop(value, distance):
    route = [(n, n ^ distance) for n in range(INNER)]
    return lax.ppermute(value, "inner", route)


def after(value, *others):
    return lax.optimization_barrier((value,) + others)[0]


def gather_places(own):
    near = [own] + [hop(own, offset_of(place)) for place in (1, 2, 3)]
    return near + [hop(piece, 1) for piece in near]


def scatter_start(give, keep):
    return fold(keep, hop(give, 1))


def scatter_finish(parts):
    return [hop(part, offset_of(place)) for place, part in enumerate(parts, 1)]


def scatter_places(give, keep):
    own, *parts = scatter_start(give, keep)
    return own, scatter_finish(parts)


def dot(a, b):
    return jnp.dot(a, b, preferred_element_type=WIDE)


def under(a, b):
    return lax.dot_general(a, b, (((0,), (0,)), ((), ())), preferred_element_type=WIDE)


def per_device(
    target,
    source,
    cotangent,
    target_lengths,
    source_lengths,
    self_in,
    self_out,
    cross_query,
    cross_kv,
    cross_out,
    mlp_in,
    mlp_out,
    vectors,
    hidden_bias,
):
    rows, width = target.shape[1:]
    here = lax.axis_index("inner")
    core, chip = here & 1, here >> 1
    stream = lax.axis_index("ulys")
    group = lax.axis_index("outer")
    groups = lax.axis_size("outer")
    shares = lax.axis_size("ulys") * groups
    devices = shares * INNER
    span = rows * INNER
    pair = width // INNER
    size = pair // 2
    share = width // devices
    hidden = hidden_bias.shape[0]
    count = vectors.shape[0]
    chips = INNER // 2
    matched = shares * chips == HEADS and 2 * share == size
    target_ends = jnp.cumsum(target_lengths[stream])
    source_ends = jnp.cumsum(source_lengths[stream])
    start = jnp.stack([here, group * span]).astype(jnp.int32)
    cores = jnp.stack([core, 1 - core])
    self_table = jnp.concatenate([start, target_ends, target_ends, cores]).astype(jnp.int32)
    cross_table = jnp.concatenate([start, target_ends, source_ends, cores]).astype(jnp.int32)
    if matched:
        head_at = [(2 * core + n) * (width // shares) + chip * size for n in (0, 1)]
    else:
        head_at = [here * pair + n * size for n in (0, 1)]
    plane_at = [jnp.zeros((), jnp.int32)]
    head_table = jnp.stack(head_at + plane_at).astype(jnp.int32)

    def by_device(value):
        lead = value.shape[:-1]
        if matched:
            split = value.reshape(lead + (2, 2, chips, size))
            value = jnp.moveaxis(split, -2, -4)
        return value.reshape(lead + (INNER, pair))

    def by_column(value):
        lead = value.shape[:-2]
        if matched:
            split = value.reshape(lead + (chips, 2, 2, size))
            value = jnp.moveaxis(split, -4, -2)
        return value.reshape(lead + (width,))

    def cut_columns(*weights):
        whole = jnp.concatenate([w.reshape(share, -1, width) for w in weights], axis=1)
        cut = jnp.transpose(by_device(whole), (2, 0, 1, 3))
        return cut.reshape(INNER, share, -1)

    def exchange(value):
        return lax.all_to_all(value, "inner", 0, 0)

    order = here ^ jnp.array([offset_of(n) for n in range(INNER)], jnp.int32)

    core_table = jnp.stack([2 * core, 2 - 2 * core, core, 1 - core]).astype(jnp.int32)

    def head_rows(weight, packed):
        if not matched:
            whole = lax.all_gather(weight, ALL, axis=0, tiled=True)
            mine = lax.dynamic_slice_in_dim(whole, here * pair, pair, axis=0)
            placed = jnp.take(whole.reshape(INNER, pair, width), order, axis=0)
            return mine, [placed[n] for n in range(INNER)]
        own, give = pick(core_table, packed)
        mine = merge(core_table, own, hop(give, 1))
        return mine, gather_places(mine)

    def shard_features(pieces):
        whole = jnp.stack(
            [
                piece.reshape(INNER, rows, pair)[jnp.array([n ^ place for n in range(INNER)])]
                for place, piece in enumerate(pieces)
            ]
        ).reshape(INNER, span, pair)
        whole = jnp.transpose(whole, (1, 0, 2)).reshape(span, width)
        cut = []
        for n in range(shares):
            first = (n * INNER + here) * share
            mixed = (first // pair) ^ here
            place = ((mixed >> 1) & 3) | ((mixed & 1) << 2)
            cut.append(
                lax.dynamic_slice_in_dim(whole, place * pair + first % pair, share, axis=1)
            )
        return jnp.concatenate(cut, axis=1)

    def row_grads(keep, give, pieces, branch):
        if not matched:
            grad = under(shard_features(pieces), jnp.concatenate(branch, axis=0))
            return [grad.astype(LOW).reshape(shares, share, width)]
        return [keep, hop(give, 1)]

    def rows_stack(*parts):
        if not matched:
            return jnp.concatenate([part[0] for part in parts], axis=1)
        return stack(core_table, *parts[0], *parts[1])

    def rows_home(row):
        row = row.reshape(shares * row.shape[1], width)
        return lax.psum_scatter(row, OUTER, scatter_dimension=0, tiled=True).astype(WIDE)

    def column_send(grad):
        return lax.all_to_all(grad.reshape(devices, share, -1), ALL, 0, 0)

    def column_home(got):
        if matched:
            return home_columns(got)
        total = jnp.sum(got.astype(WIDE).reshape(shares, INNER, share, -1, pair), axis=0)
        return jnp.transpose(total, (1, 2, 0, 3)).reshape(share, -1)

    small = jnp.concatenate([jnp.transpose(vectors), hidden_bias.reshape(share, -1)], axis=1)
    extras = small.shape[1]
    small = jnp.pad(small, ((0, 0), (0, LANES - extras)))
    small = jnp.broadcast_to(small[None], (INNER, share, LANES))
    first_cut = jnp.transpose(mlp_in.reshape(share, shares, INNER, hidden), (2, 0, 1, 3))
    first_cut = first_cut.reshape(INNER, share, shares * hidden)
    def over(value):
        return lax.all_gather(value, OUTER, axis=0)

    def planes_of(value):
        return [over(value).reshape(width, -1)]

    def row_lanes(weight):
        return jnp.transpose(weight.reshape(-1, INNER, LANES), (1, 0, 2))

    self_cut = jnp.concatenate([cut_columns(self_in), small], axis=2)
    self_mine = exchange(self_cut)
    self_planes = planes_of(jnp.concatenate([self_mine, row_lanes(self_out)], axis=2))
    pieces = gather_places(after(target[0], self_mine))
    cut = [cut_columns(cross_kv, cross_query), first_cut]
    states = gather_places(after(source[0], *pieces[1:4]))
    cut = exchange(after(jnp.concatenate(cut, axis=2), *states[1:4]))
    cross_mine = jnp.concatenate([cut[:, :, : 3 * pair], row_lanes(cross_out)], axis=2)
    cross_planes = planes_of(after(cross_mine, self_planes))
    first_mine = cut[:, :, 3 * pair :].reshape(INNER * share, -1)
    feed_mine = jnp.concatenate([first_mine, mlp_out], axis=0)
    feed_packed = over(after(feed_mine, self_planes))

    q, k, v, h1, params, biases, self_packed, x_all = enter(
        head_table, rows, pieces, self_planes
    )
    sout_mine, w_sout = head_rows(self_out, after(self_packed, q)[:, 4 * pair :])
    q = after(q, *w_sout[1:4])
    h_bias = self_packed.reshape(shares, INNER, share, -1)
    h_bias = h_bias[..., 3 * pair + count : 3 * pair + extras]
    h_bias = lax.dynamic_index_in_dim(h_bias, here, 1, False).reshape(1, -1).astype(WIDE)

    def stream_keys(own):
        return lax.all_gather(own, "outer", axis=0, tiled=True) if groups > 1 else own

    def own_keys(partial):
        if groups == 1:
            return partial
        return lax.psum_scatter(partial, "outer", scatter_dimension=0, tiled=True)

    k, v = stream_keys(k), stream_keys(v)
    att, self_total = attend(self_table, q, k, v, rows, True)
    att = gather_places(att)
    states, ck, cv, cross_packed = pair_heads(head_table, rows, states, cross_planes, biases)
    ck, cv = stream_keys(ck), stream_keys(cv)
    y1, h2, y1_all, cq = join_self(att, w_sout, x_all, params, cross_packed, biases)
    cout_mine, w_cout = head_rows(cross_out, after(cross_packed, *att[1:4])[:, 3 * pair :])
    catt, cross_total = attend(cross_table, cq, ck, cv, rows, False)
    catt = gather_places(catt)
    pull_up = gather_places(after(cotangent[0], *w_cout[1:4]))
    y2, h3 = join_cross(catt, w_cout, y1_all, y1, params)
    active, before_grad, give, keep, h_bias_grad, up = feed(h3, h_bias, feed_packed, pull_up)
    third_own, third_parts = scatter_places(give, keep)
    mlp_grad = feed_grad(active, before_grad, after(h3, third_own), up)
    third_parts, mlp_grad = lax.optimization_barrier((third_parts, mlp_grad))
    mlp_home = lax.psum_scatter(mlp_grad, OUTER, scatter_dimension=0, tiled=True)
    late_grad, cross_branch, late_sums = norm_back(
        4, third_own, third_parts, y2, cotangent[0], params
    )
    cross_all = gather_places(cross_branch)
    fed_own, *fed_parts = scatter_start(*feed_out(after(active, cross_all[1]), feed_packed))
    cross_all, fed_own, fed_parts = lax.optimization_barrier((cross_all, fed_own, fed_parts))
    give, keep, dcq, dck, dcv, cross_sums, row_keep, row_give = attend_back(
        cross_table,
        cq,
        ck,
        cv,
        cross_total,
        cout_mine,
        catt[0],
        cross_all,
        rows,
        False,
        (2, cross_packed),
    )
    cross_rows = (row_keep, row_give)
    fed_parts = scatter_finish(fed_parts)
    give, fed_parts = lax.optimization_barrier((give, fed_parts))
    fed = fed_own + sum(part.astype(WIDE) for part in fed_parts)
    layer_out = (y2 + fed + params[12]).astype(LOW)[None]
    dck, dcv = own_keys(dck), own_keys(dcv)
    second_own, second_parts = scatter_places(give, keep)
    cross_grad = column_part((after(states, second_own), (dck, dcv)), (h2, (dcq,)))
    source_give, source_keep = spread(0, [after(dck, second_own), dcv], cross_packed)
    second_parts, cross_grad, source_give, source_keep = lax.optimization_barrier(
        (second_parts, cross_grad, source_give, source_keep)
    )
    cross_got = column_send(cross_grad)
    cross_rows = row_grads(*cross_rows, catt, cross_all)
    middle_grad, self_branch, middle_sums = norm_back(
        2, second_own, second_parts, y1, late_grad, params
    )
    self_all = gather_places(self_branch)
    source_own, *source_parts = scatter_start(after(source_give, self_all[1]), source_keep)
    self_all, source_own, source_parts, cross_got = lax.optimization_barrier(
        (self_all, source_own, source_parts, cross_got)
    )
    dq, dk, dv, self_sums, row_keep, row_give = attend_back(
        self_table, q, k, v, self_total, sout_mine, att[0], self_all, rows, True
    )
    dk, dv = own_keys(dk), own_keys(dv)
    give, keep, target_sums = spread_self(dq, dk, dv, self_packed, x_all)
    first_own, first_parts = scatter_places(give, keep)
    self_grad = column_part((after(h1, first_own), (dq, dk, dv)))
    self_got = column_send(self_grad)
    target_grad, target_low, _ = norm_back(
        0, first_own, first_parts, target[0], middle_grad, params
    )
    source_parts, row_give, mlp_home, self_sums = lax.optimization_barrier(
        (source_parts, row_give, mlp_home, self_sums, first_parts)
    )[:4]
    self_rows = row_grads(row_keep, row_give, att, self_all)
    out_home = rows_home(rows_stack(self_rows, cross_rows))
    source_parts = scatter_finish(source_parts)
    source_grad = source_own + sum(part.astype(WIDE) for part in source_parts)
    second_home, first_home = mlp_home[:, :width], mlp_home[:, width:]
    first_home = exchange(first_home.reshape(INNER, share, shares * hidden))
    first_home = first_home.reshape(INNER, share, shares, hidden)
    first_home = jnp.transpose(first_home, (1, 2, 0, 3)).reshape(share, -1)
    cross_home = column_home(cross_got)
    self_home = column_home(self_got)

    head_sums = jnp.concatenate([self_sums, cross_sums])[:, None]
    head_sums = lax.dynamic_update_slice_in_dim(
        jnp.zeros((4, INNER, pair), WIDE), head_sums, here, 1
    )
    vector_grad = jnp.concatenate(
        [
            target_sums[:2],
            middle_sums[:2],
            late_sums[:2],
            by_column(head_sums)[:2],
            middle_sums[2:3],
            by_column(head_sums)[2:],
            late_sums[2:],
        ]
    )
    vector_part = jnp.transpose(vector_grad.reshape(count, devices, share), (1, 0, 2))
    bias_part = lax.dynamic_update_slice_in_dim(
        jnp.zeros((shares, INNER, hidden), WIDE), h_bias_grad.reshape(shares, 1, hidden), here, 1
    ).reshape(devices, hidden)
    tiny = jnp.concatenate([vector_part.reshape(devices, -1), bias_part], axis=1)
    tiny = jnp.sum(lax.all_to_all(tiny, ALL, 0, 0, tiled=True), axis=0)

    return (
        layer_out,
        target_low[None],
        source_grad.astype(LOW)[None],
        self_home,
        out_home[:share],
        cross_home[:, 2 * width :],
        cross_home[:, : 2 * width],
        out_home[share:],
        first_home.astype(WIDE),
        second_home.astype(WIDE),
        tiny[: count * share].reshape(count, share),
        tiny[count * share :],
    )


def solution(mesh):
    streams, blocks = mesh.devices.shape
    grid = mesh.devices.reshape(streams, blocks // INNER, INNER)
    inner_mesh = Mesh(grid, ALL)
    rows = P("ulys", ("outer", "inner"), None)
    matrix = P(ALL, None)
    row_vectors = P(None, ALL)
    in_specs = (rows,) * 3 + (P(), P()) + (matrix,) * 7 + (row_vectors, P(ALL))
    out_specs = (rows,) * 3 + (matrix,) * 7 + (row_vectors, P(ALL))
    return jax.shard_map(
        per_device, mesh=inner_mesh, in_specs=in_specs, out_specs=out_specs, check_vma=False
    )
```

```python
import functools

import jax
import jax.numpy as jnp
from jax import lax
from jax.experimental import pallas as pl
from jax.experimental.pallas import tpu as pltpu
from jax.sharding import Mesh
from jax.sharding import PartitionSpec as P

HEADS = 16
LOW = jnp.bfloat16
WIDE = jnp.float32
INNER = 8
STEP = 256
LANES = 128
OUTER = ("ulys", "outer")
ALL = ("ulys", "outer", "inner")


def offset_of(place):
    return ((place & 3) << 1) | (place >> 2)


def dot_t(a, b):
    return lax.dot_general(a, b, (((1,), (1,)), ((), ())), preferred_element_type=WIDE)


def dot_n(a, b):
    return lax.dot_general(a, b, (((1,), (0,)), ((), ())), preferred_element_type=WIDE)


def dot_c(a, b):
    return lax.dot_general(a, b, (((0,), (0,)), ((), ())), preferred_element_type=WIDE)


def seg_of(position, table, first):
    count = jnp.zeros_like(position)
    for n in range(3):
        count = count + (table[first + n] <= position).astype(jnp.int32)
    return count


def iota(shape, axis):
    return lax.broadcasted_iota(jnp.int32, shape, axis)


def to_order(table, source, target, rows, factor=None):
    span = rows * INNER
    for chunk in range(source.shape[0] // span):
        for place in range(INNER):
            at = pl.multiple_of((table[0] ^ offset_of(place)) * rows, rows) + chunk * span
            value = source[pl.ds(chunk * span + place * rows, rows), :]
            if factor is not None:
                value = value * factor
            target[pl.ds(at, rows), :] = value


def from_order(table, source, target, rows):
    span = rows * INNER
    for chunk in range(target.shape[0] // span):
        for place in range(INNER):
            at = pl.multiple_of((table[0] ^ offset_of(place)) * rows, rows) + chunk * span
            target[pl.ds(chunk * span + place * rows, rows), :] = source[pl.ds(at, rows), :].astype(
                target.dtype
            )


def half_lanes(value, head, size):
    lane = iota(value.shape, 1)
    keep = (lane >= head * size) & (lane < (head + 1) * size)
    return jnp.where(keep, value, jnp.zeros_like(value))


def attend_kernel(causal, rows, size, table, q, k, v, out, log_total, qs, ks, vs, ordered):
    span, keys = q.shape[0], k.shape[0]
    chunks = keys // span
    to_order(table, q, qs, rows, jnp.asarray(size**-0.5, LOW))
    to_order(table, k, ks, rows)
    to_order(table, v, vs, rows)
    for step in range(span // STEP):
        lo = step * STEP
        queries = qs[lo : lo + STEP, :]
        q_at = table[1] + lo + iota((STEP, 1), 0)
        q_seg = seg_of(q_at, table, 2)
        count = lo + STEP if causal and chunks == 1 else span

        def scores(head, start):
            k_at = start + iota((1, count), 1)
            allowed = q_seg == seg_of(k_at, table, 5)
            if causal:
                allowed = allowed & (k_at <= q_at)
            raw = dot_t(queries, half_lanes(ks[pl.ds(start, count), :], head, size))
            return jnp.where(allowed, raw, -1e30)

        parts = []
        for head in range(2):
            if chunks == 1:
                raw = scores(head, 0)
                top = jnp.max(raw, axis=1, keepdims=True)
                weight = jnp.exp(raw - top)
                total = jnp.sum(weight, axis=1, keepdims=True)
                running = dot_n(weight.astype(LOW), vs[:count, :])
            else:

                def absorb(chunk, carry, head=head):
                    top, total, running = carry
                    start = pl.multiple_of(chunk * span, span)
                    raw = scores(head, start)
                    new_top = jnp.maximum(top, jnp.max(raw, axis=1, keepdims=True))
                    weight = jnp.exp(raw - new_top)
                    fade = jnp.exp(top - new_top)
                    total = total * fade + jnp.sum(weight, axis=1, keepdims=True)
                    running = running * fade + dot_n(weight.astype(LOW), vs[pl.ds(start, span), :])
                    return new_top, total, running

                top, total, running = lax.fori_loop(
                    0,
                    chunks,
                    absorb,
                    (
                        jnp.full((STEP, 1), -1e30, WIDE),
                        jnp.zeros((STEP, 1), WIDE),
                        jnp.zeros((STEP, 2 * size), WIDE),
                    ),
                )
            parts.append(running / total)
            logs = jnp.broadcast_to(top + jnp.log(total), (STEP, 2 * size))
            log_total[head : head + 1, lo : lo + STEP] = jnp.transpose(logs)[0:1, :]
        lane = iota((STEP, 2 * size), 1)
        ordered[lo : lo + STEP, :] = jnp.where(lane < size, parts[0], parts[1])
    from_order(table, ordered, out, rows)


def split_rows(table, first, own, branch, row, keep, give):
    row[...] = dot_c(own[...], branch[...]).astype(LOW)
    share = keep.shape[1]
    for core, out in ((table[first], keep), (table[first + 1], give)):
        for n in range(2):
            at = pl.multiple_of((2 * n + core) * share, share)
            out[n] = row[pl.ds(at, share), :]


def attend_back_kernel(causal, rows, size, start, lined, table, q, k, v, log_total, weight, *refs):
    own = refs[0] if lined else None
    refs = refs[1:] if lined else refs
    pieces, refs = refs[:INNER], refs[INNER:]
    if start is not None:
        packed, refs = refs[0], refs[1:]
        if start == 0:
            x_all, refs = refs[0], refs[1:]
            give, keep, norm_sums, refs = *refs[:3], refs[3:]
        else:
            give, keep, refs = *refs[:2], refs[2:]
    dq, dk, dv, sums, refs = *refs[:4], refs[4:]
    if lined:
        row_keep, row_give, refs = *refs[:2], refs[2:]
    qs, ks, vs, ups, dqs, dks, dvs, branch, row, marks = refs
    copies = pull(pieces, 0, branch, marks)
    span, keys = q.shape[0], k.shape[0]
    chunks = keys // span
    scale = size**-0.5
    to_order(table, q, qs, rows, jnp.asarray(scale, LOW))
    to_order(table, k, ks, rows)
    to_order(table, v, vs, rows)
    finish(copies)
    upstream = dot_t(branch[...], weight[...]).astype(LOW)
    for place in range(INNER):
        at = pl.multiple_of((table[0] ^ offset_of(place)) * rows, rows)
        ups[pl.ds(at, rows), :] = upstream[place * rows : (place + 1) * rows, :]
    if lined:
        split_rows(table, 8, own, branch, row, row_keep, row_give)
    dks[...] = jnp.zeros_like(dks)
    dvs[...] = jnp.zeros_like(dvs)
    for step in range(span // STEP):
        lo = step * STEP
        queries = qs[lo : lo + STEP, :]
        upstream = ups[lo : lo + STEP, :]
        q_at = table[1] + lo + iota((1, STEP), 1)
        q_seg = seg_of(q_at, table, 2)
        count = lo + STEP if causal and chunks == 1 else span
        total_dq = jnp.zeros((STEP, 2 * size), WIDE)
        for head in range(2):
            head_q = half_lanes(queries, head, size)
            head_up = half_lanes(upstream, head, size)
            logs = log_total[head : head + 1, lo : lo + STEP]

            def pieces(start, logs=logs, head_up=head_up, head=head):
                k_at = start + iota((count, 1), 0)
                allowed = q_seg == seg_of(k_at, table, 5)
                if causal:
                    allowed = allowed & (k_at <= q_at)
                head_k = half_lanes(ks[pl.ds(start, count), :], head, size)
                raw = dot_t(head_k, queries)
                probs = jnp.exp(jnp.where(allowed, raw - logs, -1e30))
                slope = dot_t(vs[pl.ds(start, count), :], head_up)
                return head_k, probs, probs * slope

            def spread(start, delta, made, head_q=head_q, head_up=head_up):
                head_k, probs, lean = made
                push = (lean - probs * delta).astype(LOW)
                dvs[pl.ds(start, count), :] += dot_n(probs.astype(LOW), head_up)
                dks[pl.ds(start, count), :] += dot_n(push, head_q)
                return dot_c(push, head_k)

            if chunks == 1:
                made = pieces(0)
                delta = jnp.sum(made[2], axis=0, keepdims=True)
                total_dq = total_dq + spread(0, delta, made)
            else:

                def measure(chunk, delta):
                    made = pieces(pl.multiple_of(chunk * span, span))
                    return delta + jnp.sum(made[2], axis=0, keepdims=True)

                delta = lax.fori_loop(0, chunks, measure, jnp.zeros((1, STEP), WIDE))

                def absorb(chunk, running, delta=delta):
                    start = pl.multiple_of(chunk * span, span)
                    return running + spread(start, delta, pieces(start))

                total_dq = lax.fori_loop(0, chunks, absorb, total_dq)
        dqs[lo : lo + STEP, :] = total_dq * scale
    from_order(table, dqs, dq, rows)
    from_order(table, dks, dk, rows)
    from_order(table, dvs, dv, rows)
    if start is not None:
        kinds = 3 if start == 0 else 1
        back = packed[:, start * LANES : (start + kinds) * LANES]
        first = second = None
        for at, out in ((span // 2, give), (0, keep)):
            at = slice(at, at + span // 2)
            left = [part[at, :] for part in (dq, dk, dv)[:kinds]]
            left = left[0] if kinds == 1 else jnp.concatenate(left, axis=1)
            slope = dot_t(left, back)
            out[...] = slope.astype(out.dtype)
            if start == 0:
                centred, inverse = centre(x_all[at, :].astype(WIDE))
                gain = jnp.sum(slope * (centred * inverse), axis=0, keepdims=True)
                shift = jnp.sum(slope, axis=0, keepdims=True)
                first = gain if first is None else first + gain
                second = shift if second is None else second + shift
        if start == 0:
            norm_sums[0:1, :] = first
            norm_sums[1:2, :] = second
    sums[0:1, :] = jnp.sum(dqs[...].astype(LOW).astype(WIDE), axis=0, keepdims=True)
    sums[1:2, :] = jnp.sum(dvs[...].astype(LOW).astype(WIDE), axis=0, keepdims=True)


HBM = pl.BlockSpec(memory_space=pl.ANY)


def room(megabytes):
    return pltpu.CompilerParams(vmem_limit_bytes=megabytes * 2**20)


def pull(pieces, index, target, marks):
    rows = target.shape[0] // INNER
    copies = []
    for place in range(INNER):
        source = pieces[place].at[pl.ds(index * rows, rows), :]
        aim = target.at[pl.ds(place * rows, rows), :]
        copies.append(pltpu.make_async_copy(source, aim, marks.at[place]))
    for copy in copies:
        copy.start()
    return copies


def finish(copies):
    for copy in copies:
        copy.wait()


def cost(micros):
    return pl.CostEstimate(
        flops=int(micros * 1.1e9), bytes_accessed=int(micros * 3.5e6), transcendentals=0
    )


SMEM = pl.BlockSpec(memory_space=pltpu.SMEM)
VMEM = pl.BlockSpec(memory_space=pltpu.VMEM)


def attend(table, q, k, v, rows, causal):
    span, pair = q.shape
    keys = k.shape[0]
    return pl.pallas_call(
        functools.partial(attend_kernel, causal, rows, pair // 2),
        out_shape=(
            jax.ShapeDtypeStruct((span, pair), LOW),
            jax.ShapeDtypeStruct((2, span), WIDE),
        ),
        in_specs=[SMEM, VMEM, VMEM, VMEM],
        out_specs=(VMEM, VMEM),
        scratch_shapes=[
            pltpu.VMEM((span, pair), LOW),
            pltpu.VMEM((keys, pair), LOW),
            pltpu.VMEM((keys, pair), LOW),
            pltpu.VMEM((span, pair), WIDE),
        ],
        compiler_params=room(60),
        cost_estimate=cost(6),
    )(table, q, k, v)


def attend_back(table, q, k, v, log_total, weight, own, pieces, rows, causal, back=None):
    span, pair = q.shape
    keys = k.shape[0]
    width = weight.shape[1]
    part = jax.ShapeDtypeStruct((2, pair // 4, width), LOW)
    lined = [] if own is None else [own]
    spread_shape = (
        jax.ShapeDtypeStruct((span // 2, width), LOW),
        jax.ShapeDtypeStruct((span // 2, width), WIDE),
    )
    start, *extra = back if back else (None,)
    if start == 0:
        spread_shape += (jax.ShapeDtypeStruct((2, width), WIDE),)
    return pl.pallas_call(
        functools.partial(attend_back_kernel, causal, rows, pair // 2, start, bool(lined)),
        out_shape=(spread_shape if back else ())
        + (
            jax.ShapeDtypeStruct((span, pair), LOW),
            jax.ShapeDtypeStruct((keys, pair), LOW),
            jax.ShapeDtypeStruct((keys, pair), LOW),
            jax.ShapeDtypeStruct((2, pair), WIDE),
        )
        + ((part, part) if lined else ()),
        in_specs=[SMEM] + [VMEM] * (5 + len(lined)) + [HBM] * INNER + [VMEM] * len(extra),
        out_specs=(VMEM,) * (4 + 2 * len(lined) + (len(spread_shape) if back else 0)),
        scratch_shapes=[
            pltpu.VMEM((span, pair), LOW),
            pltpu.VMEM((keys, pair), LOW),
            pltpu.VMEM((keys, pair), LOW),
            pltpu.VMEM((span, pair), LOW),
            pltpu.VMEM((span, pair), WIDE),
            pltpu.VMEM((keys, pair), WIDE),
            pltpu.VMEM((keys, pair), WIDE),
            pltpu.VMEM((span, width), LOW),
            pltpu.VMEM((pair, width), LOW),
            pltpu.SemaphoreType.DMA((INNER,)),
        ],
        compiler_params=room(60),
        cost_estimate=cost(10),
    )(table, q, k, v, log_total, weight, *lined, *pieces, *extra)


def centre(value):
    center = jnp.mean(value, axis=-1, keepdims=True)
    centred = value - center
    spread = jnp.mean(centred * centred, axis=-1, keepdims=True)
    return centred, lax.rsqrt(spread + 1e-05)


def norm_of(value, gain, shift):
    centred, inverse = centre(value)
    return (centred * inverse * gain + shift).astype(LOW)


def enter_kernel(kinds, table, far, *refs):
    pieces, refs = refs[:INNER], refs[INNER:]
    q, k, v, h, params, biases, packed, x_all, marks, mark = refs
    load = pltpu.make_async_copy(far.at[:, pl.ds(0, packed.shape[1])], packed, mark)
    load.start()
    copies = pull(pieces, 0, x_all, marks)
    load.wait()
    edge = kinds * LANES
    extra = packed[:, edge : edge + LANES].astype(WIDE)
    params[...] = jnp.transpose(extra)[:16, :]
    size = LANES // 2
    mine = [packed[pl.ds(pl.multiple_of(table[n], 16), size), edge : edge + LANES] for n in (0, 1)]
    biases[...] = jnp.transpose(jnp.concatenate(mine, axis=0).astype(WIDE))[:16, :]
    finish(copies)
    half = x_all.shape[0] // 2
    for part in range(2):
        at = slice(part * half, (part + 1) * half)
        low = norm_of(x_all[at, :].astype(WIDE), params[0:1, :], params[1:2, :])
        h[at, :] = low
        made = dot_n(low, packed[:, :edge])
        q[at, :] = (made[:, :LANES] + biases[6:7, :]).astype(LOW)
        k[at, :] = made[:, LANES : 2 * LANES].astype(LOW)
        v[at, :] = (made[:, 2 * LANES :] + biases[7:8, :]).astype(LOW)


def enter(table, rows, pieces, packed):
    width = pieces[0].shape[1]
    span = rows * INNER
    heads = jax.ShapeDtypeStruct((span, LANES), LOW)
    return pl.pallas_call(
        functools.partial(enter_kernel, 3),
        out_shape=(
            heads,
            heads,
            heads,
            jax.ShapeDtypeStruct((span, width), LOW),
            jax.ShapeDtypeStruct((16, width), WIDE),
            jax.ShapeDtypeStruct((16, LANES), WIDE),
            jax.ShapeDtypeStruct((width, 4 * LANES), LOW),
            jax.ShapeDtypeStruct((span, width), LOW),
        ),
        in_specs=[SMEM] + [HBM] * (1 + INNER),
        out_specs=(VMEM,) * 8,
        scratch_shapes=[pltpu.SemaphoreType.DMA((INNER,)), pltpu.SemaphoreType.DMA],
        compiler_params=room(60),
        cost_estimate=cost(4),
    )(table, packed, *pieces)


def join_kernel(vector, first, query, *refs):
    pieces, weights, refs = refs[:INNER], refs[INNER : 2 * INNER], refs[2 * INNER :]
    if query is None:
        base, base_own, params, y_own, h, weight, left, heads, marks = refs
    else:
        base, params, packed, biases, y_own, h, y_all, cq, weight, left, heads, marks = refs
    span = left.shape[0]
    block = span // INNER
    loads = pull(weights, 0, weight, marks.at[1])
    copies = []
    for place in range(INNER):
        copies.append(pltpu.make_async_copy(pieces[place], heads.at[place], marks.at[0, place]))
    for copy in copies:
        copy.start()
    finish(copies + loads)
    parts = INNER // 2
    for part in range(parts):
        at = slice(part * 2 * block, (part + 1) * 2 * block)
        for n in range(2 * part, 2 * part + 2):
            for place in range(INNER):
                first_row = (n ^ place) * block
                left[n * block : (n + 1) * block, place * LANES : (place + 1) * LANES] = heads[
                    place, first_row : first_row + block, :
                ]
        value = base[at, :].astype(WIDE)
        if query is None and part == 0:
            value = jnp.concatenate([base_own[...], value[block:, :]], axis=0)
        y = value + dot_n(left[at, :], weight[...]) + params[vector : vector + 1, :]
        if part == 0:
            y_own[...] = y[:block, :]
        low = norm_of(y, params[first : first + 1, :], params[first + 1 : first + 2, :])
        h[at, :] = low
        if query is not None:
            y_all[at, :] = y.astype(LOW)
            made = dot_n(low, packed[:, query * LANES : (query + 1) * LANES])
            cq[at, :] = (made + biases[9:10, :]).astype(LOW)


def join_self(pieces, weights, base, params, packed, biases):
    span, width = base.shape
    return pl.pallas_call(
        functools.partial(join_kernel, 8, 2, 2),
        out_shape=(
            jax.ShapeDtypeStruct((span // INNER, width), WIDE),
            jax.ShapeDtypeStruct((span, width), LOW),
            jax.ShapeDtypeStruct((span, width), LOW),
            jax.ShapeDtypeStruct((span, LANES), LOW),
        ),
        in_specs=[HBM] * (2 * INNER) + [VMEM] * 4,
        out_specs=(VMEM,) * 4,
        scratch_shapes=[
            pltpu.VMEM((width, width), LOW),
            pltpu.VMEM((span, width), LOW),
            pltpu.VMEM((INNER, span, LANES), LOW),
            pltpu.SemaphoreType.DMA((2, INNER)),
        ],
        compiler_params=room(60),
        cost_estimate=cost(6),
    )(*pieces, *weights, base, params, packed, biases)


def join_cross(pieces, weights, base, base_own, params):
    span, width = base.shape
    return pl.pallas_call(
        functools.partial(join_kernel, 11, 4, None),
        out_shape=(
            jax.ShapeDtypeStruct((span // INNER, width), WIDE),
            jax.ShapeDtypeStruct((span, width), LOW),
        ),
        in_specs=[HBM] * (2 * INNER) + [VMEM] * 3,
        out_specs=(VMEM,) * 2,
        scratch_shapes=[
            pltpu.VMEM((width, width), LOW),
            pltpu.VMEM((span, width), LOW),
            pltpu.VMEM((INNER, span, LANES), LOW),
            pltpu.SemaphoreType.DMA((2, INNER)),
        ],
        compiler_params=room(60),
        cost_estimate=cost(5),
    )(*pieces, *weights, base, base_own, params)


def load_rows(packed, start, target, marks):
    shares = packed.shape[0]
    rows = target.shape[0] // shares
    copies = []
    for n in range(shares):
        source = packed.at[n, pl.ds(start, rows), :]
        aim = target.at[pl.ds(n * rows, rows), :]
        copies.append(pltpu.make_async_copy(source, aim, marks.at[n]))
    for copy in copies:
        copy.start()
    return copies


def feed_kernel(h, bias, packed, *refs):
    pieces = refs[:INNER]
    act, slope, give, keep, bias_grad, up, first, second, marks, weight_marks = refs[INNER:]
    span, width = up.shape
    hidden = second.shape[0]
    loads = load_rows(packed, 0, first, weight_marks.at[0])
    copies = load_rows(packed, width // packed.shape[0], second, weight_marks.at[1])
    copies += pull(pieces, 0, up, marks)
    finish(loads)
    step = 256
    inner = (2.0 / 3.141592653589793) ** 0.5
    for n in range(hidden // step):
        at = slice(n * step, (n + 1) * step)
        pre = dot_n(h[...], first[:, at]) + bias[:, at]
        square = pre * pre
        bend = jnp.tanh(pre * (inner + (inner * 0.044715) * square))
        half = 0.5 * bend + 0.5
        act[:, at] = (pre * half).astype(LOW)
        if n == 0:
            finish(copies)
        rise = half + 0.5 * pre * (1.0 - bend * bend) * (inner + (3 * inner * 0.044715) * square)
        low = (dot_t(up[...], second[at, :]) * rise).astype(LOW)
        slope[:, at] = low
        bias_grad[:, at] = jnp.sum(low.astype(WIDE), axis=0, keepdims=True)
    give[...] = dot_t(slope[span // 2 :, :], first[...]).astype(LOW)
    keep[...] = dot_t(slope[: span // 2, :], first[...])


def feed(h, bias, packed, pieces):
    span, width = h.shape
    hidden = bias.shape[1]
    shares = packed.shape[0]
    return pl.pallas_call(
        feed_kernel,
        out_shape=(
            jax.ShapeDtypeStruct((span, hidden), LOW),
            jax.ShapeDtypeStruct((span, hidden), LOW),
            jax.ShapeDtypeStruct((span // 2, width), LOW),
            jax.ShapeDtypeStruct((span // 2, width), WIDE),
            jax.ShapeDtypeStruct((1, hidden), WIDE),
            jax.ShapeDtypeStruct((span, width), LOW),
        ),
        in_specs=[VMEM] * 2 + [HBM] * (1 + INNER),
        out_specs=(VMEM,) * 6,
        scratch_shapes=[
            pltpu.VMEM((width, hidden), LOW),
            pltpu.VMEM((hidden, width), LOW),
            pltpu.SemaphoreType.DMA((INNER,)),
            pltpu.SemaphoreType.DMA((2, shares)),
        ],
        compiler_params=room(44),
        cost_estimate=cost(13),
    )(h, bias, packed, *pieces)


def side_kernel(act, packed, dk, dv, pair_weight, give, keep, second, marks):
    copies = load_rows(packed, second.shape[1] // packed.shape[0], second, marks)
    half, width = keep.shape[0], second.shape[1]
    weight = pair_weight[:, : 2 * LANES]
    spans = ((half, give), (0, keep))
    for at, out in spans:
        left = jnp.concatenate([dk[at : at + half, :], dv[at : at + half, :]], axis=1)
        out[:, width:] = dot_t(left, weight).astype(out.dtype)
    finish(copies)
    for at, out in spans:
        out[:, :width] = dot_n(act[at : at + half, :], second[...]).astype(out.dtype)


def side_out(act, packed, dk, dv, pair_weight):
    span, hidden = act.shape
    shares, _, width = packed.shape
    return pl.pallas_call(
        side_kernel,
        out_shape=(
            jax.ShapeDtypeStruct((span // 2, 2 * width), LOW),
            jax.ShapeDtypeStruct((span // 2, 2 * width), WIDE),
        ),
        in_specs=[VMEM, HBM] + [VMEM] * 3,
        out_specs=(VMEM,) * 2,
        scratch_shapes=[
            pltpu.VMEM((hidden, width), LOW),
            pltpu.SemaphoreType.DMA((shares,)),
        ],
        compiler_params=room(24),
        cost_estimate=cost(4),
    )(act, packed, dk, dv, pair_weight)


def side_sum_kernel(own, one, two, three, y, params, layer, source):
    total = own[...] + one[...].astype(WIDE) + two[...].astype(WIDE) + three[...].astype(WIDE)
    width = y.shape[1]
    layer[...] = (y[...] + total[:, :width] + params[12:13, :]).astype(LOW)
    source[...] = total[:, width:].astype(LOW)


def side_sum(own, parts, y, params):
    out = jax.ShapeDtypeStruct(y.shape, LOW)
    return pl.pallas_call(
        side_sum_kernel,
        out_shape=(out, out),
        in_specs=[VMEM] * 6,
        out_specs=(VMEM,) * 2,
        compiler_params=room(16),
        cost_estimate=cost(1),
    )(own, *parts, y, params)


def feed_grad_kernel(act, slope, h, up, out):
    width = up.shape[1]
    step = 256
    for n in range(width // step):
        at = slice(n * step, (n + 1) * step)
        out[at, width:] = dot_c(h[:, at], slope[...]).astype(LOW)
    for n in range(act.shape[1] // step):
        at = slice(n * step, (n + 1) * step)
        out[at, :width] = dot_c(act[:, at], up[...]).astype(LOW)


def feed_grad(act, slope, h, up):
    width = h.shape[1]
    hidden = act.shape[1]
    return pl.pallas_call(
        feed_grad_kernel,
        out_shape=jax.ShapeDtypeStruct((width, width + hidden), LOW),
        in_specs=[VMEM] * 4,
        out_specs=VMEM,
        compiler_params=room(40),
        cost_estimate=cost(6),
    )(act, slope, h, up)


def fold_kernel(keep, took, own, one, two, three):
    rows = own.shape[0]
    own[...] = keep[:rows, :] + took[:rows, :].astype(WIDE)
    for n, part in enumerate((one, two, three), 1):
        at = slice(n * rows, (n + 1) * rows)
        part[...] = (keep[at, :] + took[at, :].astype(WIDE)).astype(LOW)


def fold(keep, took):
    half, width = keep.shape
    part = jax.ShapeDtypeStruct((half // 4, width), LOW)
    return pl.pallas_call(
        fold_kernel,
        out_shape=(jax.ShapeDtypeStruct((half // 4, width), WIDE), part, part, part),
        in_specs=[VMEM] * 2,
        out_specs=(VMEM,) * 4,
        compiler_params=room(16),
        cost_estimate=cost(1),
    )(keep, took)


def norm_back_kernel(first, own, one, two, three, value, base, params, grad, low, sums):
    slope = own[...] + one[...].astype(WIDE) + two[...].astype(WIDE) + three[...].astype(WIDE)
    centred, inverse = centre(value[...].astype(WIDE))
    unit = centred * inverse
    lean = slope * params[first : first + 1, :]
    flat = jnp.mean(lean, axis=-1, keepdims=True)
    tilt = jnp.mean(lean * unit, axis=-1, keepdims=True)
    total = base[...].astype(WIDE) + inverse * (lean - flat - unit * tilt)
    grad[...] = total
    cut = total.astype(LOW)
    low[...] = cut
    sums[0:1, :] = jnp.sum(slope * unit, axis=0, keepdims=True)
    sums[1:2, :] = jnp.sum(slope, axis=0, keepdims=True)
    sums[2:3, :] = jnp.sum(cut.astype(WIDE), axis=0, keepdims=True)
    sums[3:4, :] = jnp.sum(base[...].astype(WIDE), axis=0, keepdims=True)


def norm_back(first, own, parts, value, base, params):
    rows, width = own.shape
    return pl.pallas_call(
        functools.partial(norm_back_kernel, first),
        out_shape=(
            jax.ShapeDtypeStruct((rows, width), WIDE),
            jax.ShapeDtypeStruct((rows, width), LOW),
            jax.ShapeDtypeStruct((4, width), WIDE),
        ),
        in_specs=[VMEM] * 7,
        out_specs=(VMEM,) * 3,
        compiler_params=room(16),
        cost_estimate=cost(2),
    )(own, *parts, value, base, params)


def pair_kernel(biases, far, *refs):
    pieces, (states, k, v, packed, marks, mark) = refs[:INNER], refs[INNER:]
    load = pltpu.make_async_copy(far.at[:, pl.ds(0, packed.shape[1])], packed, mark)
    load.start()
    finish(pull(pieces, 0, states, marks) + [load])
    made = dot_n(states[...], packed[:, : 2 * LANES])
    k[...] = made[:, :LANES].astype(LOW)
    v[...] = (made[:, LANES:] + biases[10:11, :]).astype(LOW)


def pair_heads(rows, pieces, packed, biases):
    width = pieces[0].shape[1]
    span = rows * INNER
    heads = jax.ShapeDtypeStruct((span, LANES), LOW)
    return pl.pallas_call(
        pair_kernel,
        out_shape=(
            jax.ShapeDtypeStruct((span, width), LOW),
            heads,
            heads,
            jax.ShapeDtypeStruct((width, 3 * LANES), LOW),
        ),
        in_specs=[VMEM] + [HBM] * (1 + INNER),
        out_specs=(VMEM,) * 4,
        scratch_shapes=[pltpu.SemaphoreType.DMA((INNER,)), pltpu.SemaphoreType.DMA],
        compiler_params=room(60),
        cost_estimate=cost(3),
    )(biases, packed, *pieces)


def spread_self_kernel(dq, dk, dv, packed, x_all, give, keep, sums):
    half = x_all.shape[0] // 2
    weight = packed[:, : 3 * LANES]
    first = second = None
    for part, out in ((1, give), (0, keep)):
        at = slice(part * half, (part + 1) * half)
        left = jnp.concatenate([dq[at, :], dk[at, :], dv[at, :]], axis=1)
        slope = dot_t(left, weight)
        out[...] = slope.astype(out.dtype)
        centred, inverse = centre(x_all[at, :].astype(WIDE))
        gain = jnp.sum(slope * (centred * inverse), axis=0, keepdims=True)
        shift = jnp.sum(slope, axis=0, keepdims=True)
        first = gain if first is None else first + gain
        second = shift if second is None else second + shift
    sums[0:1, :] = first
    sums[1:2, :] = second


def spread_self(dq, dk, dv, packed, x_all):
    span, width = x_all.shape
    return pl.pallas_call(
        spread_self_kernel,
        out_shape=(
            jax.ShapeDtypeStruct((span // 2, width), LOW),
            jax.ShapeDtypeStruct((span // 2, width), WIDE),
            jax.ShapeDtypeStruct((2, width), WIDE),
        ),
        in_specs=[VMEM] * 5,
        out_specs=(VMEM,) * 3,
        compiler_params=room(32),
        cost_estimate=cost(4),
    )(dq, dk, dv, packed, x_all)


def spread_columns(got, kinds, out):
    size = LANES // 2
    for kind in range(kinds):
        heads = {}
        for place in range(INNER):
            for n in (0, 1):
                at = kind * LANES + n * size
                number = (2 * (place & 1) + n) * (INNER // 2) + (place >> 1)
                heads[number] = got[place][:, at : at + size].astype(WIDE)
        for number in range(0, 2 * INNER, 2):
            at = kind * INNER * LANES + number * size
            both = jnp.concatenate([heads[number], heads[number + 1]], axis=1)
            out[:, at : at + LANES] = both


def spread_rows(packed, start, out):
    share = out.shape[0]
    for place in range(INNER):
        block = packed[place * share : (place + 1) * share, start : start + LANES]
        out[:, place * LANES : (place + 1) * LANES] = block.astype(WIDE)


def home_kernel(kinds, got, packed, columns, rows):
    spread_columns(got, kinds, columns)
    spread_rows(packed, kinds * LANES, rows)


def home(got, packed):
    share, lanes = got.shape[1:]
    return pl.pallas_call(
        functools.partial(home_kernel, lanes // LANES),
        out_shape=(
            jax.ShapeDtypeStruct((share, lanes * INNER), WIDE),
            jax.ShapeDtypeStruct((share, LANES * INNER), WIDE),
        ),
        in_specs=[VMEM] * 2,
        out_specs=(VMEM,) * 2,
        compiler_params=room(16),
        cost_estimate=cost(2),
    )(got, packed)


def home_feed_kernel(kinds, hidden, got, packed, feed_sum, *outs):
    columns, rows, first, second = outs
    spread_columns(got, kinds, columns)
    spread_rows(packed, kinds * LANES, rows)
    width = second.shape[1]
    second[...] = feed_sum[:, :width].astype(WIDE)
    lanes = got.shape[2] - kinds * LANES
    for n in range(lanes // hidden):
        for place in range(INNER):
            at = (n * INNER + place) * hidden
            start = kinds * LANES + n * hidden
            first[:, at : at + hidden] = got[place, :, start : start + hidden].astype(WIDE)


def home_feed(kinds, hidden, got, packed, feed_sum):
    share, lanes = got.shape[1:]
    rows = jax.ShapeDtypeStruct((share, LANES * INNER), WIDE)
    return pl.pallas_call(
        functools.partial(home_feed_kernel, kinds, hidden),
        out_shape=(
            jax.ShapeDtypeStruct((share, kinds * LANES * INNER), WIDE),
            rows,
            jax.ShapeDtypeStruct((share, (lanes - kinds * LANES) * INNER), WIDE),
            jax.ShapeDtypeStruct((feed_sum.shape[0], LANES * INNER), WIDE),
        ),
        in_specs=[VMEM] * 3,
        out_specs=(VMEM,) * 4,
        compiler_params=room(24),
        cost_estimate=cost(3),
    )(got, packed, feed_sum)


def column_part_kernel(kinds, *refs):
    count = len(kinds)
    lefts, rights, column = refs[:count], refs[count:-1], refs[-1]
    at = first = 0
    for left, kind in zip(lefts, kinds):
        right = [value[...] for value in rights[first : first + kind]]
        right = right[0] if kind == 1 else jnp.concatenate(right, axis=1)
        lanes = kind * LANES
        column[:, at : at + lanes] = dot_c(left[...], right).astype(LOW)
        at, first = at + lanes, first + kind


def column_part(*pairs):
    width = pairs[0][0].shape[1]
    kinds = tuple(len(rights) for _, rights in pairs)
    lefts = [left for left, _ in pairs]
    rights = [value for _, values in pairs for value in values]
    return pl.pallas_call(
        functools.partial(column_part_kernel, kinds),
        out_shape=jax.ShapeDtypeStruct((width, LANES * sum(kinds)), LOW),
        in_specs=[VMEM] * (len(lefts) + len(rights)),
        out_specs=VMEM,
        compiler_params=room(24),
        cost_estimate=cost(3),
    )(*lefts, *rights)


def pick_kernel(table, packed, own, give):
    share = own.shape[1]
    for first, out in ((table[0], own), (table[1], give)):
        for n in range(2):
            for place in range(INNER):
                at = pl.multiple_of(((first + n) * INNER + place) * share, share)
                out[n, :, place * LANES : (place + 1) * LANES] = packed[pl.ds(at, share), :]


def pick(table, packed):
    width = packed.shape[0]
    part = jax.ShapeDtypeStruct((2, width // (4 * INNER), width), LOW)
    return pl.pallas_call(
        pick_kernel,
        out_shape=(part, part),
        in_specs=[SMEM, VMEM],
        out_specs=(VMEM,) * 2,
        compiler_params=room(16),
        cost_estimate=cost(1),
    )(table, packed)


def merge_kernel(table, own, took, out):
    share = own.shape[1]
    for n in range(2):
        for core, value in ((table[2], own), (table[3], took)):
            first = pl.multiple_of((2 * n + core) * share, share)
            out[pl.ds(first, share), :] = value[n]


def merge(table, own, took):
    _, rows, width = own.shape
    return pl.pallas_call(
        merge_kernel,
        out_shape=jax.ShapeDtypeStruct((4 * rows, width), LOW),
        in_specs=[SMEM, VMEM, VMEM],
        out_specs=VMEM,
        compiler_params=room(16),
        cost_estimate=cost(1),
    )(table, own, took)


def pack_kernel(table, columns, *refs):
    rows, out = refs[:-1], refs[-1]
    lanes = columns.shape[1]
    out[:, :lanes] = columns[...]
    share = rows[0].shape[1]
    for kind in range(len(rows) // 2):
        for first, value in ((table[0], rows[2 * kind]), (table[1], rows[2 * kind + 1])):
            for n in range(2):
                for place in range(INNER):
                    at = pl.multiple_of(((first + n) * INNER + place) * share, share)
                    start = lanes + kind * LANES
                    block = value[n, :, place * LANES : (place + 1) * LANES]
                    out[pl.ds(at, share), start : start + LANES] = block


def pack(table, columns, *rows):
    width, lanes = columns.shape
    lanes += LANES * len(rows) // 2
    return pl.pallas_call(
        pack_kernel,
        out_shape=jax.ShapeDtypeStruct((width, lanes), LOW),
        in_specs=[SMEM] + [VMEM] * (1 + len(rows)),
        out_specs=VMEM,
        compiler_params=room(16),
        cost_estimate=cost(2),
    )(table, columns, *rows)


def hop(value, distance):
    route = [(n, n ^ distance) for n in range(INNER)]
    return lax.ppermute(value, "inner", route)


def after(value, *others):
    return lax.optimization_barrier((value,) + others)[0]


def gather_places(own, *filler):
    near = [own] + [hop(own, offset_of(place)) for place in (1, 2, 3)]
    if filler:
        near, filler = lax.optimization_barrier((near, filler))
    pieces = near + [hop(piece, 1) for piece in near]
    return (pieces, *filler) if filler else pieces


def scatter_start(give, keep):
    return fold(keep, hop(give, 1))


def scatter_finish(parts):
    return [hop(part, offset_of(place)) for place, part in enumerate(parts, 1)]


def scatter_places(give, keep):
    own, *parts = scatter_start(give, keep)
    return own, scatter_finish(parts)


def dot(a, b):
    return jnp.dot(a, b, preferred_element_type=WIDE)


def under(a, b):
    return lax.dot_general(a, b, (((0,), (0,)), ((), ())), preferred_element_type=WIDE)


def per_device(
    target,
    source,
    cotangent,
    target_lengths,
    source_lengths,
    self_in,
    self_out,
    cross_query,
    cross_kv,
    cross_out,
    mlp_in,
    mlp_out,
    vectors,
    hidden_bias,
):
    rows, width = target.shape[1:]
    here = lax.axis_index("inner")
    core, chip = here & 1, here >> 1
    stream = lax.axis_index("ulys")
    group = lax.axis_index("outer")
    groups = lax.axis_size("outer")
    shares = lax.axis_size("ulys") * groups
    devices = shares * INNER
    span = rows * INNER
    pair = width // INNER
    size = pair // 2
    share = width // devices
    hidden = hidden_bias.shape[0]
    count = vectors.shape[0]
    chips = INNER // 2
    matched = shares * chips == HEADS and 2 * share == size
    target_ends = jnp.cumsum(target_lengths[stream])
    source_ends = jnp.cumsum(source_lengths[stream])
    start = jnp.stack([here, group * span]).astype(jnp.int32)
    cores = jnp.stack([core, 1 - core])
    self_table = jnp.concatenate([start, target_ends, target_ends, cores]).astype(jnp.int32)
    cross_table = jnp.concatenate([start, target_ends, source_ends, cores]).astype(jnp.int32)
    if matched:
        head_at = [(2 * core + n) * (width // shares) + chip * size for n in (0, 1)]
    else:
        head_at = [here * pair + n * size for n in (0, 1)]
    head_table = jnp.stack(head_at).astype(jnp.int32)

    def by_device(value):
        lead = value.shape[:-1]
        if matched:
            split = value.reshape(lead + (2, 2, chips, size))
            value = jnp.moveaxis(split, -2, -4)
        return value.reshape(lead + (INNER, pair))

    def by_column(value):
        lead = value.shape[:-2]
        if matched:
            split = value.reshape(lead + (chips, 2, 2, size))
            value = jnp.moveaxis(split, -4, -2)
        return value.reshape(lead + (width,))

    def cut_columns(*weights):
        whole = jnp.concatenate([w.reshape(share, -1, width) for w in weights], axis=1)
        cut = jnp.transpose(by_device(whole), (2, 0, 1, 3))
        return cut.reshape(INNER, share, -1)

    def exchange(value):
        return lax.all_to_all(value, "inner", 0, 0)

    order = here ^ jnp.array([offset_of(n) for n in range(INNER)], jnp.int32)

    core_table = jnp.stack([2 * core, 2 - 2 * core, core, 1 - core]).astype(jnp.int32)

    def head_rows(weight, packed):
        if not matched:
            whole = lax.all_gather(weight, ALL, axis=0, tiled=True)
            mine = lax.dynamic_slice_in_dim(whole, here * pair, pair, axis=0)
            placed = jnp.take(whole.reshape(INNER, pair, width), order, axis=0)
            return mine, [placed[n] for n in range(INNER)]
        own, give = pick(core_table, packed)
        mine = merge(core_table, own, hop(give, 1))
        return mine, gather_places(mine)

    def shard_features(pieces):
        whole = jnp.stack(
            [
                piece.reshape(INNER, rows, pair)[jnp.array([n ^ place for n in range(INNER)])]
                for place, piece in enumerate(pieces)
            ]
        ).reshape(INNER, span, pair)
        whole = jnp.transpose(whole, (1, 0, 2)).reshape(span, width)
        cut = []
        for n in range(shares):
            first = (n * INNER + here) * share
            mixed = (first // pair) ^ here
            place = ((mixed >> 1) & 3) | ((mixed & 1) << 2)
            cut.append(
                lax.dynamic_slice_in_dim(whole, place * pair + first % pair, share, axis=1)
            )
        return jnp.concatenate(cut, axis=1)

    def row_grads(parts, pieces, branch):
        if not matched:
            grad = under(shard_features(pieces), jnp.concatenate(branch, axis=0))
            return [grad.astype(LOW).reshape(shares, share, width)]
        return [parts[0], hop(parts[1], 1)]

    def pack_grads(columns, *rows):
        if matched:
            return pack(core_table, columns, *[part for parts in rows for part in parts])
        lined = [
            jnp.transpose(parts[0].reshape(shares, share, INNER, LANES), (0, 2, 1, 3))
            for parts in rows
        ]
        return jnp.concatenate([columns] + [r.reshape(width, LANES) for r in lined], axis=1)

    def lanes_to_columns(got):
        kinds = got.shape[2] // pair
        got = got.reshape(INNER, share, kinds, pair).astype(WIDE)
        return jnp.transpose(got, (1, 2, 0, 3)).reshape(share, kinds * width)

    def lanes_to_rows(packed, start):
        rows = packed[:, start : start + LANES].reshape(INNER, share, LANES).astype(WIDE)
        return jnp.transpose(rows, (1, 0, 2)).reshape(share, width)

    small = jnp.concatenate([jnp.transpose(vectors), hidden_bias.reshape(share, -1)], axis=1)
    extras = small.shape[1]
    small = jnp.pad(small, ((0, 0), (0, LANES - extras)))
    small = jnp.broadcast_to(small[None], (INNER, share, LANES))
    first_cut = jnp.transpose(mlp_in.reshape(share, shares, INNER, hidden), (2, 0, 1, 3))
    first_cut = first_cut.reshape(INNER, share, shares * hidden)
    def over(value):
        return lax.all_gather(value, OUTER, axis=0)

    def row_lanes(weight):
        return jnp.transpose(weight.reshape(-1, INNER, LANES), (1, 0, 2))

    mine = exchange(jnp.concatenate([cut_columns(self_in), small], axis=2))
    self_far = over(jnp.concatenate([mine, row_lanes(self_out)], axis=2)).reshape(width, -1)
    pieces = gather_places(after(target[0], mine))
    other = [cut_columns(cross_kv, cross_query), first_cut]
    other = exchange(after(jnp.concatenate(other, axis=2), *pieces[1:4]))
    states = gather_places(after(source[0], other))
    cross_far = jnp.concatenate([other[:, :, : 3 * pair], row_lanes(cross_out)], axis=2)
    cross_far = over(after(cross_far, self_far)).reshape(width, -1)
    first_mine = other[:, :, 3 * pair :].reshape(INNER * share, -1)
    feed_mine = jnp.concatenate([first_mine, mlp_out], axis=0)
    feed_packed = over(after(feed_mine, self_far))

    q, k, v, h1, params, biases, self_packed, x_all = enter(head_table, rows, pieces, self_far)
    sout_mine, w_sout = head_rows(self_out, after(self_far, q, *states[1:4])[:, 4 * pair :])
    q = after(q, *w_sout[1:4])
    h_bias = self_packed.reshape(shares, INNER, share, -1)
    h_bias = h_bias[..., 3 * pair + count : 3 * pair + extras]
    h_bias = lax.dynamic_index_in_dim(h_bias, here, 1, False).reshape(1, -1).astype(WIDE)

    def stream_keys(own):
        return lax.all_gather(own, "outer", axis=0, tiled=True) if groups > 1 else own

    def own_keys(partial):
        if groups == 1:
            return partial
        return lax.psum_scatter(partial, "outer", scatter_dimension=0, tiled=True)

    k, v = stream_keys(k), stream_keys(v)
    att, self_total = attend(self_table, q, k, v, rows, True)
    att = gather_places(att)
    states, ck, cv, cross_packed = pair_heads(rows, states, cross_far, biases)
    ck, cv = stream_keys(ck), stream_keys(cv)
    y1, h2, y1_all, cq = join_self(att, w_sout, x_all, params, cross_packed, biases)
    cout_mine, w_cout = head_rows(cross_out, after(cross_far, *att[1:4])[:, 3 * pair :])
    pull_up = gather_places(after(cotangent[0], *w_cout[1:4]))
    cq = after(cq, *w_cout[1:4])
    catt, cross_total = attend(cross_table, cq, ck, cv, rows, False)
    catt = gather_places(after(catt, *pull_up[1:4]))
    y2, h3 = join_cross(catt, w_cout, y1_all, y1, params)
    active, before_grad, give, keep, h_bias_grad, up = feed(h3, h_bias, feed_packed, pull_up)
    third_own, third_parts = scatter_places(give, keep)
    mlp_grad = feed_grad(active, before_grad, after(h3, third_own), up)
    third_parts, mlp_grad = lax.optimization_barrier((third_parts, mlp_grad))
    mlp_home = lax.psum_scatter(mlp_grad, OUTER, scatter_dimension=0, tiled=True)
    late_grad, cross_branch, late_sums = norm_back(
        4, third_own, third_parts, y2, cotangent[0], params
    )
    cross_all = gather_places(cross_branch)
    give, keep, dcq, dck, dcv, cross_sums, *cross_rows = attend_back(
        cross_table,
        cq,
        ck,
        cv,
        cross_total,
        cout_mine,
        catt[0],
        cross_all,
        rows,
        False,
        (2, cross_packed),
    )
    dck, dcv = own_keys(dck), own_keys(dcv)
    second_own, second_parts = scatter_places(give, keep)
    cross_grad = column_part((after(states, second_own), (dck, dcv)), (h2, (dcq,)))
    side_give, side_keep = side_out(
        after(active, second_own), feed_packed, dck, dcv, cross_packed
    )
    second_parts, cross_grad, side_give, side_keep = lax.optimization_barrier(
        (second_parts, cross_grad, side_give, side_keep)
    )
    cross_rows = row_grads(cross_rows, catt, cross_all)
    middle_grad, self_branch, middle_sums = norm_back(
        2, second_own, second_parts, y1, late_grad, params
    )
    packed_grad = pack_grads(cross_grad, cross_rows)
    side_own, *side_parts = scatter_start(after(side_give, self_branch), side_keep)
    self_all, packed_grad, side_own, side_parts = gather_places(
        self_branch, packed_grad, side_own, side_parts
    )
    self_all, mlp_home, packed_grad, side_parts = lax.optimization_barrier(
        (self_all, mlp_home, packed_grad, side_parts)
    )
    side_parts = scatter_finish(side_parts)
    cross_sum = lax.psum_scatter(packed_grad, OUTER, scatter_dimension=0, tiled=True)
    made = attend_back(
        self_table,
        q,
        k,
        v,
        self_total,
        sout_mine,
        att[0],
        self_all,
        rows,
        True,
        (0, self_packed, x_all) if groups == 1 else None,
    )
    dq, dk, dv, self_sums, *self_rows = made[-6:]
    dk, dv = own_keys(dk), own_keys(dv)
    if groups == 1:
        give, keep, target_sums = made[:3]
    else:
        give, keep, target_sums = spread_self(dq, dk, dv, self_packed, x_all)
    head_sums = jnp.concatenate([self_sums, cross_sums])[:, None]
    head_sums = lax.dynamic_update_slice_in_dim(
        jnp.zeros((4, INNER, pair), WIDE), head_sums, here, 1
    )
    vector_grad = jnp.concatenate(
        [
            target_sums[:2],
            middle_sums[:2],
            late_sums[:2],
            by_column(head_sums)[:2],
            middle_sums[2:3],
            by_column(head_sums)[2:],
            late_sums[2:],
        ]
    )
    vector_part = jnp.transpose(vector_grad.reshape(count, devices, share), (1, 0, 2))
    bias_part = lax.dynamic_update_slice_in_dim(
        jnp.zeros((shares, INNER, hidden), WIDE), h_bias_grad.reshape(shares, 1, hidden), here, 1
    ).reshape(devices, hidden)
    tiny = jnp.concatenate([vector_part.reshape(devices, -1), bias_part], axis=1)
    tiny = lax.all_to_all(tiny, ALL, 0, 0, tiled=True)
    give, side_parts, tiny = lax.optimization_barrier((give, side_parts, tiny))
    tiny = jnp.sum(after(tiny, give), axis=0)
    first_own, *first_parts = scatter_start(give, keep)
    first_parts = scatter_finish(first_parts)
    self_grad = column_part((after(h1, first_own), (dq, dk, dv)))
    self_rows = row_grads((self_rows[0], after(self_rows[1], first_own)), att, self_all)
    packed_grad = pack_grads(self_grad, self_rows)
    self_sum = lax.psum_scatter(packed_grad, OUTER, scatter_dimension=0, tiled=True)
    target_grad, target_low, _ = norm_back(
        0, first_own, first_parts, target[0], middle_grad, params
    )
    side_own, mlp_home, cross_sum = lax.optimization_barrier(
        (side_own, mlp_home, cross_sum, first_parts)
    )[:3]
    layer_out, source_grad = side_sum(side_own, side_parts, y2, params)
    cross_lanes = cross_sum[:, : 3 * pair].reshape(INNER, share, -1)
    first_lanes = mlp_home[:, width:].reshape(INNER, share, -1)
    cross_got = exchange(jnp.concatenate([cross_lanes, first_lanes], axis=2))
    self_got = exchange(self_sum[:, : 3 * pair].reshape(INNER, share, -1))
    if matched:
        cross_home, cout_home, first_home, second_home = home_feed(
            3, hidden, cross_got, cross_sum, mlp_home
        )
        self_home, sout_home = home(self_got, self_sum)
    else:
        cross_home = lanes_to_columns(cross_got[:, :, : 3 * pair])
        first_home = cross_got[:, :, 3 * pair :].reshape(INNER, share, shares, hidden)
        first_home = jnp.transpose(first_home, (1, 2, 0, 3)).reshape(share, -1).astype(WIDE)
        second_home = mlp_home[:, :width].astype(WIDE)
        cout_home = lanes_to_rows(cross_sum, 3 * pair)
        sout_home = lanes_to_rows(self_sum, 3 * pair)
        self_home = lanes_to_columns(self_got)

    return (
        layer_out[None],
        target_low[None],
        source_grad[None],
        self_home,
        sout_home,
        cross_home[:, 2 * width :],
        cross_home[:, : 2 * width],
        cout_home,
        first_home,
        second_home,
        tiny[: count * share].reshape(count, share),
        tiny[count * share :],
    )


def solution(mesh):
    streams, blocks = mesh.devices.shape
    grid = mesh.devices.reshape(streams, blocks // INNER, INNER)
    inner_mesh = Mesh(grid, ALL)
    rows = P("ulys", ("outer", "inner"), None)
    matrix = P(ALL, None)
    row_vectors = P(None, ALL)
    in_specs = (rows,) * 3 + (P(), P()) + (matrix,) * 7 + (row_vectors, P(ALL))
    out_specs = (rows,) * 3 + (matrix,) * 7 + (row_vectors, P(ALL))
    return jax.shard_map(
        per_device, mesh=inner_mesh, in_specs=in_specs, out_specs=out_specs, check_vma=False
    )
```

```python
import functools

import jax
import jax.numpy as jnp
from jax import lax
from jax.experimental import pallas as pl
from jax.experimental.pallas import tpu as pltpu
from jax.sharding import Mesh
from jax.sharding import PartitionSpec as P

HEADS = 16
LOW = jnp.bfloat16
WIDE = jnp.float32
INNER = 8
STEP = 256
WIDE_STEP = 512
LANES = 128
OUTER = ("ulys", "outer")
ALL = ("ulys", "outer", "inner")


def offset_of(place):
    return ((place & 3) << 1) | (place >> 2)


def dot_t(a, b):
    return lax.dot_general(a, b, (((1,), (1,)), ((), ())), preferred_element_type=WIDE)


def dot_n(a, b):
    return lax.dot_general(a, b, (((1,), (0,)), ((), ())), preferred_element_type=WIDE)


def dot_c(a, b):
    return lax.dot_general(a, b, (((0,), (0,)), ((), ())), preferred_element_type=WIDE)


def seg_of(position, table, first):
    count = jnp.zeros_like(position)
    for n in range(3):
        count = count + (table[first + n] <= position).astype(jnp.int32)
    return count


def iota(shape, axis):
    return lax.broadcasted_iota(jnp.int32, shape, axis)


def to_order(table, source, target, rows, factor=None):
    span = rows * INNER
    for chunk in range(source.shape[0] // span):
        for place in range(INNER):
            at = pl.multiple_of((table[0] ^ offset_of(place)) * rows, rows) + chunk * span
            value = source[pl.ds(chunk * span + place * rows, rows), :]
            if factor is not None:
                value = value * factor
            target[pl.ds(at, rows), :] = value


def from_order(table, source, target, rows):
    span = rows * INNER
    for chunk in range(target.shape[0] // span):
        for place in range(INNER):
            at = pl.multiple_of((table[0] ^ offset_of(place)) * rows, rows) + chunk * span
            target[pl.ds(chunk * span + place * rows, rows), :] = source[pl.ds(at, rows), :].astype(
                target.dtype
            )


def half_lanes(value, head, size):
    lane = iota(value.shape, 1)
    keep = (lane >= head * size) & (lane < (head + 1) * size)
    return jnp.where(keep, value, jnp.zeros_like(value))


def attend_kernel(causal, rows, size, table, q, k, v, out, log_total, qs, ks, vs, ordered):
    span, keys = q.shape[0], k.shape[0]
    chunks = keys // span
    to_order(table, q, qs, rows, jnp.asarray(size**-0.5, LOW))
    to_order(table, k, ks, rows)
    to_order(table, v, vs, rows)
    for step in range(span // WIDE_STEP):
        lo = step * WIDE_STEP
        queries = qs[lo : lo + WIDE_STEP, :]
        q_at = table[1] + lo + iota((WIDE_STEP, 1), 0)
        q_seg = seg_of(q_at, table, 2)
        count = lo + WIDE_STEP if causal and chunks == 1 else span

        def mask(start):
            k_at = start + iota((1, count), 1)
            allowed = q_seg == seg_of(k_at, table, 5)
            if causal:
                allowed = allowed & (k_at <= q_at)
            return allowed

        def scores(head, start, allowed):
            raw = dot_t(queries, half_lanes(ks[pl.ds(start, count), :], head, size))
            return jnp.where(allowed, raw, -1e30)

        parts = []
        allowed = mask(0) if chunks == 1 else None
        for head in range(2):
            if chunks == 1:
                raw = scores(head, 0, allowed)
                top = jnp.max(raw, axis=1, keepdims=True)
                weight = jnp.exp(raw - top)
                total = jnp.sum(weight, axis=1, keepdims=True)
                running = dot_n(weight.astype(LOW), vs[:count, :])
            else:

                def absorb(chunk, carry, head=head):
                    top, total, running = carry
                    start = pl.multiple_of(chunk * span, span)
                    raw = scores(head, start, mask(start))
                    new_top = jnp.maximum(top, jnp.max(raw, axis=1, keepdims=True))
                    weight = jnp.exp(raw - new_top)
                    fade = jnp.exp(top - new_top)
                    total = total * fade + jnp.sum(weight, axis=1, keepdims=True)
                    running = running * fade + dot_n(weight.astype(LOW), vs[pl.ds(start, span), :])
                    return new_top, total, running

                top, total, running = lax.fori_loop(
                    0,
                    chunks,
                    absorb,
                    (
                        jnp.full((WIDE_STEP, 1), -1e30, WIDE),
                        jnp.zeros((WIDE_STEP, 1), WIDE),
                        jnp.zeros((WIDE_STEP, 2 * size), WIDE),
                    ),
                )
            parts.append(running / total)
            logs = jnp.broadcast_to(top + jnp.log(total), (WIDE_STEP, 2 * size))
            log_total[head : head + 1, lo : lo + WIDE_STEP] = jnp.transpose(logs)[0:1, :]
        lane = iota((WIDE_STEP, 2 * size), 1)
        ordered[lo : lo + WIDE_STEP, :] = jnp.where(lane < size, parts[0], parts[1])
    from_order(table, ordered, out, rows)


def split_rows(table, first, own, branch, row, keep, give):
    row[...] = dot_c(own[...], branch[...]).astype(LOW)
    share = keep.shape[1]
    for core, out in ((table[first], keep), (table[first + 1], give)):
        for n in range(2):
            at = pl.multiple_of((2 * n + core) * share, share)
            out[n] = row[pl.ds(at, share), :]


def attend_back_kernel(causal, rows, size, start, lined, table, q, k, v, log_total, weight, *refs):
    own = refs[0] if lined else None
    refs = refs[1:] if lined else refs
    pieces, refs = refs[:INNER], refs[INNER:]
    late = []
    if start is not None:
        late, refs = [refs[0]], refs[1:]
        if start == 0:
            late, refs = late + [refs[0]], refs[1:]
            give, keep, norm_sums, refs = *refs[:3], refs[3:]
        else:
            give, keep, refs = *refs[:2], refs[2:]
    dq, dk, dv, sums, refs = *refs[:4], refs[4:]
    if lined:
        row_keep, row_give, refs = *refs[:2], refs[2:]
    qs, ks, vs, ups, dqs, dks, dvs, branch, row, marks, *near = refs
    copies = pull(pieces, 0, branch, marks)
    loads = []
    for n, source in enumerate(late):
        loads.append(pltpu.make_async_copy(source, near[n], near[-1].at[n]))
    for load in loads:
        load.start()
    span, keys = q.shape[0], k.shape[0]
    chunks = keys // span
    scale = size**-0.5
    to_order(table, q, qs, rows, jnp.asarray(scale, LOW))
    to_order(table, k, ks, rows)
    to_order(table, v, vs, rows)
    finish(copies)
    upstream = dot_t(branch[...], weight[...]).astype(LOW)
    for place in range(INNER):
        at = pl.multiple_of((table[0] ^ offset_of(place)) * rows, rows)
        ups[pl.ds(at, rows), :] = upstream[place * rows : (place + 1) * rows, :]
    if lined:
        split_rows(table, 8, own, branch, row, row_keep, row_give)
    dks[...] = jnp.zeros_like(dks)
    dvs[...] = jnp.zeros_like(dvs)
    for step in range(span // STEP):
        lo = step * STEP
        queries = qs[lo : lo + STEP, :]
        upstream = ups[lo : lo + STEP, :]
        q_at = table[1] + lo + iota((1, STEP), 1)
        q_seg = seg_of(q_at, table, 2)
        count = lo + STEP if causal and chunks == 1 else span
        q_pair = [half_lanes(queries, head, size) for head in range(2)]
        up_pair = [half_lanes(upstream, head, size) for head in range(2)]
        logs = [log_total[head : head + 1, lo : lo + STEP] for head in range(2)]

        def make(start):
            k_at = start + iota((count, 1), 0)
            allowed = q_seg == seg_of(k_at, table, 5)
            if causal:
                allowed = allowed & (k_at <= q_at)
            keys_here = ks[pl.ds(start, count), :]
            k_pair = [half_lanes(keys_here, head, size) for head in range(2)]
            probs, lean = [], []
            for head in range(2):
                raw = dot_t(k_pair[head], queries)
                probs.append(jnp.exp(jnp.where(allowed, raw - logs[head], -1e30)))
                slope = dot_t(vs[pl.ds(start, count), :], up_pair[head])
                lean.append(probs[head] * slope)
            return k_pair, probs, lean

        def settle(start, delta, made):
            k_pair, probs, lean = made
            push = [(lean[n] - probs[n] * delta[n]).astype(LOW) for n in range(2)]
            low = [probs[n].astype(LOW) for n in range(2)]
            at = pl.ds(start, count)
            dvs[at, :] += dot_n(jnp.concatenate(low, axis=1), jnp.concatenate(up_pair, axis=0))
            dks[at, :] += dot_n(jnp.concatenate(push, axis=1), jnp.concatenate(q_pair, axis=0))
            return dot_c(jnp.concatenate(push, axis=0), jnp.concatenate(k_pair, axis=0))

        def slopes(made):
            return [jnp.sum(made[2][n], axis=0, keepdims=True) for n in range(2)]

        if chunks == 1:
            made = make(0)
            total_dq = settle(0, slopes(made), made)
        else:

            def measure(chunk, delta):
                more = slopes(make(pl.multiple_of(chunk * span, span)))
                return [delta[n] + more[n] for n in range(2)]

            delta = lax.fori_loop(0, chunks, measure, [jnp.zeros((1, STEP), WIDE)] * 2)

            def absorb(chunk, running, delta=delta):
                start = pl.multiple_of(chunk * span, span)
                return running + settle(start, delta, make(start))

            total_dq = lax.fori_loop(0, chunks, absorb, jnp.zeros((STEP, 2 * size), WIDE))
        dqs[lo : lo + STEP, :] = total_dq * scale
    from_order(table, dqs, dq, rows)
    from_order(table, dks, dk, rows)
    from_order(table, dvs, dv, rows)
    finish(loads)
    if start is not None:
        packed = near[0]
        x_all = near[1] if start == 0 else None
        kinds = 3 if start == 0 else 1
        back = packed[:, start * LANES : (start + kinds) * LANES]
        first = second = None
        for at, out in ((span // 2, give), (0, keep)):
            at = slice(at, at + span // 2)
            left = [part[at, :] for part in (dq, dk, dv)[:kinds]]
            left = left[0] if kinds == 1 else jnp.concatenate(left, axis=1)
            slope = dot_t(left, back)
            out[...] = slope.astype(out.dtype)
            if start == 0:
                centred, inverse = centre(x_all[at, :].astype(WIDE))
                gain = jnp.sum(slope * (centred * inverse), axis=0, keepdims=True)
                shift = jnp.sum(slope, axis=0, keepdims=True)
                first = gain if first is None else first + gain
                second = shift if second is None else second + shift
        if start == 0:
            norm_sums[0:1, :] = first
            norm_sums[1:2, :] = second
    sums[0:1, :] = jnp.sum(dqs[...].astype(LOW).astype(WIDE), axis=0, keepdims=True)
    sums[1:2, :] = jnp.sum(dvs[...].astype(LOW).astype(WIDE), axis=0, keepdims=True)


HBM = pl.BlockSpec(memory_space=pl.ANY)


def room(megabytes):
    return pltpu.CompilerParams(vmem_limit_bytes=megabytes * 2**20)


def pull(pieces, index, target, marks):
    rows = target.shape[0] // INNER
    copies = []
    for place in range(INNER):
        source = pieces[place].at[pl.ds(index * rows, rows), :]
        aim = target.at[pl.ds(place * rows, rows), :]
        copies.append(pltpu.make_async_copy(source, aim, marks.at[place]))
    for copy in copies:
        copy.start()
    return copies


def finish(copies):
    for copy in copies:
        copy.wait()


def cost(micros):
    return pl.CostEstimate(
        flops=int(micros * 1.1e9), bytes_accessed=int(micros * 3.5e6), transcendentals=0
    )


SMEM = pl.BlockSpec(memory_space=pltpu.SMEM)
VMEM = pl.BlockSpec(memory_space=pltpu.VMEM)


def attend(table, q, k, v, rows, causal):
    span, pair = q.shape
    keys = k.shape[0]
    return pl.pallas_call(
        functools.partial(attend_kernel, causal, rows, pair // 2),
        out_shape=(
            jax.ShapeDtypeStruct((span, pair), LOW),
            jax.ShapeDtypeStruct((2, span), WIDE),
        ),
        in_specs=[SMEM, VMEM, VMEM, VMEM],
        out_specs=(VMEM, VMEM),
        scratch_shapes=[
            pltpu.VMEM((span, pair), LOW),
            pltpu.VMEM((keys, pair), LOW),
            pltpu.VMEM((keys, pair), LOW),
            pltpu.VMEM((span, pair), WIDE),
        ],
        compiler_params=room(60),
        cost_estimate=cost(6),
    )(table, q, k, v)


def attend_back(table, q, k, v, log_total, weight, own, pieces, rows, causal, back=None):
    span, pair = q.shape
    keys = k.shape[0]
    width = weight.shape[1]
    part = jax.ShapeDtypeStruct((2, pair // 4, width), LOW)
    lined = [] if own is None else [own]
    spread_shape = (
        jax.ShapeDtypeStruct((span // 2, width), LOW),
        jax.ShapeDtypeStruct((span // 2, width), WIDE),
    )
    start, *extra = back if back else (None,)
    if start == 0:
        spread_shape += (jax.ShapeDtypeStruct((2, width), WIDE),)
    return pl.pallas_call(
        functools.partial(attend_back_kernel, causal, rows, pair // 2, start, bool(lined)),
        out_shape=(spread_shape if back else ())
        + (
            jax.ShapeDtypeStruct((span, pair), LOW),
            jax.ShapeDtypeStruct((keys, pair), LOW),
            jax.ShapeDtypeStruct((keys, pair), LOW),
            jax.ShapeDtypeStruct((2, pair), WIDE),
        )
        + ((part, part) if lined else ()),
        in_specs=[SMEM] + [VMEM] * (5 + len(lined)) + [HBM] * (INNER + len(extra)),
        out_specs=(VMEM,) * (4 + 2 * len(lined) + (len(spread_shape) if back else 0)),
        scratch_shapes=[
            pltpu.VMEM((span, pair), LOW),
            pltpu.VMEM((keys, pair), LOW),
            pltpu.VMEM((keys, pair), LOW),
            pltpu.VMEM((span, pair), LOW),
            pltpu.VMEM((span, pair), WIDE),
            pltpu.VMEM((keys, pair), WIDE),
            pltpu.VMEM((keys, pair), WIDE),
            pltpu.VMEM((span, width), LOW),
            pltpu.VMEM((pair, width), LOW),
            pltpu.SemaphoreType.DMA((INNER,)),
        ]
        + [pltpu.VMEM(value.shape, LOW) for value in extra]
        + ([pltpu.SemaphoreType.DMA((2,))] if extra else []),
        compiler_params=room(60),
        cost_estimate=cost(10),
    )(table, q, k, v, log_total, weight, *lined, *pieces, *extra)


def centre(value):
    center = jnp.mean(value, axis=-1, keepdims=True)
    centred = value - center
    spread = jnp.mean(centred * centred, axis=-1, keepdims=True)
    return centred, lax.rsqrt(spread + 1e-05)


def norm_of(value, gain, shift):
    centred, inverse = centre(value)
    return (centred * inverse * gain + shift).astype(LOW)


def enter_kernel(kinds, table, far, *refs):
    pieces, refs = refs[:INNER], refs[INNER:]
    q, k, v, h, params, biases, packed, x_all, blocks, marks, mark = refs
    loads = []
    for place in range(far.shape[0]):
        loads.append(pltpu.make_async_copy(far.at[place], blocks.at[:, place], mark.at[place]))
    for load in loads:
        load.start()
    copies = pull(pieces, 0, x_all, marks)
    finish(loads)
    packed[...] = blocks[...].reshape(packed.shape)
    edge = kinds * LANES
    extra = packed[:, edge : edge + LANES].astype(WIDE)
    params[...] = jnp.transpose(extra)[:16, :]
    size = LANES // 2
    mine = [packed[pl.ds(pl.multiple_of(table[n], 16), size), edge : edge + LANES] for n in (0, 1)]
    biases[...] = jnp.transpose(jnp.concatenate(mine, axis=0).astype(WIDE))[:16, :]
    finish(copies)
    half = x_all.shape[0] // 2
    for part in range(2):
        at = slice(part * half, (part + 1) * half)
        low = norm_of(x_all[at, :].astype(WIDE), params[0:1, :], params[1:2, :])
        h[at, :] = low
        made = dot_n(low, packed[:, :edge])
        q[at, :] = (made[:, :LANES] + biases[6:7, :]).astype(LOW)
        k[at, :] = made[:, LANES : 2 * LANES].astype(LOW)
        v[at, :] = (made[:, 2 * LANES :] + biases[7:8, :]).astype(LOW)


def enter(table, rows, pieces, packed):
    width = pieces[0].shape[1]
    span = rows * INNER
    heads = jax.ShapeDtypeStruct((span, LANES), LOW)
    return pl.pallas_call(
        functools.partial(enter_kernel, 3),
        out_shape=(
            heads,
            heads,
            heads,
            jax.ShapeDtypeStruct((span, width), LOW),
            jax.ShapeDtypeStruct((16, width), WIDE),
            jax.ShapeDtypeStruct((16, LANES), WIDE),
            jax.ShapeDtypeStruct((width, 4 * LANES), LOW),
            jax.ShapeDtypeStruct((span, width), LOW),
        ),
        in_specs=[SMEM] + [HBM] * (1 + INNER),
        out_specs=(VMEM,) * 8,
        scratch_shapes=[
            pltpu.VMEM((packed.shape[1], packed.shape[0]) + packed.shape[2:], LOW),
            pltpu.SemaphoreType.DMA((INNER,)),
            pltpu.SemaphoreType.DMA((packed.shape[0],)),
        ],
        compiler_params=room(60),
        cost_estimate=cost(4),
    )(table, packed, *pieces)


def join_kernel(vector, first, query, *refs):
    pieces, weights, refs = refs[:INNER], refs[INNER : 2 * INNER], refs[2 * INNER :]
    if query is None:
        far, base_own, params, y_own, h, weight, left, heads, marks, base, base_mark = refs
    else:
        far, params, packed, biases, y_own, h, y_all, cq, weight, left, heads, marks, base, base_mark = refs
    span = left.shape[0]
    block = span // INNER
    loads = pull(weights, 0, weight, marks.at[1])
    base_load = pltpu.make_async_copy(far, base, base_mark)
    copies = []
    for place in range(INNER):
        copies.append(pltpu.make_async_copy(pieces[place], heads.at[place], marks.at[0, place]))
    for copy in copies:
        copy.start()
    base_load.start()
    finish(copies + loads + [base_load])
    parts = INNER // 2
    for part in range(parts):
        at = slice(part * 2 * block, (part + 1) * 2 * block)
        for n in range(2 * part, 2 * part + 2):
            for place in range(INNER):
                first_row = (n ^ place) * block
                left[n * block : (n + 1) * block, place * LANES : (place + 1) * LANES] = heads[
                    place, first_row : first_row + block, :
                ]
        value = base[at, :].astype(WIDE)
        if query is None and part == 0:
            value = jnp.concatenate([base_own[...], value[block:, :]], axis=0)
        y = value + dot_n(left[at, :], weight[...]) + params[vector : vector + 1, :]
        if part == 0:
            y_own[...] = y[:block, :]
        low = norm_of(y, params[first : first + 1, :], params[first + 1 : first + 2, :])
        h[at, :] = low
        if query is not None:
            y_all[at, :] = y.astype(LOW)
            made = dot_n(low, packed[:, query * LANES : (query + 1) * LANES])
            cq[at, :] = (made + biases[9:10, :]).astype(LOW)


def join_self(pieces, weights, base, params, packed, biases):
    span, width = base.shape
    return pl.pallas_call(
        functools.partial(join_kernel, 8, 2, 2),
        out_shape=(
            jax.ShapeDtypeStruct((span // INNER, width), WIDE),
            jax.ShapeDtypeStruct((span, width), LOW),
            jax.ShapeDtypeStruct((span, width), LOW),
            jax.ShapeDtypeStruct((span, LANES), LOW),
        ),
        in_specs=[HBM] * (2 * INNER + 1) + [VMEM] * 3,
        out_specs=(VMEM,) * 4,
        scratch_shapes=[
            pltpu.VMEM((width, width), LOW),
            pltpu.VMEM((span, width), LOW),
            pltpu.VMEM((INNER, span, LANES), LOW),
            pltpu.SemaphoreType.DMA((2, INNER)),
            pltpu.VMEM((span, width), LOW),
            pltpu.SemaphoreType.DMA,
        ],
        compiler_params=room(60),
        cost_estimate=cost(6),
    )(*pieces, *weights, base, params, packed, biases)


def join_cross(pieces, weights, base, base_own, params):
    span, width = base.shape
    return pl.pallas_call(
        functools.partial(join_kernel, 11, 4, None),
        out_shape=(
            jax.ShapeDtypeStruct((span // INNER, width), WIDE),
            jax.ShapeDtypeStruct((span, width), LOW),
        ),
        in_specs=[HBM] * (2 * INNER + 1) + [VMEM] * 2,
        out_specs=(VMEM,) * 2,
        scratch_shapes=[
            pltpu.VMEM((width, width), LOW),
            pltpu.VMEM((span, width), LOW),
            pltpu.VMEM((INNER, span, LANES), LOW),
            pltpu.SemaphoreType.DMA((2, INNER)),
            pltpu.VMEM((span, width), LOW),
            pltpu.SemaphoreType.DMA,
        ],
        compiler_params=room(60),
        cost_estimate=cost(5),
    )(*pieces, *weights, base, base_own, params)


def load_rows(packed, start, target, marks):
    shares = packed.shape[0]
    rows = target.shape[0] // shares
    copies = []
    for n in range(shares):
        source = packed.at[n, pl.ds(start, rows), :]
        aim = target.at[pl.ds(n * rows, rows), :]
        copies.append(pltpu.make_async_copy(source, aim, marks.at[n]))
    for copy in copies:
        copy.start()
    return copies


def feed_kernel(h, bias, packed, *refs):
    pieces = refs[:INNER]
    act, slope, give, keep, bias_grad, up, first, second, marks, weight_marks = refs[INNER:]
    span, width = up.shape
    hidden = second.shape[0]
    loads = load_rows(packed, 0, first, weight_marks.at[0])
    copies = load_rows(packed, width // packed.shape[0], second, weight_marks.at[1])
    copies += pull(pieces, 0, up, marks)
    finish(loads)
    step = 256
    inner = (2.0 / 3.141592653589793) ** 0.5
    for n in range(hidden // step):
        at = slice(n * step, (n + 1) * step)
        pre = dot_n(h[...], first[:, at]) + bias[:, at]
        square = pre * pre
        bend = jnp.tanh(pre * (inner + (inner * 0.044715) * square))
        half = 0.5 * bend + 0.5
        act[:, at] = (pre * half).astype(LOW)
        if n == 0:
            finish(copies)
        rise = half + 0.5 * pre * (1.0 - bend * bend) * (inner + (3 * inner * 0.044715) * square)
        low = (dot_t(up[...], second[at, :]) * rise).astype(LOW)
        slope[:, at] = low
        bias_grad[:, at] = jnp.sum(low.astype(WIDE), axis=0, keepdims=True)
    give[...] = dot_t(slope[span // 2 :, :], first[...]).astype(LOW)
    keep[...] = dot_t(slope[: span // 2, :], first[...])


def feed(h, bias, packed, pieces):
    span, width = h.shape
    hidden = bias.shape[1]
    shares = packed.shape[0]
    return pl.pallas_call(
        feed_kernel,
        out_shape=(
            jax.ShapeDtypeStruct((span, hidden), LOW),
            jax.ShapeDtypeStruct((span, hidden), LOW),
            jax.ShapeDtypeStruct((span // 2, width), LOW),
            jax.ShapeDtypeStruct((span // 2, width), WIDE),
            jax.ShapeDtypeStruct((1, hidden), WIDE),
            jax.ShapeDtypeStruct((span, width), LOW),
        ),
        in_specs=[VMEM] * 2 + [HBM] * (1 + INNER),
        out_specs=(VMEM,) * 6,
        scratch_shapes=[
            pltpu.VMEM((width, hidden), LOW),
            pltpu.VMEM((hidden, width), LOW),
            pltpu.SemaphoreType.DMA((INNER,)),
            pltpu.SemaphoreType.DMA((2, shares)),
        ],
        compiler_params=room(44),
        cost_estimate=cost(13),
    )(h, bias, packed, *pieces)


def side_kernel(act, packed, dk, dv, pair_weight, give, keep, second, marks):
    copies = load_rows(packed, second.shape[1] // packed.shape[0], second, marks)
    half, width = keep.shape[0], second.shape[1]
    weight = pair_weight[:, : 2 * LANES]
    spans = ((half, give), (0, keep))
    for at, out in spans:
        left = jnp.concatenate([dk[at : at + half, :], dv[at : at + half, :]], axis=1)
        out[:, width:] = dot_t(left, weight).astype(out.dtype)
    finish(copies)
    for at, out in spans:
        out[:, :width] = dot_n(act[at : at + half, :], second[...]).astype(out.dtype)


def side_out(act, packed, dk, dv, pair_weight):
    span, hidden = act.shape
    shares, _, width = packed.shape
    return pl.pallas_call(
        side_kernel,
        out_shape=(
            jax.ShapeDtypeStruct((span // 2, 2 * width), LOW),
            jax.ShapeDtypeStruct((span // 2, 2 * width), WIDE),
        ),
        in_specs=[VMEM, HBM] + [VMEM] * 3,
        out_specs=(VMEM,) * 2,
        scratch_shapes=[
            pltpu.VMEM((hidden, width), LOW),
            pltpu.SemaphoreType.DMA((shares,)),
        ],
        compiler_params=room(24),
        cost_estimate=cost(4),
    )(act, packed, dk, dv, pair_weight)


def side_sum_kernel(own, one, two, three, y, params, layer, source):
    total = own[...] + one[...].astype(WIDE) + two[...].astype(WIDE) + three[...].astype(WIDE)
    width = y.shape[1]
    layer[...] = (y[...] + total[:, :width] + params[12:13, :]).astype(LOW)
    source[...] = total[:, width:].astype(LOW)


def side_sum(own, parts, y, params):
    out = jax.ShapeDtypeStruct(y.shape, LOW)
    return pl.pallas_call(
        side_sum_kernel,
        out_shape=(out, out),
        in_specs=[VMEM] * 6,
        out_specs=(VMEM,) * 2,
        compiler_params=room(16),
        cost_estimate=cost(1),
    )(own, *parts, y, params)


def feed_grad_kernel(act, slope, h, up, out):
    width = up.shape[1]
    step = 256
    for n in range(width // step):
        at = slice(n * step, (n + 1) * step)
        out[at, width:] = dot_c(h[:, at], slope[...]).astype(LOW)
    for n in range(act.shape[1] // step):
        at = slice(n * step, (n + 1) * step)
        out[at, :width] = dot_c(act[:, at], up[...]).astype(LOW)


def feed_grad(act, slope, h, up):
    width = h.shape[1]
    hidden = act.shape[1]
    return pl.pallas_call(
        feed_grad_kernel,
        out_shape=jax.ShapeDtypeStruct((width, width + hidden), LOW),
        in_specs=[VMEM] * 4,
        out_specs=VMEM,
        compiler_params=room(40),
        cost_estimate=cost(6),
    )(act, slope, h, up)


def fold_kernel(keep, took, own, one, two, three):
    rows = own.shape[0]
    own[...] = keep[:rows, :] + took[:rows, :].astype(WIDE)
    for n, part in enumerate((one, two, three), 1):
        at = slice(n * rows, (n + 1) * rows)
        part[...] = (keep[at, :] + took[at, :].astype(WIDE)).astype(LOW)


def fold(keep, took):
    half, width = keep.shape
    part = jax.ShapeDtypeStruct((half // 4, width), LOW)
    return pl.pallas_call(
        fold_kernel,
        out_shape=(jax.ShapeDtypeStruct((half // 4, width), WIDE), part, part, part),
        in_specs=[VMEM] * 2,
        out_specs=(VMEM,) * 4,
        compiler_params=room(16),
        cost_estimate=cost(1),
    )(keep, took)


def norm_back_kernel(first, own, one, two, three, value, base, params, grad, low, sums):
    slope = own[...] + one[...].astype(WIDE) + two[...].astype(WIDE) + three[...].astype(WIDE)
    centred, inverse = centre(value[...].astype(WIDE))
    unit = centred * inverse
    lean = slope * params[first : first + 1, :]
    flat = jnp.mean(lean, axis=-1, keepdims=True)
    tilt = jnp.mean(lean * unit, axis=-1, keepdims=True)
    total = base[...].astype(WIDE) + inverse * (lean - flat - unit * tilt)
    grad[...] = total
    cut = total.astype(LOW)
    low[...] = cut
    sums[0:1, :] = jnp.sum(slope * unit, axis=0, keepdims=True)
    sums[1:2, :] = jnp.sum(slope, axis=0, keepdims=True)
    sums[2:3, :] = jnp.sum(cut.astype(WIDE), axis=0, keepdims=True)
    sums[3:4, :] = jnp.sum(base[...].astype(WIDE), axis=0, keepdims=True)


def norm_back(first, own, parts, value, base, params):
    rows, width = own.shape
    return pl.pallas_call(
        functools.partial(norm_back_kernel, first),
        out_shape=(
            jax.ShapeDtypeStruct((rows, width), WIDE),
            jax.ShapeDtypeStruct((rows, width), LOW),
            jax.ShapeDtypeStruct((4, width), WIDE),
        ),
        in_specs=[VMEM] * 7,
        out_specs=(VMEM,) * 3,
        compiler_params=room(16),
        cost_estimate=cost(2),
    )(own, *parts, value, base, params)


def pair_kernel(biases, far, *refs):
    pieces, (states, k, v, packed, marks, mark) = refs[:INNER], refs[INNER:]
    load = pltpu.make_async_copy(far.at[:, pl.ds(0, packed.shape[1])], packed, mark)
    load.start()
    finish(pull(pieces, 0, states, marks) + [load])
    made = dot_n(states[...], packed[:, : 2 * LANES])
    k[...] = made[:, :LANES].astype(LOW)
    v[...] = (made[:, LANES:] + biases[10:11, :]).astype(LOW)


def pair_heads(rows, pieces, packed, biases):
    width = pieces[0].shape[1]
    span = rows * INNER
    heads = jax.ShapeDtypeStruct((span, LANES), LOW)
    return pl.pallas_call(
        pair_kernel,
        out_shape=(
            jax.ShapeDtypeStruct((span, width), LOW),
            heads,
            heads,
            jax.ShapeDtypeStruct((width, 3 * LANES), LOW),
        ),
        in_specs=[VMEM] + [HBM] * (1 + INNER),
        out_specs=(VMEM,) * 4,
        scratch_shapes=[pltpu.SemaphoreType.DMA((INNER,)), pltpu.SemaphoreType.DMA],
        compiler_params=room(60),
        cost_estimate=cost(3),
    )(biases, packed, *pieces)


def spread_self_kernel(dq, dk, dv, packed, x_all, give, keep, sums):
    half = x_all.shape[0] // 2
    weight = packed[:, : 3 * LANES]
    first = second = None
    for part, out in ((1, give), (0, keep)):
        at = slice(part * half, (part + 1) * half)
        left = jnp.concatenate([dq[at, :], dk[at, :], dv[at, :]], axis=1)
        slope = dot_t(left, weight)
        out[...] = slope.astype(out.dtype)
        centred, inverse = centre(x_all[at, :].astype(WIDE))
        gain = jnp.sum(slope * (centred * inverse), axis=0, keepdims=True)
        shift = jnp.sum(slope, axis=0, keepdims=True)
        first = gain if first is None else first + gain
        second = shift if second is None else second + shift
    sums[0:1, :] = first
    sums[1:2, :] = second


def spread_self(dq, dk, dv, packed, x_all):
    span, width = x_all.shape
    return pl.pallas_call(
        spread_self_kernel,
        out_shape=(
            jax.ShapeDtypeStruct((span // 2, width), LOW),
            jax.ShapeDtypeStruct((span // 2, width), WIDE),
            jax.ShapeDtypeStruct((2, width), WIDE),
        ),
        in_specs=[VMEM] * 5,
        out_specs=(VMEM,) * 3,
        compiler_params=room(32),
        cost_estimate=cost(4),
    )(dq, dk, dv, packed, x_all)


def spread_columns(got, kinds, out):
    size = LANES // 2
    for kind in range(kinds):
        heads = {}
        for place in range(INNER):
            for n in (0, 1):
                at = kind * LANES + n * size
                number = (2 * (place & 1) + n) * (INNER // 2) + (place >> 1)
                heads[number] = got[place][:, at : at + size].astype(WIDE)
        for number in range(0, 2 * INNER, 2):
            at = kind * INNER * LANES + number * size
            both = jnp.concatenate([heads[number], heads[number + 1]], axis=1)
            out[:, at : at + LANES] = both


def spread_rows(packed, start, out):
    share = out.shape[0]
    for place in range(INNER):
        block = packed[place * share : (place + 1) * share, start : start + LANES]
        out[:, place * LANES : (place + 1) * LANES] = block.astype(WIDE)


def home_kernel(kinds, got, packed, columns, rows):
    spread_columns(got, kinds, columns)
    spread_rows(packed, kinds * LANES, rows)


def home(got, packed):
    share, lanes = got.shape[1:]
    return pl.pallas_call(
        functools.partial(home_kernel, lanes // LANES),
        out_shape=(
            jax.ShapeDtypeStruct((share, lanes * INNER), WIDE),
            jax.ShapeDtypeStruct((share, LANES * INNER), WIDE),
        ),
        in_specs=[VMEM] * 2,
        out_specs=(VMEM,) * 2,
        compiler_params=room(16),
        cost_estimate=cost(2),
    )(got, packed)


def home_feed_kernel(kinds, hidden, got, packed, feed_sum, *outs):
    columns, rows, first, second = outs
    spread_columns(got, kinds, columns)
    spread_rows(packed, kinds * LANES, rows)
    width = second.shape[1]
    second[...] = feed_sum[:, :width].astype(WIDE)
    lanes = got.shape[2] - kinds * LANES
    for n in range(lanes // hidden):
        for place in range(INNER):
            at = (n * INNER + place) * hidden
            start = kinds * LANES + n * hidden
            first[:, at : at + hidden] = got[place, :, start : start + hidden].astype(WIDE)


def home_feed(kinds, hidden, got, packed, feed_sum):
    share, lanes = got.shape[1:]
    rows = jax.ShapeDtypeStruct((share, LANES * INNER), WIDE)
    return pl.pallas_call(
        functools.partial(home_feed_kernel, kinds, hidden),
        out_shape=(
            jax.ShapeDtypeStruct((share, kinds * LANES * INNER), WIDE),
            rows,
            jax.ShapeDtypeStruct((share, (lanes - kinds * LANES) * INNER), WIDE),
            jax.ShapeDtypeStruct((feed_sum.shape[0], LANES * INNER), WIDE),
        ),
        in_specs=[VMEM] * 3,
        out_specs=(VMEM,) * 4,
        compiler_params=room(24),
        cost_estimate=cost(3),
    )(got, packed, feed_sum)


def column_part_kernel(kinds, *refs):
    count = len(kinds)
    lefts, rights, column = refs[:count], refs[count:-1], refs[-1]
    at = first = 0
    for left, kind in zip(lefts, kinds):
        right = [value[...] for value in rights[first : first + kind]]
        right = right[0] if kind == 1 else jnp.concatenate(right, axis=1)
        lanes = kind * LANES
        column[:, at : at + lanes] = dot_c(left[...], right).astype(LOW)
        at, first = at + lanes, first + kind


def column_part(*pairs):
    width = pairs[0][0].shape[1]
    kinds = tuple(len(rights) for _, rights in pairs)
    lefts = [left for left, _ in pairs]
    rights = [value for _, values in pairs for value in values]
    return pl.pallas_call(
        functools.partial(column_part_kernel, kinds),
        out_shape=jax.ShapeDtypeStruct((width, LANES * sum(kinds)), LOW),
        in_specs=[VMEM] * (len(lefts) + len(rights)),
        out_specs=VMEM,
        compiler_params=room(24),
        cost_estimate=cost(3),
    )(*lefts, *rights)


def head_lanes(source, start, device):
    size = LANES // 2
    at = [start + ((2 * (device & 1) + n) * (INNER // 2) + (device >> 1)) * size for n in (0, 1)]
    return jnp.concatenate([source[:, a : a + size] for a in at], axis=1)


def cut_self_kernel(raw, out):
    width = INNER * LANES
    for device in range(INNER):
        for kind in range(3):
            at = slice(kind * LANES, (kind + 1) * LANES)
            out[device, :, at] = head_lanes(raw, kind * width, device)
        out[device, :, 3 * LANES :] = raw[:, 4 * width :]


def cut_self(raw):
    rows = raw.shape[0]
    return pl.pallas_call(
        cut_self_kernel,
        out_shape=jax.ShapeDtypeStruct((INNER, rows, 4 * LANES), LOW),
        in_specs=[VMEM],
        out_specs=VMEM,
        compiler_params=room(16),
        cost_estimate=cost(2),
    )(raw)


def cut_other_kernel(hidden, pair_weight, query, first, out):
    width = INNER * LANES
    groups = first.shape[1] // (INNER * hidden)
    for device in range(INNER):
        for kind, source in enumerate((pair_weight, pair_weight, query)):
            at = slice(kind * LANES, (kind + 1) * LANES)
            out[device, :, at] = head_lanes(source, (kind % 2) * width, device)
        for n in range(groups):
            at = (n * INNER + device) * hidden
            start = 3 * LANES + n * hidden
            out[device, :, start : start + hidden] = first[:, at : at + hidden]


def cut_other(pair_weight, query, first, hidden):
    rows = query.shape[0]
    lanes = 3 * LANES + first.shape[1] // INNER
    return pl.pallas_call(
        functools.partial(cut_other_kernel, hidden),
        out_shape=jax.ShapeDtypeStruct((INNER, rows, lanes), LOW),
        in_specs=[VMEM] * 3,
        out_specs=VMEM,
        compiler_params=room(16),
        cost_estimate=cost(1),
    )(pair_weight, query, first)


def pick_rows_kernel(start, table, raw, own, give, marks):
    width = own.shape[2]
    copies = []
    for n, out in enumerate((own, give)):
        source = raw.at[pl.ds(table[n], 2), :, pl.ds(start, width)]
        copies.append(pltpu.make_async_copy(source, out, marks.at[n]))
    for copy in copies:
        copy.start()
    finish(copies)


def pick_rows(table, start, raw, width):
    part = jax.ShapeDtypeStruct((2, raw.shape[1], width), LOW)
    return pl.pallas_call(
        functools.partial(pick_rows_kernel, start),
        out_shape=(part, part),
        in_specs=[SMEM, HBM],
        out_specs=(VMEM,) * 2,
        scratch_shapes=[pltpu.SemaphoreType.DMA((2,))],
        compiler_params=room(16),
        cost_estimate=cost(1),
    )(table, raw)


def pick_kernel(table, packed, own, give):
    share = own.shape[1]
    for first, out in ((table[0], own), (table[1], give)):
        for n in range(2):
            for place in range(INNER):
                at = pl.multiple_of(((first + n) * INNER + place) * share, share)
                out[n, :, place * LANES : (place + 1) * LANES] = packed[pl.ds(at, share), :]


def pick(table, packed):
    width = packed.shape[0]
    part = jax.ShapeDtypeStruct((2, width // (4 * INNER), width), LOW)
    return pl.pallas_call(
        pick_kernel,
        out_shape=(part, part),
        in_specs=[SMEM, VMEM],
        out_specs=(VMEM,) * 2,
        compiler_params=room(16),
        cost_estimate=cost(1),
    )(table, packed)


def merge_kernel(table, own, took, out):
    share = own.shape[1]
    for n in range(2):
        for core, value in ((table[2], own), (table[3], took)):
            first = pl.multiple_of((2 * n + core) * share, share)
            out[pl.ds(first, share), :] = value[n]


def merge(table, own, took):
    _, rows, width = own.shape
    return pl.pallas_call(
        merge_kernel,
        out_shape=jax.ShapeDtypeStruct((4 * rows, width), LOW),
        in_specs=[SMEM, VMEM, VMEM],
        out_specs=VMEM,
        compiler_params=room(16),
        cost_estimate=cost(1),
    )(table, own, took)


def pack_kernel(table, columns, *refs):
    rows, out = refs[:-1], refs[-1]
    lanes = columns.shape[1]
    out[:, :lanes] = columns[...]
    share = rows[0].shape[1]
    for kind in range(len(rows) // 2):
        for first, value in ((table[0], rows[2 * kind]), (table[1], rows[2 * kind + 1])):
            for n in range(2):
                for place in range(INNER):
                    at = pl.multiple_of(((first + n) * INNER + place) * share, share)
                    start = lanes + kind * LANES
                    block = value[n, :, place * LANES : (place + 1) * LANES]
                    out[pl.ds(at, share), start : start + LANES] = block


def pack(table, columns, *rows):
    width, lanes = columns.shape
    lanes += LANES * len(rows) // 2
    return pl.pallas_call(
        pack_kernel,
        out_shape=jax.ShapeDtypeStruct((width, lanes), LOW),
        in_specs=[SMEM] + [VMEM] * (1 + len(rows)),
        out_specs=VMEM,
        compiler_params=room(16),
        cost_estimate=cost(2),
    )(table, columns, *rows)


def hop(value, distance):
    route = [(n, n ^ distance) for n in range(INNER)]
    return lax.ppermute(value, "inner", route)


def after(value, *others):
    return lax.optimization_barrier((value,) + others)[0]


def gather_places(own, *filler):
    near = [own] + [hop(own, offset_of(place)) for place in (1, 2, 3)]
    if filler:
        near, filler = lax.optimization_barrier((near, filler))
    pieces = near + [hop(piece, 1) for piece in near]
    return (pieces, *filler) if filler else pieces


def scatter_start(give, keep):
    return fold(keep, hop(give, 1))


def scatter_finish(parts):
    return [hop(part, offset_of(place)) for place, part in enumerate(parts, 1)]


def scatter_places(give, keep):
    own, *parts = scatter_start(give, keep)
    return own, scatter_finish(parts)


def dot(a, b):
    return jnp.dot(a, b, preferred_element_type=WIDE)


def under(a, b):
    return lax.dot_general(a, b, (((0,), (0,)), ((), ())), preferred_element_type=WIDE)


def per_device(
    target,
    source,
    cotangent,
    target_lengths,
    source_lengths,
    self_in,
    self_out,
    cross_query,
    cross_kv,
    cross_out,
    mlp_in,
    mlp_out,
    vectors,
    hidden_bias,
):
    rows, width = target.shape[1:]
    here = lax.axis_index("inner")
    core, chip = here & 1, here >> 1
    stream = lax.axis_index("ulys")
    group = lax.axis_index("outer")
    groups = lax.axis_size("outer")
    shares = lax.axis_size("ulys") * groups
    devices = shares * INNER
    span = rows * INNER
    pair = width // INNER
    size = pair // 2
    share = width // devices
    hidden = hidden_bias.shape[0]
    count = vectors.shape[0]
    chips = INNER // 2
    matched = shares * chips == HEADS and 2 * share == size
    target_ends = jnp.cumsum(target_lengths[stream])
    source_ends = jnp.cumsum(source_lengths[stream])
    start = jnp.stack([here, group * span]).astype(jnp.int32)
    cores = jnp.stack([core, 1 - core])
    self_table = jnp.concatenate([start, target_ends, target_ends, cores]).astype(jnp.int32)
    cross_table = jnp.concatenate([start, target_ends, source_ends, cores]).astype(jnp.int32)
    if matched:
        head_at = [(2 * core + n) * (width // shares) + chip * size for n in (0, 1)]
    else:
        head_at = [here * pair + n * size for n in (0, 1)]
    head_table = jnp.stack(head_at).astype(jnp.int32)

    def by_device(value):
        lead = value.shape[:-1]
        if matched:
            split = value.reshape(lead + (2, 2, chips, size))
            value = jnp.moveaxis(split, -2, -4)
        return value.reshape(lead + (INNER, pair))

    def by_column(value):
        lead = value.shape[:-2]
        if matched:
            split = value.reshape(lead + (chips, 2, 2, size))
            value = jnp.moveaxis(split, -4, -2)
        return value.reshape(lead + (width,))

    def cut_columns(*weights):
        whole = jnp.concatenate([w.reshape(share, -1, width) for w in weights], axis=1)
        cut = jnp.transpose(by_device(whole), (2, 0, 1, 3))
        return cut.reshape(INNER, share, -1)

    def exchange(value):
        return lax.all_to_all(value, "inner", 0, 0)

    order = here ^ jnp.array([offset_of(n) for n in range(INNER)], jnp.int32)

    core_table = jnp.stack([2 * core, 2 - 2 * core, core, 1 - core]).astype(jnp.int32)

    def head_rows(weight, found):
        if not matched:
            whole = lax.all_gather(weight, ALL, axis=0, tiled=True)
            return lax.dynamic_slice_in_dim(whole, here * pair, pair, axis=0)
        own, give = found()
        return merge(core_table, own, hop(give, 1))

    def shard_features(pieces):
        whole = jnp.stack(
            [
                piece.reshape(INNER, rows, pair)[jnp.array([n ^ place for n in range(INNER)])]
                for place, piece in enumerate(pieces)
            ]
        ).reshape(INNER, span, pair)
        whole = jnp.transpose(whole, (1, 0, 2)).reshape(span, width)
        cut = []
        for n in range(shares):
            first = (n * INNER + here) * share
            mixed = (first // pair) ^ here
            place = ((mixed >> 1) & 3) | ((mixed & 1) << 2)
            cut.append(
                lax.dynamic_slice_in_dim(whole, place * pair + first % pair, share, axis=1)
            )
        return jnp.concatenate(cut, axis=1)

    def row_grads(parts, pieces, branch):
        if not matched:
            grad = under(shard_features(pieces), jnp.concatenate(branch, axis=0))
            return [grad.astype(LOW).reshape(shares, share, width)]
        return [parts[0], hop(parts[1], 1)]

    def pack_grads(columns, *rows):
        if matched:
            return pack(core_table, columns, *[part for parts in rows for part in parts])
        lined = [
            jnp.transpose(parts[0].reshape(shares, share, INNER, LANES), (0, 2, 1, 3))
            for parts in rows
        ]
        return jnp.concatenate([columns] + [r.reshape(width, LANES) for r in lined], axis=1)

    def lanes_to_columns(got):
        kinds = got.shape[2] // pair
        got = got.reshape(INNER, share, kinds, pair).astype(WIDE)
        return jnp.transpose(got, (1, 2, 0, 3)).reshape(share, kinds * width)

    def lanes_to_rows(packed, start):
        rows = packed[:, start : start + LANES].reshape(INNER, share, LANES).astype(WIDE)
        return jnp.transpose(rows, (1, 0, 2)).reshape(share, width)

    small = jnp.concatenate([jnp.transpose(vectors), hidden_bias.reshape(share, -1)], axis=1)
    extras = small.shape[1]
    small = jnp.pad(small, ((0, 0), (0, LANES - extras)))
    def over(value):
        return lax.all_gather(value, OUTER, axis=0)

    def row_lanes(weight):
        return jnp.transpose(weight.reshape(-1, INNER, LANES), (1, 0, 2))

    raw = over(jnp.concatenate([self_in, self_out, small], axis=1))
    if matched:
        other = exchange(cut_other(cross_kv, cross_query, mlp_in, hidden))
    else:
        first_cut = jnp.transpose(mlp_in.reshape(share, shares, INNER, hidden), (2, 0, 1, 3))
        first_cut = first_cut.reshape(INNER, share, shares * hidden)
        other = [cut_columns(cross_kv, cross_query), first_cut]
        other = exchange(jnp.concatenate(other, axis=2))
    pieces = gather_places(after(target[0], other))
    cross_far = jnp.concatenate([other[:, :, : 3 * pair], row_lanes(cross_out)], axis=2)
    cross_far = over(after(cross_far, raw, *pieces[1:4])).reshape(width, -1)
    first_mine = other[:, :, 3 * pair :].reshape(INNER * share, -1)
    feed_mine = jnp.concatenate([first_mine, mlp_out], axis=0)

    raw = after(raw, *pieces[1:4])
    if matched:
        self_far = exchange(cut_self(raw.reshape(shares * share, -1)))
        self_far = self_far.reshape(INNER, shares, share, -1)
    else:
        cut = by_device(raw[:, :, : 3 * width].reshape(shares, share, 3, width))
        cut = jnp.transpose(cut, (3, 0, 1, 2, 4)).reshape(INNER, shares, share, 3 * pair)
        extra = jnp.broadcast_to(raw[None, :, :, 4 * width :], (INNER, shares, share, LANES))
        self_far = exchange(jnp.concatenate([cut, extra], axis=3))
        self_far = jnp.transpose(self_far, (1, 0, 2, 3)).reshape(1, 1, width, -1)
    q, k, v, h1, params, biases, self_packed, x_all = enter(head_table, rows, pieces, self_far)
    states, q = gather_places(after(source[0], self_far), q)
    raw = after(raw, q)
    feed_packed = over(after(feed_mine, cross_far, q))
    sout_mine = head_rows(self_out, lambda: pick_rows(core_table, 3 * width, raw, width))
    q = after(q, sout_mine)
    h_bias = self_packed.reshape(shares, INNER, share, -1)
    h_bias = h_bias[..., 3 * pair + count : 3 * pair + extras]
    h_bias = lax.dynamic_index_in_dim(h_bias, here, 1, False).reshape(1, -1).astype(WIDE)

    def stream_keys(own):
        return lax.all_gather(own, "outer", axis=0, tiled=True) if groups > 1 else own

    def own_keys(partial):
        if groups == 1:
            return partial
        return lax.psum_scatter(partial, "outer", scatter_dimension=0, tiled=True)

    k, v = stream_keys(k), stream_keys(v)
    att, self_total = attend(self_table, q, k, v, rows, True)
    w_sout, att = gather_places(sout_mine, att)
    cross_far = after(cross_far, att)
    cout_mine = head_rows(cross_out, lambda: pick(core_table, cross_far[:, 3 * pair :]))
    states, ck, cv, cross_packed = pair_heads(rows, states, cross_far, biases)
    att, cout_mine, states, ck, cv, cross_packed = gather_places(
        att, cout_mine, states, ck, cv, cross_packed
    )
    ck, cv = stream_keys(ck), stream_keys(cv)
    y1, h2, y1_all, cq = join_self(att, w_sout, x_all, params, cross_packed, biases)
    w_cout, y1, h2, y1_all, cq = gather_places(
        after(cout_mine, *att[1:4]), y1, h2, y1_all, cq
    )
    catt, cross_total = attend(cross_table, cq, ck, cv, rows, False)
    catt = gather_places(catt)
    y2, h3 = join_cross(catt, w_cout, y1_all, y1, params)
    pull_up, y2, h3 = gather_places(after(cotangent[0], *catt[1:4]), y2, h3)
    active, before_grad, give, keep, h_bias_grad, up = feed(h3, h_bias, feed_packed, pull_up)
    third_own, third_parts = scatter_places(give, keep)
    mlp_grad = feed_grad(active, before_grad, after(h3, third_own), up)
    third_parts, mlp_grad = lax.optimization_barrier((third_parts, mlp_grad))
    mlp_home = lax.psum_scatter(mlp_grad, OUTER, scatter_dimension=0, tiled=True)
    late_grad, cross_branch, late_sums = norm_back(
        4, third_own, third_parts, y2, cotangent[0], params
    )
    cross_all = gather_places(cross_branch)
    give, keep, dcq, dck, dcv, cross_sums, *cross_rows = attend_back(
        cross_table,
        cq,
        ck,
        cv,
        cross_total,
        cout_mine,
        catt[0],
        cross_all,
        rows,
        False,
        (2, cross_packed),
    )
    dck, dcv = own_keys(dck), own_keys(dcv)
    second_own, second_parts = scatter_places(give, keep)
    cross_grad = column_part((after(states, second_own), (dck, dcv)), (h2, (dcq,)))
    side_give, side_keep = side_out(
        after(active, second_own), feed_packed, dck, dcv, cross_packed
    )
    second_parts, cross_grad, side_give, side_keep = lax.optimization_barrier(
        (second_parts, cross_grad, side_give, side_keep)
    )
    cross_rows = row_grads(cross_rows, catt, cross_all)
    middle_grad, self_branch, middle_sums = norm_back(
        2, second_own, second_parts, y1, late_grad, params
    )
    packed_grad = pack_grads(cross_grad, cross_rows)
    side_own, *side_parts = scatter_start(after(side_give, self_branch), side_keep)
    self_all, packed_grad, side_own, side_parts = gather_places(
        self_branch, packed_grad, side_own, side_parts
    )
    self_all, packed_grad, side_parts = lax.optimization_barrier(
        (self_all, packed_grad, side_parts)
    )
    side_parts = scatter_finish(side_parts)
    cross_sum = lax.psum_scatter(packed_grad, OUTER, scatter_dimension=0, tiled=True)
    made = attend_back(
        self_table,
        q,
        k,
        v,
        self_total,
        sout_mine,
        att[0],
        self_all,
        rows,
        True,
        (0, self_packed, x_all) if groups == 1 else None,
    )
    dq, dk, dv, self_sums, *self_rows = made[-6:]
    dk, dv = own_keys(dk), own_keys(dv)
    if groups == 1:
        give, keep, target_sums = made[:3]
    else:
        give, keep, target_sums = spread_self(dq, dk, dv, self_packed, x_all)
    head_sums = jnp.concatenate([self_sums, cross_sums])[:, None]
    head_sums = lax.dynamic_update_slice_in_dim(
        jnp.zeros((4, INNER, pair), WIDE), head_sums, here, 1
    )
    vector_grad = jnp.concatenate(
        [
            target_sums[:2],
            middle_sums[:2],
            late_sums[:2],
            by_column(head_sums)[:2],
            middle_sums[2:3],
            by_column(head_sums)[2:],
            late_sums[2:],
        ]
    )
    vector_part = jnp.transpose(vector_grad.reshape(count, devices, share), (1, 0, 2))
    bias_part = lax.dynamic_update_slice_in_dim(
        jnp.zeros((shares, INNER, hidden), WIDE), h_bias_grad.reshape(shares, 1, hidden), here, 1
    ).reshape(devices, hidden)
    tiny = jnp.concatenate([vector_part.reshape(devices, -1), bias_part], axis=1)
    tiny = lax.all_to_all(tiny, ALL, 0, 0, tiled=True)
    give, side_parts, tiny, mlp_home = lax.optimization_barrier(
        (give, side_parts, tiny, mlp_home)
    )
    tiny = jnp.sum(after(tiny, give), axis=0)
    first_own, *first_parts = scatter_start(give, keep)
    first_parts = scatter_finish(first_parts)
    self_grad = column_part((after(h1, first_own), (dq, dk, dv)))
    self_rows = row_grads((self_rows[0], after(self_rows[1], first_own)), att, self_all)
    packed_grad = pack_grads(self_grad, self_rows)
    self_sum = lax.psum_scatter(packed_grad, OUTER, scatter_dimension=0, tiled=True)
    target_grad, target_low, _ = norm_back(
        0, first_own, first_parts, target[0], middle_grad, params
    )
    side_own, mlp_home, cross_sum = lax.optimization_barrier(
        (side_own, mlp_home, cross_sum, first_parts)
    )[:3]
    layer_out, source_grad = side_sum(side_own, side_parts, y2, params)
    cross_lanes = cross_sum[:, : 3 * pair].reshape(INNER, share, -1)
    first_lanes = mlp_home[:, width:].reshape(INNER, share, -1)
    cross_got = exchange(jnp.concatenate([cross_lanes, first_lanes], axis=2))
    self_got = exchange(self_sum[:, : 3 * pair].reshape(INNER, share, -1))
    if matched:
        cross_home, cout_home, first_home, second_home = home_feed(
            3, hidden, cross_got, cross_sum, mlp_home
        )
        self_home, sout_home = home(self_got, self_sum)
    else:
        cross_home = lanes_to_columns(cross_got[:, :, : 3 * pair])
        first_home = cross_got[:, :, 3 * pair :].reshape(INNER, share, shares, hidden)
        first_home = jnp.transpose(first_home, (1, 2, 0, 3)).reshape(share, -1).astype(WIDE)
        second_home = mlp_home[:, :width].astype(WIDE)
        cout_home = lanes_to_rows(cross_sum, 3 * pair)
        sout_home = lanes_to_rows(self_sum, 3 * pair)
        self_home = lanes_to_columns(self_got)

    return (
        layer_out[None],
        target_low[None],
        source_grad[None],
        self_home,
        sout_home,
        cross_home[:, 2 * width :],
        cross_home[:, : 2 * width],
        cout_home,
        first_home,
        second_home,
        tiny[: count * share].reshape(count, share),
        tiny[count * share :],
    )


def solution(mesh):
    streams, blocks = mesh.devices.shape
    grid = mesh.devices.reshape(streams, blocks // INNER, INNER)
    inner_mesh = Mesh(grid, ALL)
    rows = P("ulys", ("outer", "inner"), None)
    matrix = P(ALL, None)
    row_vectors = P(None, ALL)
    in_specs = (rows,) * 3 + (P(), P()) + (matrix,) * 7 + (row_vectors, P(ALL))
    out_specs = (rows,) * 3 + (matrix,) * 7 + (row_vectors, P(ALL))
    return jax.shard_map(
        per_device, mesh=inner_mesh, in_specs=in_specs, out_specs=out_specs, check_vma=False
    )
```

```python
import functools

import jax
import jax.numpy as jnp
from jax import lax
from jax.experimental import pallas as pl
from jax.experimental.pallas import tpu as pltpu
from jax.sharding import Mesh
from jax.sharding import PartitionSpec as P

HEADS = 16
LOW = jnp.bfloat16
WIDE = jnp.float32
INNER = 8
STEP = 256
WIDE_STEP = 512
LANES = 128
OUTER = ("ulys", "outer")
ALL = ("ulys", "outer", "inner")


def offset_of(place):
    return ((place & 3) << 1) | (place >> 2)


def dot_t(a, b):
    return lax.dot_general(a, b, (((1,), (1,)), ((), ())), preferred_element_type=WIDE)


def dot_n(a, b):
    return lax.dot_general(a, b, (((1,), (0,)), ((), ())), preferred_element_type=WIDE)


def dot_c(a, b):
    return lax.dot_general(a, b, (((0,), (0,)), ((), ())), preferred_element_type=WIDE)


def seg_of(position, table, first):
    count = jnp.zeros_like(position)
    for n in range(3):
        count = count + (table[first + n] <= position).astype(jnp.int32)
    return count


def iota(shape, axis):
    return lax.broadcasted_iota(jnp.int32, shape, axis)


def to_order(table, source, target, rows, factor=None):
    span = rows * INNER
    for chunk in range(source.shape[0] // span):
        for place in range(INNER):
            at = pl.multiple_of((table[0] ^ offset_of(place)) * rows, rows) + chunk * span
            value = source[pl.ds(chunk * span + place * rows, rows), :]
            if factor is not None:
                value = value * factor
            target[pl.ds(at, rows), :] = value


def from_order(table, source, target, rows):
    span = rows * INNER
    for chunk in range(target.shape[0] // span):
        for place in range(INNER):
            at = pl.multiple_of((table[0] ^ offset_of(place)) * rows, rows) + chunk * span
            target[pl.ds(chunk * span + place * rows, rows), :] = source[pl.ds(at, rows), :].astype(
                target.dtype
            )


def half_lanes(value, head, size):
    lane = iota(value.shape, 1)
    keep = (lane >= head * size) & (lane < (head + 1) * size)
    return jnp.where(keep, value, jnp.zeros_like(value))


def attend_kernel(causal, rows, size, table, q, k, v, out, log_total, qs, ks, vs, ordered):
    span, keys = q.shape[0], k.shape[0]
    chunks = keys // span
    to_order(table, q, qs, rows, jnp.asarray(size**-0.5, LOW))
    to_order(table, k, ks, rows)
    to_order(table, v, vs, rows)
    for step in range(span // WIDE_STEP):
        lo = step * WIDE_STEP
        queries = qs[lo : lo + WIDE_STEP, :]
        q_at = table[1] + lo + iota((WIDE_STEP, 1), 0)
        q_seg = seg_of(q_at, table, 2)
        count = lo + WIDE_STEP if causal and chunks == 1 else span

        def mask(start):
            k_at = start + iota((1, count), 1)
            allowed = q_seg == seg_of(k_at, table, 5)
            if causal:
                allowed = allowed & (k_at <= q_at)
            return allowed

        def scores(head, start, allowed):
            raw = dot_t(queries, half_lanes(ks[pl.ds(start, count), :], head, size))
            return jnp.where(allowed, raw, -1e30)

        parts = []
        allowed = mask(0) if chunks == 1 else None
        for head in range(2):
            if chunks == 1:
                raw = scores(head, 0, allowed)
                top = jnp.max(raw, axis=1, keepdims=True)
                weight = jnp.exp(raw - top)
                total = jnp.sum(weight, axis=1, keepdims=True)
                running = dot_n(weight.astype(LOW), vs[:count, :])
            else:

                def absorb(chunk, carry, head=head):
                    top, total, running = carry
                    start = pl.multiple_of(chunk * span, span)
                    raw = scores(head, start, mask(start))
                    new_top = jnp.maximum(top, jnp.max(raw, axis=1, keepdims=True))
                    weight = jnp.exp(raw - new_top)
                    fade = jnp.exp(top - new_top)
                    total = total * fade + jnp.sum(weight, axis=1, keepdims=True)
                    running = running * fade + dot_n(weight.astype(LOW), vs[pl.ds(start, span), :])
                    return new_top, total, running

                top, total, running = lax.fori_loop(
                    0,
                    chunks,
                    absorb,
                    (
                        jnp.full((WIDE_STEP, 1), -1e30, WIDE),
                        jnp.zeros((WIDE_STEP, 1), WIDE),
                        jnp.zeros((WIDE_STEP, 2 * size), WIDE),
                    ),
                )
            parts.append(running / total)
            logs = jnp.broadcast_to(top + jnp.log(total), (WIDE_STEP, 2 * size))
            log_total[head : head + 1, lo : lo + WIDE_STEP] = jnp.transpose(logs)[0:1, :]
        lane = iota((WIDE_STEP, 2 * size), 1)
        ordered[lo : lo + WIDE_STEP, :] = jnp.where(lane < size, parts[0], parts[1])
    from_order(table, ordered, out, rows)


def split_rows(table, first, own, branch, row, keep, give):
    row[...] = dot_c(own[...], branch[...]).astype(LOW)
    share = keep.shape[1]
    for core, out in ((table[first], keep), (table[first + 1], give)):
        for n in range(2):
            at = pl.multiple_of((2 * n + core) * share, share)
            out[n] = row[pl.ds(at, share), :]


def attend_back_kernel(causal, rows, size, start, lined, table, q, k, v, log_total, weight, *refs):
    own = refs[0] if lined else None
    refs = refs[1:] if lined else refs
    pieces, refs = refs[:INNER], refs[INNER:]
    late = []
    if start is not None:
        late, refs = [refs[0]], refs[1:]
        if start == 0:
            late, refs = late + [refs[0]], refs[1:]
            give, keep, norm_sums, refs = *refs[:3], refs[3:]
        else:
            give, keep, refs = *refs[:2], refs[2:]
    dq, dk, dv, sums, refs = *refs[:4], refs[4:]
    if lined:
        row_keep, row_give, refs = *refs[:2], refs[2:]
    qs, ks, vs, ups, dqs, dks, dvs, branch, row, marks, *near = refs
    copies = pull(pieces, 0, branch, marks)
    loads = []
    for n, source in enumerate(late):
        loads.append(pltpu.make_async_copy(source, near[n], near[-1].at[n]))
    for load in loads:
        load.start()
    span, keys = q.shape[0], k.shape[0]
    chunks = keys // span
    scale = size**-0.5
    to_order(table, q, qs, rows, jnp.asarray(scale, LOW))
    to_order(table, k, ks, rows)
    to_order(table, v, vs, rows)
    finish(copies)
    upstream = dot_t(branch[...], weight[...]).astype(LOW)
    for place in range(INNER):
        at = pl.multiple_of((table[0] ^ offset_of(place)) * rows, rows)
        ups[pl.ds(at, rows), :] = upstream[place * rows : (place + 1) * rows, :]
    if lined:
        split_rows(table, 8, own, branch, row, row_keep, row_give)
    dks[...] = jnp.zeros_like(dks)
    dvs[...] = jnp.zeros_like(dvs)
    for step in range(span // STEP):
        lo = step * STEP
        queries = qs[lo : lo + STEP, :]
        upstream = ups[lo : lo + STEP, :]
        q_at = table[1] + lo + iota((1, STEP), 1)
        q_seg = seg_of(q_at, table, 2)
        count = lo + STEP if causal and chunks == 1 else span
        q_pair = [half_lanes(queries, head, size) for head in range(2)]
        up_pair = [half_lanes(upstream, head, size) for head in range(2)]
        logs = [log_total[head : head + 1, lo : lo + STEP] for head in range(2)]

        def make(start):
            k_at = start + iota((count, 1), 0)
            allowed = q_seg == seg_of(k_at, table, 5)
            if causal:
                allowed = allowed & (k_at <= q_at)
            keys_here = ks[pl.ds(start, count), :]
            k_pair = [half_lanes(keys_here, head, size) for head in range(2)]
            probs, lean = [], []
            for head in range(2):
                raw = dot_t(k_pair[head], queries)
                probs.append(jnp.exp(jnp.where(allowed, raw - logs[head], -1e30)))
                slope = dot_t(vs[pl.ds(start, count), :], up_pair[head])
                lean.append(probs[head] * slope)
            return k_pair, probs, lean

        def settle(start, delta, made):
            k_pair, probs, lean = made
            push = [(lean[n] - probs[n] * delta[n]).astype(LOW) for n in range(2)]
            low = [probs[n].astype(LOW) for n in range(2)]
            at = pl.ds(start, count)
            dvs[at, :] += dot_n(jnp.concatenate(low, axis=1), jnp.concatenate(up_pair, axis=0))
            dks[at, :] += dot_n(jnp.concatenate(push, axis=1), jnp.concatenate(q_pair, axis=0))
            return dot_c(jnp.concatenate(push, axis=0), jnp.concatenate(k_pair, axis=0))

        def slopes(made):
            return [jnp.sum(made[2][n], axis=0, keepdims=True) for n in range(2)]

        if chunks == 1:
            made = make(0)
            total_dq = settle(0, slopes(made), made)
        else:

            def measure(chunk, delta):
                more = slopes(make(pl.multiple_of(chunk * span, span)))
                return [delta[n] + more[n] for n in range(2)]

            delta = lax.fori_loop(0, chunks, measure, [jnp.zeros((1, STEP), WIDE)] * 2)

            def absorb(chunk, running, delta=delta):
                start = pl.multiple_of(chunk * span, span)
                return running + settle(start, delta, make(start))

            total_dq = lax.fori_loop(0, chunks, absorb, jnp.zeros((STEP, 2 * size), WIDE))
        dqs[lo : lo + STEP, :] = total_dq * scale
    from_order(table, dqs, dq, rows)
    from_order(table, dks, dk, rows)
    from_order(table, dvs, dv, rows)
    finish(loads)
    if start is not None:
        packed = near[0]
        x_all = near[1] if start == 0 else None
        kinds = 3 if start == 0 else 1
        back = packed[:, start * LANES : (start + kinds) * LANES]
        first = second = None
        for at, out in ((span // 2, give), (0, keep)):
            at = slice(at, at + span // 2)
            left = [part[at, :] for part in (dq, dk, dv)[:kinds]]
            left = left[0] if kinds == 1 else jnp.concatenate(left, axis=1)
            slope = dot_t(left, back)
            out[...] = slope.astype(out.dtype)
            if start == 0:
                centred, inverse = centre(x_all[at, :].astype(WIDE))
                gain = jnp.sum(slope * (centred * inverse), axis=0, keepdims=True)
                shift = jnp.sum(slope, axis=0, keepdims=True)
                first = gain if first is None else first + gain
                second = shift if second is None else second + shift
        if start == 0:
            norm_sums[0:1, :] = first
            norm_sums[1:2, :] = second
    sums[0:1, :] = jnp.sum(dqs[...].astype(LOW).astype(WIDE), axis=0, keepdims=True)
    sums[1:2, :] = jnp.sum(dvs[...].astype(LOW).astype(WIDE), axis=0, keepdims=True)


HBM = pl.BlockSpec(memory_space=pl.ANY)


def room(megabytes):
    return pltpu.CompilerParams(vmem_limit_bytes=megabytes * 2**20)


def pull(pieces, index, target, marks):
    rows = target.shape[0] // INNER
    copies = []
    for place in range(INNER):
        source = pieces[place].at[pl.ds(index * rows, rows), :]
        aim = target.at[pl.ds(place * rows, rows), :]
        copies.append(pltpu.make_async_copy(source, aim, marks.at[place]))
    for copy in copies:
        copy.start()
    return copies


def finish(copies):
    for copy in copies:
        copy.wait()


def cost(micros):
    return pl.CostEstimate(
        flops=int(micros * 1.1e9), bytes_accessed=int(micros * 3.5e6), transcendentals=0
    )


SMEM = pl.BlockSpec(memory_space=pltpu.SMEM)
VMEM = pl.BlockSpec(memory_space=pltpu.VMEM)


def attend(table, q, k, v, rows, causal):
    span, pair = q.shape
    keys = k.shape[0]
    return pl.pallas_call(
        functools.partial(attend_kernel, causal, rows, pair // 2),
        out_shape=(
            jax.ShapeDtypeStruct((span, pair), LOW),
            jax.ShapeDtypeStruct((2, span), WIDE),
        ),
        in_specs=[SMEM, VMEM, VMEM, VMEM],
        out_specs=(VMEM, VMEM),
        scratch_shapes=[
            pltpu.VMEM((span, pair), LOW),
            pltpu.VMEM((keys, pair), LOW),
            pltpu.VMEM((keys, pair), LOW),
            pltpu.VMEM((span, pair), WIDE),
        ],
        compiler_params=room(60),
        cost_estimate=cost(6),
    )(table, q, k, v)


def attend_back(table, q, k, v, log_total, weight, own, pieces, rows, causal, back=None):
    span, pair = q.shape
    keys = k.shape[0]
    width = weight.shape[1]
    part = jax.ShapeDtypeStruct((2, pair // 4, width), LOW)
    lined = [] if own is None else [own]
    spread_shape = (
        jax.ShapeDtypeStruct((span // 2, width), LOW),
        jax.ShapeDtypeStruct((span // 2, width), WIDE),
    )
    start, *extra = back if back else (None,)
    if start == 0:
        spread_shape += (jax.ShapeDtypeStruct((2, width), WIDE),)
    return pl.pallas_call(
        functools.partial(attend_back_kernel, causal, rows, pair // 2, start, bool(lined)),
        out_shape=(spread_shape if back else ())
        + (
            jax.ShapeDtypeStruct((span, pair), LOW),
            jax.ShapeDtypeStruct((keys, pair), LOW),
            jax.ShapeDtypeStruct((keys, pair), LOW),
            jax.ShapeDtypeStruct((2, pair), WIDE),
        )
        + ((part, part) if lined else ()),
        in_specs=[SMEM] + [VMEM] * (5 + len(lined)) + [HBM] * (INNER + len(extra)),
        out_specs=(VMEM,) * (4 + 2 * len(lined) + (len(spread_shape) if back else 0)),
        scratch_shapes=[
            pltpu.VMEM((span, pair), LOW),
            pltpu.VMEM((keys, pair), LOW),
            pltpu.VMEM((keys, pair), LOW),
            pltpu.VMEM((span, pair), LOW),
            pltpu.VMEM((span, pair), WIDE),
            pltpu.VMEM((keys, pair), WIDE),
            pltpu.VMEM((keys, pair), WIDE),
            pltpu.VMEM((span, width), LOW),
            pltpu.VMEM((pair, width), LOW),
            pltpu.SemaphoreType.DMA((INNER,)),
        ]
        + [pltpu.VMEM(value.shape, LOW) for value in extra]
        + ([pltpu.SemaphoreType.DMA((2,))] if extra else []),
        compiler_params=room(60),
        cost_estimate=cost(10),
    )(table, q, k, v, log_total, weight, *lined, *pieces, *extra)


def centre(value):
    center = jnp.mean(value, axis=-1, keepdims=True)
    centred = value - center
    spread = jnp.mean(centred * centred, axis=-1, keepdims=True)
    return centred, lax.rsqrt(spread + 1e-05)


def norm_of(value, gain, shift):
    centred, inverse = centre(value)
    return (centred * inverse * gain + shift).astype(LOW)


def enter_kernel(kinds, table, far, *refs):
    pieces, refs = refs[:INNER], refs[INNER:]
    q, k, v, h, params, biases, packed, x_all, blocks, marks, mark = refs
    loads = []
    for place in range(far.shape[0]):
        loads.append(pltpu.make_async_copy(far.at[place], blocks.at[:, place], mark.at[place]))
    for load in loads:
        load.start()
    copies = pull(pieces, 0, x_all, marks)
    finish(loads)
    packed[...] = blocks[...].reshape(packed.shape)
    edge = kinds * LANES
    extra = packed[:, edge : edge + LANES].astype(WIDE)
    params[...] = jnp.transpose(extra)[:16, :]
    size = LANES // 2
    mine = [packed[pl.ds(pl.multiple_of(table[n], 16), size), edge : edge + LANES] for n in (0, 1)]
    biases[...] = jnp.transpose(jnp.concatenate(mine, axis=0).astype(WIDE))[:16, :]
    finish(copies)
    half = x_all.shape[0] // 2
    for part in range(2):
        at = slice(part * half, (part + 1) * half)
        low = norm_of(x_all[at, :].astype(WIDE), params[0:1, :], params[1:2, :])
        h[at, :] = low
        made = dot_n(low, packed[:, :edge])
        q[at, :] = (made[:, :LANES] + biases[6:7, :]).astype(LOW)
        k[at, :] = made[:, LANES : 2 * LANES].astype(LOW)
        v[at, :] = (made[:, 2 * LANES :] + biases[7:8, :]).astype(LOW)


def enter(table, rows, pieces, packed):
    width = pieces[0].shape[1]
    span = rows * INNER
    heads = jax.ShapeDtypeStruct((span, LANES), LOW)
    return pl.pallas_call(
        functools.partial(enter_kernel, 3),
        out_shape=(
            heads,
            heads,
            heads,
            jax.ShapeDtypeStruct((span, width), LOW),
            jax.ShapeDtypeStruct((16, width), WIDE),
            jax.ShapeDtypeStruct((16, LANES), WIDE),
            jax.ShapeDtypeStruct((width, 4 * LANES), LOW),
            jax.ShapeDtypeStruct((span, width), LOW),
        ),
        in_specs=[SMEM] + [HBM] * (1 + INNER),
        out_specs=(VMEM,) * 8,
        scratch_shapes=[
            pltpu.VMEM((packed.shape[1], packed.shape[0]) + packed.shape[2:], LOW),
            pltpu.SemaphoreType.DMA((INNER,)),
            pltpu.SemaphoreType.DMA((packed.shape[0],)),
        ],
        compiler_params=room(60),
        cost_estimate=cost(4),
    )(table, packed, *pieces)


def join_kernel(vector, first, query, *refs):
    pieces, weights, refs = refs[:INNER], refs[INNER : 2 * INNER], refs[2 * INNER :]
    if query is None:
        far, base_own, params, y_own, h, weight, left, heads, marks, base, base_mark = refs
    else:
        far, params, packed, biases, y_own, h, y_all, cq, weight, left, heads, marks, base, base_mark = refs
    span = left.shape[0]
    block = span // INNER
    loads = pull(weights, 0, weight, marks.at[1])
    base_load = pltpu.make_async_copy(far, base, base_mark)
    copies = []
    for place in range(INNER):
        copies.append(pltpu.make_async_copy(pieces[place], heads.at[place], marks.at[0, place]))
    for copy in copies:
        copy.start()
    base_load.start()
    finish(copies + loads + [base_load])
    parts = INNER // 2
    for part in range(parts):
        at = slice(part * 2 * block, (part + 1) * 2 * block)
        for n in range(2 * part, 2 * part + 2):
            for place in range(INNER):
                first_row = (n ^ place) * block
                left[n * block : (n + 1) * block, place * LANES : (place + 1) * LANES] = heads[
                    place, first_row : first_row + block, :
                ]
        value = base[at, :].astype(WIDE)
        if query is None and part == 0:
            value = jnp.concatenate([base_own[...], value[block:, :]], axis=0)
        y = value + dot_n(left[at, :], weight[...]) + params[vector : vector + 1, :]
        if part == 0:
            y_own[...] = y[:block, :]
        low = norm_of(y, params[first : first + 1, :], params[first + 1 : first + 2, :])
        h[at, :] = low
        if query is not None:
            y_all[at, :] = y.astype(LOW)
            made = dot_n(low, packed[:, query * LANES : (query + 1) * LANES])
            cq[at, :] = (made + biases[9:10, :]).astype(LOW)


def join_self(pieces, weights, base, params, packed, biases):
    span, width = base.shape
    return pl.pallas_call(
        functools.partial(join_kernel, 8, 2, 2),
        out_shape=(
            jax.ShapeDtypeStruct((span // INNER, width), WIDE),
            jax.ShapeDtypeStruct((span, width), LOW),
            jax.ShapeDtypeStruct((span, width), LOW),
            jax.ShapeDtypeStruct((span, LANES), LOW),
        ),
        in_specs=[HBM] * (2 * INNER + 1) + [VMEM] * 3,
        out_specs=(VMEM,) * 4,
        scratch_shapes=[
            pltpu.VMEM((width, width), LOW),
            pltpu.VMEM((span, width), LOW),
            pltpu.VMEM((INNER, span, LANES), LOW),
            pltpu.SemaphoreType.DMA((2, INNER)),
            pltpu.VMEM((span, width), LOW),
            pltpu.SemaphoreType.DMA,
        ],
        compiler_params=room(60),
        cost_estimate=cost(6),
    )(*pieces, *weights, base, params, packed, biases)


def join_cross(pieces, weights, base, base_own, params):
    span, width = base.shape
    return pl.pallas_call(
        functools.partial(join_kernel, 11, 4, None),
        out_shape=(
            jax.ShapeDtypeStruct((span // INNER, width), WIDE),
            jax.ShapeDtypeStruct((span, width), LOW),
        ),
        in_specs=[HBM] * (2 * INNER + 1) + [VMEM] * 2,
        out_specs=(VMEM,) * 2,
        scratch_shapes=[
            pltpu.VMEM((width, width), LOW),
            pltpu.VMEM((span, width), LOW),
            pltpu.VMEM((INNER, span, LANES), LOW),
            pltpu.SemaphoreType.DMA((2, INNER)),
            pltpu.VMEM((span, width), LOW),
            pltpu.SemaphoreType.DMA,
        ],
        compiler_params=room(60),
        cost_estimate=cost(5),
    )(*pieces, *weights, base, base_own, params)


def load_rows(packed, start, target, marks):
    shares = packed.shape[0]
    rows = target.shape[0] // shares
    copies = []
    for n in range(shares):
        source = packed.at[n, pl.ds(start, rows), :]
        aim = target.at[pl.ds(n * rows, rows), :]
        copies.append(pltpu.make_async_copy(source, aim, marks.at[n]))
    for copy in copies:
        copy.start()
    return copies


def feed_kernel(h, bias, packed, *refs):
    pieces = refs[:INNER]
    act, slope, give, keep, bias_grad, up, first, second, marks, weight_marks = refs[INNER:]
    span, width = up.shape
    hidden = second.shape[0]
    loads = load_rows(packed, 0, first, weight_marks.at[0])
    copies = load_rows(packed, width // packed.shape[0], second, weight_marks.at[1])
    copies += pull(pieces, 0, up, marks)
    finish(loads)
    step = 256
    inner = (2.0 / 3.141592653589793) ** 0.5
    for n in range(hidden // step):
        at = slice(n * step, (n + 1) * step)
        pre = dot_n(h[...], first[:, at]) + bias[:, at]
        square = pre * pre
        bend = jnp.tanh(pre * (inner + (inner * 0.044715) * square))
        half = 0.5 * bend + 0.5
        act[:, at] = (pre * half).astype(LOW)
        if n == 0:
            finish(copies)
        rise = half + 0.5 * pre * (1.0 - bend * bend) * (inner + (3 * inner * 0.044715) * square)
        low = (dot_t(up[...], second[at, :]) * rise).astype(LOW)
        slope[:, at] = low
        bias_grad[:, at] = jnp.sum(low.astype(WIDE), axis=0, keepdims=True)
    give[...] = dot_t(slope[span // 2 :, :], first[...]).astype(LOW)
    keep[...] = dot_t(slope[: span // 2, :], first[...])


def feed(h, bias, packed, pieces):
    span, width = h.shape
    hidden = bias.shape[1]
    shares = packed.shape[0]
    return pl.pallas_call(
        feed_kernel,
        out_shape=(
            jax.ShapeDtypeStruct((span, hidden), LOW),
            jax.ShapeDtypeStruct((span, hidden), LOW),
            jax.ShapeDtypeStruct((span // 2, width), LOW),
            jax.ShapeDtypeStruct((span // 2, width), WIDE),
            jax.ShapeDtypeStruct((1, hidden), WIDE),
            jax.ShapeDtypeStruct((span, width), LOW),
        ),
        in_specs=[VMEM] * 2 + [HBM] * (1 + INNER),
        out_specs=(VMEM,) * 6,
        scratch_shapes=[
            pltpu.VMEM((width, hidden), LOW),
            pltpu.VMEM((hidden, width), LOW),
            pltpu.SemaphoreType.DMA((INNER,)),
            pltpu.SemaphoreType.DMA((2, shares)),
        ],
        compiler_params=room(44),
        cost_estimate=cost(13),
    )(h, bias, packed, *pieces)


def side_kernel(act, packed, dk, dv, pair_weight, give, keep, second, marks):
    copies = load_rows(packed, second.shape[1] // packed.shape[0], second, marks)
    half, width = keep.shape[0], second.shape[1]
    weight = pair_weight[:, : 2 * LANES]
    spans = ((half, give), (0, keep))
    for at, out in spans:
        left = jnp.concatenate([dk[at : at + half, :], dv[at : at + half, :]], axis=1)
        out[:, width:] = dot_t(left, weight).astype(out.dtype)
    finish(copies)
    for at, out in spans:
        out[:, :width] = dot_n(act[at : at + half, :], second[...]).astype(out.dtype)


def side_out(act, packed, dk, dv, pair_weight):
    span, hidden = act.shape
    shares, _, width = packed.shape
    return pl.pallas_call(
        side_kernel,
        out_shape=(
            jax.ShapeDtypeStruct((span // 2, 2 * width), LOW),
            jax.ShapeDtypeStruct((span // 2, 2 * width), WIDE),
        ),
        in_specs=[VMEM, HBM] + [VMEM] * 3,
        out_specs=(VMEM,) * 2,
        scratch_shapes=[
            pltpu.VMEM((hidden, width), LOW),
            pltpu.SemaphoreType.DMA((shares,)),
        ],
        compiler_params=room(24),
        cost_estimate=cost(4),
    )(act, packed, dk, dv, pair_weight)


def side_sum_kernel(own, one, two, three, y, params, layer, source):
    total = own[...] + one[...].astype(WIDE) + two[...].astype(WIDE) + three[...].astype(WIDE)
    width = y.shape[1]
    layer[...] = (y[...] + total[:, :width] + params[12:13, :]).astype(LOW)
    source[...] = total[:, width:].astype(LOW)


def side_sum(own, parts, y, params):
    out = jax.ShapeDtypeStruct(y.shape, LOW)
    return pl.pallas_call(
        side_sum_kernel,
        out_shape=(out, out),
        in_specs=[VMEM] * 6,
        out_specs=(VMEM,) * 2,
        compiler_params=room(16),
        cost_estimate=cost(1),
    )(own, *parts, y, params)


def feed_grad_kernel(act, slope, h, up, out):
    width = up.shape[1]
    step = 256
    for n in range(width // step):
        at = slice(n * step, (n + 1) * step)
        out[at, width:] = dot_c(h[:, at], slope[...]).astype(LOW)
    for n in range(act.shape[1] // step):
        at = slice(n * step, (n + 1) * step)
        out[at, :width] = dot_c(act[:, at], up[...]).astype(LOW)


def feed_grad(act, slope, h, up):
    width = h.shape[1]
    hidden = act.shape[1]
    return pl.pallas_call(
        feed_grad_kernel,
        out_shape=jax.ShapeDtypeStruct((width, width + hidden), LOW),
        in_specs=[VMEM] * 4,
        out_specs=VMEM,
        compiler_params=room(40),
        cost_estimate=cost(6),
    )(act, slope, h, up)


def fold_kernel(keep, took, own, one, two, three):
    rows = own.shape[0]
    own[...] = keep[:rows, :] + took[:rows, :].astype(WIDE)
    for n, part in enumerate((one, two, three), 1):
        at = slice(n * rows, (n + 1) * rows)
        part[...] = (keep[at, :] + took[at, :].astype(WIDE)).astype(LOW)


def fold(keep, took):
    half, width = keep.shape
    part = jax.ShapeDtypeStruct((half // 4, width), LOW)
    return pl.pallas_call(
        fold_kernel,
        out_shape=(jax.ShapeDtypeStruct((half // 4, width), WIDE), part, part, part),
        in_specs=[VMEM] * 2,
        out_specs=(VMEM,) * 4,
        compiler_params=room(16),
        cost_estimate=cost(1),
    )(keep, took)


def norm_back_kernel(first, own, one, two, three, value, base, params, grad, low, sums):
    slope = own[...] + one[...].astype(WIDE) + two[...].astype(WIDE) + three[...].astype(WIDE)
    centred, inverse = centre(value[...].astype(WIDE))
    unit = centred * inverse
    lean = slope * params[first : first + 1, :]
    flat = jnp.mean(lean, axis=-1, keepdims=True)
    tilt = jnp.mean(lean * unit, axis=-1, keepdims=True)
    total = base[...].astype(WIDE) + inverse * (lean - flat - unit * tilt)
    grad[...] = total
    cut = total.astype(LOW)
    low[...] = cut
    sums[0:1, :] = jnp.sum(slope * unit, axis=0, keepdims=True)
    sums[1:2, :] = jnp.sum(slope, axis=0, keepdims=True)
    sums[2:3, :] = jnp.sum(cut.astype(WIDE), axis=0, keepdims=True)
    sums[3:4, :] = jnp.sum(base[...].astype(WIDE), axis=0, keepdims=True)


def norm_back(first, own, parts, value, base, params):
    rows, width = own.shape
    return pl.pallas_call(
        functools.partial(norm_back_kernel, first),
        out_shape=(
            jax.ShapeDtypeStruct((rows, width), WIDE),
            jax.ShapeDtypeStruct((rows, width), LOW),
            jax.ShapeDtypeStruct((4, width), WIDE),
        ),
        in_specs=[VMEM] * 7,
        out_specs=(VMEM,) * 3,
        compiler_params=room(16),
        cost_estimate=cost(2),
    )(own, *parts, value, base, params)


def pair_kernel(biases, far, *refs):
    pieces, (states, k, v, packed, marks, mark) = refs[:INNER], refs[INNER:]
    load = pltpu.make_async_copy(far.at[:, pl.ds(0, packed.shape[1])], packed, mark)
    load.start()
    finish(pull(pieces, 0, states, marks) + [load])
    made = dot_n(states[...], packed[:, : 2 * LANES])
    k[...] = made[:, :LANES].astype(LOW)
    v[...] = (made[:, LANES:] + biases[10:11, :]).astype(LOW)


def pair_heads(rows, pieces, packed, biases):
    width = pieces[0].shape[1]
    span = rows * INNER
    heads = jax.ShapeDtypeStruct((span, LANES), LOW)
    return pl.pallas_call(
        pair_kernel,
        out_shape=(
            jax.ShapeDtypeStruct((span, width), LOW),
            heads,
            heads,
            jax.ShapeDtypeStruct((width, 3 * LANES), LOW),
        ),
        in_specs=[VMEM] + [HBM] * (1 + INNER),
        out_specs=(VMEM,) * 4,
        scratch_shapes=[pltpu.SemaphoreType.DMA((INNER,)), pltpu.SemaphoreType.DMA],
        compiler_params=room(60),
        cost_estimate=cost(3),
    )(biases, packed, *pieces)


def spread_self_kernel(dq, dk, dv, packed, x_all, give, keep, sums):
    half = x_all.shape[0] // 2
    weight = packed[:, : 3 * LANES]
    first = second = None
    for part, out in ((1, give), (0, keep)):
        at = slice(part * half, (part + 1) * half)
        left = jnp.concatenate([dq[at, :], dk[at, :], dv[at, :]], axis=1)
        slope = dot_t(left, weight)
        out[...] = slope.astype(out.dtype)
        centred, inverse = centre(x_all[at, :].astype(WIDE))
        gain = jnp.sum(slope * (centred * inverse), axis=0, keepdims=True)
        shift = jnp.sum(slope, axis=0, keepdims=True)
        first = gain if first is None else first + gain
        second = shift if second is None else second + shift
    sums[0:1, :] = first
    sums[1:2, :] = second


def spread_self(dq, dk, dv, packed, x_all):
    span, width = x_all.shape
    return pl.pallas_call(
        spread_self_kernel,
        out_shape=(
            jax.ShapeDtypeStruct((span // 2, width), LOW),
            jax.ShapeDtypeStruct((span // 2, width), WIDE),
            jax.ShapeDtypeStruct((2, width), WIDE),
        ),
        in_specs=[VMEM] * 5,
        out_specs=(VMEM,) * 3,
        compiler_params=room(32),
        cost_estimate=cost(4),
    )(dq, dk, dv, packed, x_all)


def spread_columns(got, kinds, out):
    size = LANES // 2
    for kind in range(kinds):
        heads = {}
        for place in range(INNER):
            for n in (0, 1):
                at = kind * LANES + n * size
                number = (2 * (place & 1) + n) * (INNER // 2) + (place >> 1)
                heads[number] = got[place][:, at : at + size].astype(WIDE)
        for number in range(0, 2 * INNER, 2):
            at = kind * INNER * LANES + number * size
            both = jnp.concatenate([heads[number], heads[number + 1]], axis=1)
            out[:, at : at + LANES] = both


def spread_rows(packed, start, out):
    share = out.shape[0]
    for place in range(INNER):
        block = packed[place * share : (place + 1) * share, start : start + LANES]
        out[:, place * LANES : (place + 1) * LANES] = block.astype(WIDE)


def home_kernel(kinds, got, packed, columns, rows):
    spread_columns(got, kinds, columns)
    spread_rows(packed, kinds * LANES, rows)


def home(got, packed):
    share, lanes = got.shape[1:]
    return pl.pallas_call(
        functools.partial(home_kernel, lanes // LANES),
        out_shape=(
            jax.ShapeDtypeStruct((share, lanes * INNER), WIDE),
            jax.ShapeDtypeStruct((share, LANES * INNER), WIDE),
        ),
        in_specs=[VMEM] * 2,
        out_specs=(VMEM,) * 2,
        compiler_params=room(16),
        cost_estimate=cost(2),
    )(got, packed)


def home_feed_kernel(kinds, hidden, got, packed, feed_sum, *outs):
    columns, rows, first, second = outs
    spread_columns(got, kinds, columns)
    spread_rows(packed, kinds * LANES, rows)
    width = second.shape[1]
    second[...] = feed_sum[:, :width].astype(WIDE)
    lanes = got.shape[2] - kinds * LANES
    for n in range(lanes // hidden):
        for place in range(INNER):
            at = (n * INNER + place) * hidden
            start = kinds * LANES + n * hidden
            first[:, at : at + hidden] = got[place, :, start : start + hidden].astype(WIDE)


def home_feed(kinds, hidden, got, packed, feed_sum):
    share, lanes = got.shape[1:]
    rows = jax.ShapeDtypeStruct((share, LANES * INNER), WIDE)
    return pl.pallas_call(
        functools.partial(home_feed_kernel, kinds, hidden),
        out_shape=(
            jax.ShapeDtypeStruct((share, kinds * LANES * INNER), WIDE),
            rows,
            jax.ShapeDtypeStruct((share, (lanes - kinds * LANES) * INNER), WIDE),
            jax.ShapeDtypeStruct((feed_sum.shape[0], LANES * INNER), WIDE),
        ),
        in_specs=[VMEM] * 3,
        out_specs=(VMEM,) * 4,
        compiler_params=room(24),
        cost_estimate=cost(3),
    )(got, packed, feed_sum)


def column_part_kernel(kinds, *refs):
    count = len(kinds)
    lefts, rights, column = refs[:count], refs[count:-1], refs[-1]
    at = first = 0
    for left, kind in zip(lefts, kinds):
        right = [value[...] for value in rights[first : first + kind]]
        right = right[0] if kind == 1 else jnp.concatenate(right, axis=1)
        lanes = kind * LANES
        column[:, at : at + lanes] = dot_c(left[...], right).astype(LOW)
        at, first = at + lanes, first + kind


def column_part(*pairs):
    width = pairs[0][0].shape[1]
    kinds = tuple(len(rights) for _, rights in pairs)
    lefts = [left for left, _ in pairs]
    rights = [value for _, values in pairs for value in values]
    return pl.pallas_call(
        functools.partial(column_part_kernel, kinds),
        out_shape=jax.ShapeDtypeStruct((width, LANES * sum(kinds)), LOW),
        in_specs=[VMEM] * (len(lefts) + len(rights)),
        out_specs=VMEM,
        compiler_params=room(24),
        cost_estimate=cost(3),
    )(*lefts, *rights)


def head_lanes(source, start, device):
    size = LANES // 2
    at = [start + ((2 * (device & 1) + n) * (INNER // 2) + (device >> 1)) * size for n in (0, 1)]
    return jnp.concatenate([source[:, a : a + size] for a in at], axis=1)


def cut_self_kernel(raw, out):
    width = INNER * LANES
    for device in range(INNER):
        for kind in range(3):
            at = slice(kind * LANES, (kind + 1) * LANES)
            out[device, :, at] = head_lanes(raw, kind * width, device)
        out[device, :, 3 * LANES :] = raw[:, 4 * width :]


def cut_self(raw):
    rows = raw.shape[0]
    return pl.pallas_call(
        cut_self_kernel,
        out_shape=jax.ShapeDtypeStruct((INNER, rows, 4 * LANES), LOW),
        in_specs=[VMEM],
        out_specs=VMEM,
        compiler_params=room(16),
        cost_estimate=cost(2),
    )(raw)


def cut_other_kernel(hidden, pair_weight, query, first, out):
    width = INNER * LANES
    groups = first.shape[1] // (INNER * hidden)
    for device in range(INNER):
        for kind, source in enumerate((pair_weight, pair_weight, query)):
            at = slice(kind * LANES, (kind + 1) * LANES)
            out[device, :, at] = head_lanes(source, (kind % 2) * width, device)
        for n in range(groups):
            at = (n * INNER + device) * hidden
            start = 3 * LANES + n * hidden
            out[device, :, start : start + hidden] = first[:, at : at + hidden]


def cut_other(pair_weight, query, first, hidden):
    rows = query.shape[0]
    lanes = 3 * LANES + first.shape[1] // INNER
    return pl.pallas_call(
        functools.partial(cut_other_kernel, hidden),
        out_shape=jax.ShapeDtypeStruct((INNER, rows, lanes), LOW),
        in_specs=[VMEM] * 3,
        out_specs=VMEM,
        compiler_params=room(16),
        cost_estimate=cost(1),
    )(pair_weight, query, first)


def pick_rows_kernel(start, table, raw, own, give, marks):
    width = own.shape[2]
    copies = []
    for n, out in enumerate((own, give)):
        source = raw.at[pl.ds(table[n], 2), :, pl.ds(start, width)]
        copies.append(pltpu.make_async_copy(source, out, marks.at[n]))
    for copy in copies:
        copy.start()
    finish(copies)


def pick_rows(table, start, raw, width):
    part = jax.ShapeDtypeStruct((2, raw.shape[1], width), LOW)
    return pl.pallas_call(
        functools.partial(pick_rows_kernel, start),
        out_shape=(part, part),
        in_specs=[SMEM, HBM],
        out_specs=(VMEM,) * 2,
        scratch_shapes=[pltpu.SemaphoreType.DMA((2,))],
        compiler_params=room(16),
        cost_estimate=cost(1),
    )(table, raw)


def pick_kernel(table, packed, own, give):
    share = own.shape[1]
    for first, out in ((table[0], own), (table[1], give)):
        for n in range(2):
            for place in range(INNER):
                at = pl.multiple_of(((first + n) * INNER + place) * share, share)
                out[n, :, place * LANES : (place + 1) * LANES] = packed[pl.ds(at, share), :]


def pick(table, packed):
    width = packed.shape[0]
    part = jax.ShapeDtypeStruct((2, width // (4 * INNER), width), LOW)
    return pl.pallas_call(
        pick_kernel,
        out_shape=(part, part),
        in_specs=[SMEM, VMEM],
        out_specs=(VMEM,) * 2,
        compiler_params=room(16),
        cost_estimate=cost(1),
    )(table, packed)


def merge_kernel(table, own, took, out):
    share = own.shape[1]
    for n in range(2):
        for core, value in ((table[2], own), (table[3], took)):
            first = pl.multiple_of((2 * n + core) * share, share)
            out[pl.ds(first, share), :] = value[n]


def merge(table, own, took):
    _, rows, width = own.shape
    return pl.pallas_call(
        merge_kernel,
        out_shape=jax.ShapeDtypeStruct((4 * rows, width), LOW),
        in_specs=[SMEM, VMEM, VMEM],
        out_specs=VMEM,
        compiler_params=room(16),
        cost_estimate=cost(1),
    )(table, own, took)


def pack_kernel(table, columns, *refs):
    rows, out = refs[:-1], refs[-1]
    lanes = columns.shape[1]
    out[:, :lanes] = columns[...]
    share = rows[0].shape[1]
    for kind in range(len(rows) // 2):
        for first, value in ((table[0], rows[2 * kind]), (table[1], rows[2 * kind + 1])):
            for n in range(2):
                for place in range(INNER):
                    at = pl.multiple_of(((first + n) * INNER + place) * share, share)
                    start = lanes + kind * LANES
                    block = value[n, :, place * LANES : (place + 1) * LANES]
                    out[pl.ds(at, share), start : start + LANES] = block


def pack(table, columns, *rows):
    width, lanes = columns.shape
    lanes += LANES * len(rows) // 2
    return pl.pallas_call(
        pack_kernel,
        out_shape=jax.ShapeDtypeStruct((width, lanes), LOW),
        in_specs=[SMEM] + [VMEM] * (1 + len(rows)),
        out_specs=VMEM,
        compiler_params=room(16),
        cost_estimate=cost(2),
    )(table, columns, *rows)


def hop(value, distance):
    route = [(n, n ^ distance) for n in range(INNER)]
    return lax.ppermute(value, "inner", route)


def after(value, *others):
    return lax.optimization_barrier((value,) + others)[0]


def gather_places(own, *filler):
    near = [own] + [hop(own, offset_of(place)) for place in (1, 2, 3)]
    if filler:
        near, filler = lax.optimization_barrier((near, filler))
    pieces = near + [hop(piece, 1) for piece in near]
    return (pieces, *filler) if filler else pieces


def scatter_start(give, keep):
    return fold(keep, hop(give, 1))


def scatter_finish(parts):
    return [hop(part, offset_of(place)) for place, part in enumerate(parts, 1)]


def scatter_places(give, keep):
    own, *parts = scatter_start(give, keep)
    return own, scatter_finish(parts)


def dot(a, b):
    return jnp.dot(a, b, preferred_element_type=WIDE)


def under(a, b):
    return lax.dot_general(a, b, (((0,), (0,)), ((), ())), preferred_element_type=WIDE)


def per_device(
    target,
    source,
    cotangent,
    target_lengths,
    source_lengths,
    self_in,
    self_out,
    cross_query,
    cross_kv,
    cross_out,
    mlp_in,
    mlp_out,
    vectors,
    hidden_bias,
):
    rows, width = target.shape[1:]
    here = lax.axis_index("inner")
    core, chip = here & 1, here >> 1
    stream = lax.axis_index("ulys")
    group = lax.axis_index("outer")
    groups = lax.axis_size("outer")
    shares = lax.axis_size("ulys") * groups
    devices = shares * INNER
    span = rows * INNER
    pair = width // INNER
    size = pair // 2
    share = width // devices
    hidden = hidden_bias.shape[0]
    count = vectors.shape[0]
    chips = INNER // 2
    matched = shares * chips == HEADS and 2 * share == size
    target_ends = jnp.cumsum(target_lengths[stream])
    source_ends = jnp.cumsum(source_lengths[stream])
    start = jnp.stack([here, group * span]).astype(jnp.int32)
    cores = jnp.stack([core, 1 - core])
    self_table = jnp.concatenate([start, target_ends, target_ends, cores]).astype(jnp.int32)
    cross_table = jnp.concatenate([start, target_ends, source_ends, cores]).astype(jnp.int32)
    if matched:
        head_at = [(2 * core + n) * (width // shares) + chip * size for n in (0, 1)]
    else:
        head_at = [here * pair + n * size for n in (0, 1)]
    head_table = jnp.stack(head_at).astype(jnp.int32)

    def by_device(value):
        lead = value.shape[:-1]
        if matched:
            split = value.reshape(lead + (2, 2, chips, size))
            value = jnp.moveaxis(split, -2, -4)
        return value.reshape(lead + (INNER, pair))

    def by_column(value):
        lead = value.shape[:-2]
        if matched:
            split = value.reshape(lead + (chips, 2, 2, size))
            value = jnp.moveaxis(split, -4, -2)
        return value.reshape(lead + (width,))

    def cut_columns(*weights):
        whole = jnp.concatenate([w.reshape(share, -1, width) for w in weights], axis=1)
        cut = jnp.transpose(by_device(whole), (2, 0, 1, 3))
        return cut.reshape(INNER, share, -1)

    def exchange(value):
        return lax.all_to_all(value, "inner", 0, 0)

    order = here ^ jnp.array([offset_of(n) for n in range(INNER)], jnp.int32)

    core_table = jnp.stack([2 * core, 2 - 2 * core, core, 1 - core]).astype(jnp.int32)

    def head_rows(weight, found):
        if not matched:
            whole = lax.all_gather(weight, ALL, axis=0, tiled=True)
            return lax.dynamic_slice_in_dim(whole, here * pair, pair, axis=0)
        own, give = found()
        return merge(core_table, own, hop(give, 1))

    def shard_features(pieces):
        whole = jnp.stack(
            [
                piece.reshape(INNER, rows, pair)[jnp.array([n ^ place for n in range(INNER)])]
                for place, piece in enumerate(pieces)
            ]
        ).reshape(INNER, span, pair)
        whole = jnp.transpose(whole, (1, 0, 2)).reshape(span, width)
        cut = []
        for n in range(shares):
            first = (n * INNER + here) * share
            mixed = (first // pair) ^ here
            place = ((mixed >> 1) & 3) | ((mixed & 1) << 2)
            cut.append(
                lax.dynamic_slice_in_dim(whole, place * pair + first % pair, share, axis=1)
            )
        return jnp.concatenate(cut, axis=1)

    def row_grads(parts, pieces, branch):
        if not matched:
            grad = under(shard_features(pieces), jnp.concatenate(branch, axis=0))
            return [grad.astype(LOW).reshape(shares, share, width)]
        return [parts[0], hop(parts[1], 1)]

    def pack_grads(columns, *rows):
        if matched:
            return pack(core_table, columns, *[part for parts in rows for part in parts])
        lined = [
            jnp.transpose(parts[0].reshape(shares, share, INNER, LANES), (0, 2, 1, 3))
            for parts in rows
        ]
        return jnp.concatenate([columns] + [r.reshape(width, LANES) for r in lined], axis=1)

    def lanes_to_columns(got):
        kinds = got.shape[2] // pair
        got = got.reshape(INNER, share, kinds, pair).astype(WIDE)
        return jnp.transpose(got, (1, 2, 0, 3)).reshape(share, kinds * width)

    def lanes_to_rows(packed, start):
        rows = packed[:, start : start + LANES].reshape(INNER, share, LANES).astype(WIDE)
        return jnp.transpose(rows, (1, 0, 2)).reshape(share, width)

    small = jnp.concatenate([jnp.transpose(vectors), hidden_bias.reshape(share, -1)], axis=1)
    extras = small.shape[1]
    small = jnp.pad(small, ((0, 0), (0, LANES - extras)))
    def over(value):
        return lax.all_gather(value, OUTER, axis=0)

    def row_lanes(weight):
        return jnp.transpose(weight.reshape(-1, INNER, LANES), (1, 0, 2))

    raw = over(jnp.concatenate([self_in, self_out, small], axis=1))
    if matched:
        other = exchange(cut_other(cross_kv, cross_query, mlp_in, hidden))
    else:
        first_cut = jnp.transpose(mlp_in.reshape(share, shares, INNER, hidden), (2, 0, 1, 3))
        first_cut = first_cut.reshape(INNER, share, shares * hidden)
        other = [cut_columns(cross_kv, cross_query), first_cut]
        other = exchange(jnp.concatenate(other, axis=2))
    pieces = gather_places(after(target[0], other))
    cross_far = jnp.concatenate([other[:, :, : 3 * pair], row_lanes(cross_out)], axis=2)
    cross_far = over(after(cross_far, raw, *pieces[1:4])).reshape(width, -1)
    first_mine = other[:, :, 3 * pair :].reshape(INNER * share, -1)
    feed_mine = jnp.concatenate([first_mine, mlp_out], axis=0)

    raw = after(raw, *pieces[1:4])
    if matched:
        self_far = exchange(cut_self(raw.reshape(shares * share, -1)))
        self_far = self_far.reshape(INNER, shares, share, -1)
    else:
        cut = by_device(raw[:, :, : 3 * width].reshape(shares, share, 3, width))
        cut = jnp.transpose(cut, (3, 0, 1, 2, 4)).reshape(INNER, shares, share, 3 * pair)
        extra = jnp.broadcast_to(raw[None, :, :, 4 * width :], (INNER, shares, share, LANES))
        self_far = exchange(jnp.concatenate([cut, extra], axis=3))
        self_far = jnp.transpose(self_far, (1, 0, 2, 3)).reshape(1, 1, width, -1)
    q, k, v, h1, params, biases, self_packed, x_all = enter(head_table, rows, pieces, self_far)
    states, q = gather_places(after(source[0], self_far), q)
    raw = after(raw, q)
    feed_packed = over(after(feed_mine, cross_far, q))
    sout_mine = head_rows(self_out, lambda: pick_rows(core_table, 3 * width, raw, width))
    q = after(q, sout_mine)
    h_bias = self_packed.reshape(shares, INNER, share, -1)
    h_bias = h_bias[..., 3 * pair + count : 3 * pair + extras]
    h_bias = lax.dynamic_index_in_dim(h_bias, here, 1, False).reshape(1, -1).astype(WIDE)

    def stream_keys(own):
        return lax.all_gather(own, "outer", axis=0, tiled=True) if groups > 1 else own

    def own_keys(partial):
        if groups == 1:
            return partial
        return lax.psum_scatter(partial, "outer", scatter_dimension=0, tiled=True)

    k, v = stream_keys(k), stream_keys(v)
    att, self_total = attend(self_table, q, k, v, rows, True)
    w_sout, att = gather_places(sout_mine, att)
    cross_far = after(cross_far, att)
    cout_mine = head_rows(cross_out, lambda: pick(core_table, cross_far[:, 3 * pair :]))
    states, ck, cv, cross_packed = pair_heads(rows, states, cross_far, biases)
    att, cout_mine, states, ck, cv, cross_packed = gather_places(
        att, cout_mine, states, ck, cv, cross_packed
    )
    ck, cv = stream_keys(ck), stream_keys(cv)
    y1, h2, y1_all, cq = join_self(att, w_sout, x_all, params, cross_packed, biases)
    w_cout, y1, h2, y1_all, cq = gather_places(
        after(cout_mine, *att[1:4]), y1, h2, y1_all, cq
    )
    catt, cross_total = attend(cross_table, cq, ck, cv, rows, False)
    catt = gather_places(catt)
    y2, h3 = join_cross(catt, w_cout, y1_all, y1, params)
    pull_up, y2, h3 = gather_places(after(cotangent[0], *catt[1:4]), y2, h3)
    active, before_grad, give, keep, h_bias_grad, up = feed(h3, h_bias, feed_packed, pull_up)
    third_own, third_parts = scatter_places(give, keep)
    mlp_grad = feed_grad(active, before_grad, after(h3, third_own), up)
    third_parts, mlp_grad = lax.optimization_barrier((third_parts, mlp_grad))
    mlp_home = lax.psum_scatter(mlp_grad, OUTER, scatter_dimension=0, tiled=True)
    late_grad, cross_branch, late_sums = norm_back(
        4, third_own, third_parts, y2, cotangent[0], params
    )
    cross_all = gather_places(cross_branch)
    give, keep, dcq, dck, dcv, cross_sums, *cross_rows = attend_back(
        cross_table,
        cq,
        ck,
        cv,
        cross_total,
        cout_mine,
        catt[0],
        cross_all,
        rows,
        False,
        (2, cross_packed),
    )
    dck, dcv = own_keys(dck), own_keys(dcv)
    second_own, second_parts = scatter_places(give, keep)
    cross_grad = column_part((after(states, second_own), (dck, dcv)), (h2, (dcq,)))
    side_give, side_keep = side_out(
        after(active, second_own), feed_packed, dck, dcv, cross_packed
    )
    second_parts, cross_grad, side_give, side_keep = lax.optimization_barrier(
        (second_parts, cross_grad, side_give, side_keep)
    )
    cross_rows = row_grads(cross_rows, catt, cross_all)
    middle_grad, self_branch, middle_sums = norm_back(
        2, second_own, second_parts, y1, late_grad, params
    )
    packed_grad = pack_grads(cross_grad, cross_rows)
    side_own, *side_parts = scatter_start(after(side_give, self_branch), side_keep)
    self_all, packed_grad, side_own, side_parts = gather_places(
        self_branch, packed_grad, side_own, side_parts
    )
    self_all, packed_grad, side_parts = lax.optimization_barrier(
        (self_all, packed_grad, side_parts)
    )
    side_parts = scatter_finish(side_parts)
    cross_sum = lax.psum_scatter(packed_grad, OUTER, scatter_dimension=0, tiled=True)
    made = attend_back(
        self_table,
        q,
        k,
        v,
        self_total,
        sout_mine,
        att[0],
        self_all,
        rows,
        True,
        (0, self_packed, x_all) if groups == 1 else None,
    )
    dq, dk, dv, self_sums, *self_rows = made[-6:]
    dk, dv = own_keys(dk), own_keys(dv)
    if groups == 1:
        give, keep, target_sums = made[:3]
    else:
        give, keep, target_sums = spread_self(dq, dk, dv, self_packed, x_all)
    head_sums = jnp.concatenate([self_sums, cross_sums])[:, None]
    head_sums = lax.dynamic_update_slice_in_dim(
        jnp.zeros((4, INNER, pair), WIDE), head_sums, here, 1
    )
    vector_grad = jnp.concatenate(
        [
            target_sums[:2],
            middle_sums[:2],
            late_sums[:2],
            by_column(head_sums)[:2],
            middle_sums[2:3],
            by_column(head_sums)[2:],
            late_sums[2:],
        ]
    )
    vector_part = jnp.transpose(vector_grad.reshape(count, devices, share), (1, 0, 2))
    bias_part = lax.dynamic_update_slice_in_dim(
        jnp.zeros((shares, INNER, hidden), WIDE), h_bias_grad.reshape(shares, 1, hidden), here, 1
    ).reshape(devices, hidden)
    tiny = jnp.concatenate([vector_part.reshape(devices, -1), bias_part], axis=1)
    give, side_parts, mlp_home = lax.optimization_barrier((give, side_parts, mlp_home))
    first_own, *first_parts = scatter_start(give, keep)
    first_parts = scatter_finish(first_parts)
    self_grad = column_part((after(h1, first_own), (dq, dk, dv)))
    self_rows = row_grads((self_rows[0], after(self_rows[1], first_own)), att, self_all)
    packed_grad = pack_grads(self_grad, self_rows)
    self_sum = lax.psum_scatter(packed_grad, OUTER, scatter_dimension=0, tiled=True)
    tiny = lax.all_to_all(after(tiny, packed_grad), ALL, 0, 0, tiled=True)
    first_parts, tiny = lax.optimization_barrier((first_parts, tiny))
    tiny = jnp.sum(tiny, axis=0)
    target_grad, target_low, _ = norm_back(
        0, first_own, first_parts, target[0], middle_grad, params
    )
    side_own, mlp_home, cross_sum = lax.optimization_barrier(
        (side_own, mlp_home, cross_sum, first_parts)
    )[:3]
    layer_out, source_grad = side_sum(side_own, side_parts, y2, params)
    cross_lanes = cross_sum[:, : 3 * pair].reshape(INNER, share, -1)
    first_lanes = mlp_home[:, width:].reshape(INNER, share, -1)
    cross_got = exchange(jnp.concatenate([cross_lanes, first_lanes], axis=2))
    self_got = exchange(self_sum[:, : 3 * pair].reshape(INNER, share, -1))
    if matched:
        cross_home, cout_home, first_home, second_home = home_feed(
            3, hidden, cross_got, cross_sum, mlp_home
        )
        self_home, sout_home = home(self_got, self_sum)
    else:
        cross_home = lanes_to_columns(cross_got[:, :, : 3 * pair])
        first_home = cross_got[:, :, 3 * pair :].reshape(INNER, share, shares, hidden)
        first_home = jnp.transpose(first_home, (1, 2, 0, 3)).reshape(share, -1).astype(WIDE)
        second_home = mlp_home[:, :width].astype(WIDE)
        cout_home = lanes_to_rows(cross_sum, 3 * pair)
        sout_home = lanes_to_rows(self_sum, 3 * pair)
        self_home = lanes_to_columns(self_got)

    return (
        layer_out[None],
        target_low[None],
        source_grad[None],
        self_home,
        sout_home,
        cross_home[:, 2 * width :],
        cross_home[:, : 2 * width],
        cout_home,
        first_home,
        second_home,
        tiny[: count * share].reshape(count, share),
        tiny[count * share :],
    )


def solution(mesh):
    streams, blocks = mesh.devices.shape
    grid = mesh.devices.reshape(streams, blocks // INNER, INNER)
    inner_mesh = Mesh(grid, ALL)
    rows = P("ulys", ("outer", "inner"), None)
    matrix = P(ALL, None)
    row_vectors = P(None, ALL)
    in_specs = (rows,) * 3 + (P(), P()) + (matrix,) * 7 + (row_vectors, P(ALL))
    out_specs = (rows,) * 3 + (matrix,) * 7 + (row_vectors, P(ALL))
    return jax.shard_map(
        per_device, mesh=inner_mesh, in_specs=in_specs, out_specs=out_specs, check_vma=False
    )
```

```python
import functools

import jax
import jax.numpy as jnp
from jax import lax
from jax.experimental import pallas as pl
from jax.experimental.pallas import tpu as pltpu
from jax.sharding import Mesh
from jax.sharding import PartitionSpec as P

HEADS = 16
LOW = jnp.bfloat16
WIDE = jnp.float32
INNER = 8
STEP = 256
WIDE_STEP = 512
LANES = 128
OUTER = ("ulys", "outer")
ALL = ("ulys", "outer", "inner")


def offset_of(place):
    return ((place & 3) << 1) | (place >> 2)


def dot_t(a, b):
    return lax.dot_general(a, b, (((1,), (1,)), ((), ())), preferred_element_type=WIDE)


def dot_n(a, b):
    return lax.dot_general(a, b, (((1,), (0,)), ((), ())), preferred_element_type=WIDE)


def dot_c(a, b):
    return lax.dot_general(a, b, (((0,), (0,)), ((), ())), preferred_element_type=WIDE)


def seg_of(position, table, first):
    count = jnp.zeros_like(position)
    for n in range(3):
        count = count + (table[first + n] <= position).astype(jnp.int32)
    return count


def iota(shape, axis):
    return lax.broadcasted_iota(jnp.int32, shape, axis)


def to_order(table, source, target, rows, factor=None):
    span = rows * INNER
    for chunk in range(source.shape[0] // span):
        for place in range(INNER):
            at = pl.multiple_of((table[0] ^ offset_of(place)) * rows, rows) + chunk * span
            value = source[pl.ds(chunk * span + place * rows, rows), :]
            if factor is not None:
                value = value * factor
            target[pl.ds(at, rows), :] = value


def from_order(table, source, target, rows):
    span = rows * INNER
    for chunk in range(target.shape[0] // span):
        for place in range(INNER):
            at = pl.multiple_of((table[0] ^ offset_of(place)) * rows, rows) + chunk * span
            target[pl.ds(chunk * span + place * rows, rows), :] = source[pl.ds(at, rows), :].astype(
                target.dtype
            )


def half_lanes(value, head, size):
    lane = iota(value.shape, 1)
    keep = (lane >= head * size) & (lane < (head + 1) * size)
    return jnp.where(keep, value, jnp.zeros_like(value))


def attend_kernel(causal, rows, size, table, q, k, v, out, log_total, qs, ks, vs, ordered):
    span, keys = q.shape[0], k.shape[0]
    chunks = keys // span
    to_order(table, q, qs, rows, jnp.asarray(size**-0.5, LOW))
    to_order(table, k, ks, rows)
    to_order(table, v, vs, rows)
    for step in range(span // WIDE_STEP):
        lo = step * WIDE_STEP
        queries = qs[lo : lo + WIDE_STEP, :]
        q_at = table[1] + lo + iota((WIDE_STEP, 1), 0)
        q_seg = seg_of(q_at, table, 2)
        count = lo + WIDE_STEP if causal and chunks == 1 else span

        def mask(start):
            k_at = start + iota((1, count), 1)
            allowed = q_seg == seg_of(k_at, table, 5)
            if causal:
                allowed = allowed & (k_at <= q_at)
            return allowed

        def scores(head, start, allowed):
            raw = dot_t(queries, half_lanes(ks[pl.ds(start, count), :], head, size))
            return jnp.where(allowed, raw, -1e30)

        parts = []
        allowed = mask(0) if chunks == 1 else None
        for head in range(2):
            if chunks == 1:
                raw = scores(head, 0, allowed)
                top = jnp.max(raw, axis=1, keepdims=True)
                weight = jnp.exp(raw - top)
                total = jnp.sum(weight, axis=1, keepdims=True)
                running = dot_n(weight.astype(LOW), vs[:count, :])
            else:

                def absorb(chunk, carry, head=head):
                    top, total, running = carry
                    start = pl.multiple_of(chunk * span, span)
                    raw = scores(head, start, mask(start))
                    new_top = jnp.maximum(top, jnp.max(raw, axis=1, keepdims=True))
                    weight = jnp.exp(raw - new_top)
                    fade = jnp.exp(top - new_top)
                    total = total * fade + jnp.sum(weight, axis=1, keepdims=True)
                    running = running * fade + dot_n(weight.astype(LOW), vs[pl.ds(start, span), :])
                    return new_top, total, running

                top, total, running = lax.fori_loop(
                    0,
                    chunks,
                    absorb,
                    (
                        jnp.full((WIDE_STEP, 1), -1e30, WIDE),
                        jnp.zeros((WIDE_STEP, 1), WIDE),
                        jnp.zeros((WIDE_STEP, 2 * size), WIDE),
                    ),
                )
            parts.append(running / total)
            logs = jnp.broadcast_to(top + jnp.log(total), (WIDE_STEP, 2 * size))
            log_total[head : head + 1, lo : lo + WIDE_STEP] = jnp.transpose(logs)[0:1, :]
        lane = iota((WIDE_STEP, 2 * size), 1)
        ordered[lo : lo + WIDE_STEP, :] = jnp.where(lane < size, parts[0], parts[1])
    from_order(table, ordered, out, rows)


def split_rows(table, first, own, branch, row, keep, give):
    row[...] = dot_c(own[...], branch[...]).astype(LOW)
    share = keep.shape[1]
    for core, out in ((table[first], keep), (table[first + 1], give)):
        for n in range(2):
            at = pl.multiple_of((2 * n + core) * share, share)
            out[n] = row[pl.ds(at, share), :]


def attend_back_kernel(causal, rows, size, start, lined, table, q, k, v, log_total, weight, *refs):
    own = refs[0] if lined else None
    refs = refs[1:] if lined else refs
    pieces, refs = refs[:INNER], refs[INNER:]
    late = []
    if start is not None:
        late, refs = [refs[0]], refs[1:]
        if start == 0:
            late, refs = late + [refs[0]], refs[1:]
            give, keep, norm_sums, refs = *refs[:3], refs[3:]
        else:
            give, keep, refs = *refs[:2], refs[2:]
    dq, dk, dv, sums, refs = *refs[:4], refs[4:]
    if lined:
        row_keep, row_give, refs = *refs[:2], refs[2:]
    qs, ks, vs, ups, dqs, dks, dvs, branch, row, marks, *near = refs
    copies = pull(pieces, 0, branch, marks)
    loads = []
    for n, source in enumerate(late):
        loads.append(pltpu.make_async_copy(source, near[n], near[-1].at[n]))
    for load in loads:
        load.start()
    span, keys = q.shape[0], k.shape[0]
    chunks = keys // span
    scale = size**-0.5
    to_order(table, q, qs, rows, jnp.asarray(scale, LOW))
    to_order(table, k, ks, rows)
    to_order(table, v, vs, rows)
    finish(copies)
    upstream = dot_t(branch[...], weight[...]).astype(LOW)
    for place in range(INNER):
        at = pl.multiple_of((table[0] ^ offset_of(place)) * rows, rows)
        ups[pl.ds(at, rows), :] = upstream[place * rows : (place + 1) * rows, :]
    if lined:
        split_rows(table, 8, own, branch, row, row_keep, row_give)
    dks[...] = jnp.zeros_like(dks)
    dvs[...] = jnp.zeros_like(dvs)
    for step in range(span // STEP):
        lo = step * STEP
        queries = qs[lo : lo + STEP, :]
        upstream = ups[lo : lo + STEP, :]
        q_at = table[1] + lo + iota((1, STEP), 1)
        q_seg = seg_of(q_at, table, 2)
        count = lo + STEP if causal and chunks == 1 else span
        q_pair = [half_lanes(queries, head, size) for head in range(2)]
        up_pair = [half_lanes(upstream, head, size) for head in range(2)]
        logs = [log_total[head : head + 1, lo : lo + STEP] for head in range(2)]

        def make(start):
            k_at = start + iota((count, 1), 0)
            allowed = q_seg == seg_of(k_at, table, 5)
            if causal:
                allowed = allowed & (k_at <= q_at)
            keys_here = ks[pl.ds(start, count), :]
            k_pair = [half_lanes(keys_here, head, size) for head in range(2)]
            probs, lean = [], []
            for head in range(2):
                raw = dot_t(k_pair[head], queries)
                probs.append(jnp.exp(jnp.where(allowed, raw - logs[head], -1e30)))
                slope = dot_t(vs[pl.ds(start, count), :], up_pair[head])
                lean.append(probs[head] * slope)
            return k_pair, probs, lean

        def settle(start, delta, made):
            k_pair, probs, lean = made
            push = [(lean[n] - probs[n] * delta[n]).astype(LOW) for n in range(2)]
            low = [probs[n].astype(LOW) for n in range(2)]
            at = pl.ds(start, count)
            dvs[at, :] += dot_n(jnp.concatenate(low, axis=1), jnp.concatenate(up_pair, axis=0))
            dks[at, :] += dot_n(jnp.concatenate(push, axis=1), jnp.concatenate(q_pair, axis=0))
            return dot_c(jnp.concatenate(push, axis=0), jnp.concatenate(k_pair, axis=0))

        def slopes(made):
            return [jnp.sum(made[2][n], axis=0, keepdims=True) for n in range(2)]

        if chunks == 1:
            made = make(0)
            total_dq = settle(0, slopes(made), made)
        else:

            def measure(chunk, delta):
                more = slopes(make(pl.multiple_of(chunk * span, span)))
                return [delta[n] + more[n] for n in range(2)]

            delta = lax.fori_loop(0, chunks, measure, [jnp.zeros((1, STEP), WIDE)] * 2)

            def absorb(chunk, running, delta=delta):
                start = pl.multiple_of(chunk * span, span)
                return running + settle(start, delta, make(start))

            total_dq = lax.fori_loop(0, chunks, absorb, jnp.zeros((STEP, 2 * size), WIDE))
        dqs[lo : lo + STEP, :] = total_dq * scale
    from_order(table, dqs, dq, rows)
    from_order(table, dks, dk, rows)
    from_order(table, dvs, dv, rows)
    finish(loads)
    if start is not None:
        packed = near[0]
        x_all = near[1] if start == 0 else None
        kinds = 3 if start == 0 else 1
        back = packed[:, start * LANES : (start + kinds) * LANES]
        first = second = None
        for at, out in ((span // 2, give), (0, keep)):
            at = slice(at, at + span // 2)
            left = [part[at, :] for part in (dq, dk, dv)[:kinds]]
            left = left[0] if kinds == 1 else jnp.concatenate(left, axis=1)
            slope = dot_t(left, back)
            out[...] = slope.astype(out.dtype)
            if start == 0:
                centred, inverse = centre(x_all[at, :].astype(WIDE))
                gain = jnp.sum(slope * (centred * inverse), axis=0, keepdims=True)
                shift = jnp.sum(slope, axis=0, keepdims=True)
                first = gain if first is None else first + gain
                second = shift if second is None else second + shift
        if start == 0:
            norm_sums[0:1, :] = first
            norm_sums[1:2, :] = second
    sums[0:1, :] = jnp.sum(dqs[...].astype(LOW).astype(WIDE), axis=0, keepdims=True)
    sums[1:2, :] = jnp.sum(dvs[...].astype(LOW).astype(WIDE), axis=0, keepdims=True)


HBM = pl.BlockSpec(memory_space=pl.ANY)


def room(megabytes):
    return pltpu.CompilerParams(vmem_limit_bytes=megabytes * 2**20)


def pull(pieces, index, target, marks):
    rows = target.shape[0] // INNER
    copies = []
    for place in range(INNER):
        source = pieces[place].at[pl.ds(index * rows, rows), :]
        aim = target.at[pl.ds(place * rows, rows), :]
        copies.append(pltpu.make_async_copy(source, aim, marks.at[place]))
    for copy in copies:
        copy.start()
    return copies


def finish(copies):
    for copy in copies:
        copy.wait()


def cost(micros):
    return pl.CostEstimate(
        flops=int(micros * 1.1e9), bytes_accessed=int(micros * 3.5e6), transcendentals=0
    )


SMEM = pl.BlockSpec(memory_space=pltpu.SMEM)
VMEM = pl.BlockSpec(memory_space=pltpu.VMEM)


def attend(table, q, k, v, rows, causal):
    span, pair = q.shape
    keys = k.shape[0]
    return pl.pallas_call(
        functools.partial(attend_kernel, causal, rows, pair // 2),
        out_shape=(
            jax.ShapeDtypeStruct((span, pair), LOW),
            jax.ShapeDtypeStruct((2, span), WIDE),
        ),
        in_specs=[SMEM, VMEM, VMEM, VMEM],
        out_specs=(VMEM, VMEM),
        scratch_shapes=[
            pltpu.VMEM((span, pair), LOW),
            pltpu.VMEM((keys, pair), LOW),
            pltpu.VMEM((keys, pair), LOW),
            pltpu.VMEM((span, pair), WIDE),
        ],
        compiler_params=room(60),
        cost_estimate=cost(6),
    )(table, q, k, v)


def attend_back(table, q, k, v, log_total, weight, own, pieces, rows, causal, back=None):
    span, pair = q.shape
    keys = k.shape[0]
    width = weight.shape[1]
    part = jax.ShapeDtypeStruct((2, pair // 4, width), LOW)
    lined = [] if own is None else [own]
    spread_shape = (
        jax.ShapeDtypeStruct((span // 2, width), LOW),
        jax.ShapeDtypeStruct((span // 2, width), WIDE),
    )
    start, *extra = back if back else (None,)
    if start == 0:
        spread_shape += (jax.ShapeDtypeStruct((2, width), WIDE),)
    return pl.pallas_call(
        functools.partial(attend_back_kernel, causal, rows, pair // 2, start, bool(lined)),
        out_shape=(spread_shape if back else ())
        + (
            jax.ShapeDtypeStruct((span, pair), LOW),
            jax.ShapeDtypeStruct((keys, pair), LOW),
            jax.ShapeDtypeStruct((keys, pair), LOW),
            jax.ShapeDtypeStruct((2, pair), WIDE),
        )
        + ((part, part) if lined else ()),
        in_specs=[SMEM] + [VMEM] * (5 + len(lined)) + [HBM] * (INNER + len(extra)),
        out_specs=(VMEM,) * (4 + 2 * len(lined) + (len(spread_shape) if back else 0)),
        scratch_shapes=[
            pltpu.VMEM((span, pair), LOW),
            pltpu.VMEM((keys, pair), LOW),
            pltpu.VMEM((keys, pair), LOW),
            pltpu.VMEM((span, pair), LOW),
            pltpu.VMEM((span, pair), WIDE),
            pltpu.VMEM((keys, pair), WIDE),
            pltpu.VMEM((keys, pair), WIDE),
            pltpu.VMEM((span, width), LOW),
            pltpu.VMEM((pair, width), LOW),
            pltpu.SemaphoreType.DMA((INNER,)),
        ]
        + [pltpu.VMEM(value.shape, LOW) for value in extra]
        + ([pltpu.SemaphoreType.DMA((2,))] if extra else []),
        compiler_params=room(60),
        cost_estimate=cost(10),
    )(table, q, k, v, log_total, weight, *lined, *pieces, *extra)


def centre(value):
    center = jnp.mean(value, axis=-1, keepdims=True)
    centred = value - center
    spread = jnp.mean(centred * centred, axis=-1, keepdims=True)
    return centred, lax.rsqrt(spread + 1e-05)


def norm_of(value, gain, shift):
    centred, inverse = centre(value)
    return (centred * inverse * gain + shift).astype(LOW)


def enter_kernel(kinds, table, far, *refs):
    pieces, refs = refs[:INNER], refs[INNER:]
    q, k, v, h, params, biases, packed, x_all, blocks, marks, mark = refs
    loads = []
    for place in range(far.shape[0]):
        loads.append(pltpu.make_async_copy(far.at[place], blocks.at[:, place], mark.at[place]))
    for load in loads:
        load.start()
    copies = pull(pieces, 0, x_all, marks)
    finish(loads)
    packed[...] = blocks[...].reshape(packed.shape)
    edge = kinds * LANES
    extra = packed[:, edge : edge + LANES].astype(WIDE)
    params[...] = jnp.transpose(extra)[:16, :]
    size = LANES // 2
    mine = [packed[pl.ds(pl.multiple_of(table[n], 16), size), edge : edge + LANES] for n in (0, 1)]
    biases[...] = jnp.transpose(jnp.concatenate(mine, axis=0).astype(WIDE))[:16, :]
    finish(copies)
    half = x_all.shape[0] // 2
    for part in range(2):
        at = slice(part * half, (part + 1) * half)
        low = norm_of(x_all[at, :].astype(WIDE), params[0:1, :], params[1:2, :])
        h[at, :] = low
        made = dot_n(low, packed[:, :edge])
        q[at, :] = (made[:, :LANES] + biases[6:7, :]).astype(LOW)
        k[at, :] = made[:, LANES : 2 * LANES].astype(LOW)
        v[at, :] = (made[:, 2 * LANES :] + biases[7:8, :]).astype(LOW)


def enter(table, rows, pieces, packed):
    width = pieces[0].shape[1]
    span = rows * INNER
    heads = jax.ShapeDtypeStruct((span, LANES), LOW)
    return pl.pallas_call(
        functools.partial(enter_kernel, 3),
        out_shape=(
            heads,
            heads,
            heads,
            jax.ShapeDtypeStruct((span, width), LOW),
            jax.ShapeDtypeStruct((16, width), WIDE),
            jax.ShapeDtypeStruct((16, LANES), WIDE),
            jax.ShapeDtypeStruct((width, 4 * LANES), LOW),
            jax.ShapeDtypeStruct((span, width), LOW),
        ),
        in_specs=[SMEM] + [HBM] * (1 + INNER),
        out_specs=(VMEM,) * 8,
        scratch_shapes=[
            pltpu.VMEM((packed.shape[1], packed.shape[0]) + packed.shape[2:], LOW),
            pltpu.SemaphoreType.DMA((INNER,)),
            pltpu.SemaphoreType.DMA((packed.shape[0],)),
        ],
        compiler_params=room(60),
        cost_estimate=cost(4),
    )(table, packed, *pieces)


def join_kernel(vector, first, query, *refs):
    pieces, weights, refs = refs[:INNER], refs[INNER : 2 * INNER], refs[2 * INNER :]
    if query is None:
        far, base_own, params, y_own, h, weight, left, heads, marks, base, base_mark = refs
    else:
        far, params, packed, biases, y_own, h, y_all, cq, weight, left, heads, marks, base, base_mark = refs
    span = left.shape[0]
    block = span // INNER
    loads = pull(weights, 0, weight, marks.at[1])
    base_load = pltpu.make_async_copy(far, base, base_mark)
    copies = []
    for place in range(INNER):
        copies.append(pltpu.make_async_copy(pieces[place], heads.at[place], marks.at[0, place]))
    for copy in copies:
        copy.start()
    base_load.start()
    finish(copies + loads + [base_load])
    parts = INNER // 2
    for part in range(parts):
        at = slice(part * 2 * block, (part + 1) * 2 * block)
        for n in range(2 * part, 2 * part + 2):
            for place in range(INNER):
                first_row = (n ^ place) * block
                left[n * block : (n + 1) * block, place * LANES : (place + 1) * LANES] = heads[
                    place, first_row : first_row + block, :
                ]
        value = base[at, :].astype(WIDE)
        if query is None and part == 0:
            value = jnp.concatenate([base_own[...], value[block:, :]], axis=0)
        y = value + dot_n(left[at, :], weight[...]) + params[vector : vector + 1, :]
        if part == 0:
            y_own[...] = y[:block, :]
        low = norm_of(y, params[first : first + 1, :], params[first + 1 : first + 2, :])
        h[at, :] = low
        if query is not None:
            y_all[at, :] = y.astype(LOW)
            made = dot_n(low, packed[:, query * LANES : (query + 1) * LANES])
            cq[at, :] = (made + biases[9:10, :]).astype(LOW)


def join_self(pieces, weights, base, params, packed, biases):
    span, width = base.shape
    return pl.pallas_call(
        functools.partial(join_kernel, 8, 2, 2),
        out_shape=(
            jax.ShapeDtypeStruct((span // INNER, width), WIDE),
            jax.ShapeDtypeStruct((span, width), LOW),
            jax.ShapeDtypeStruct((span, width), LOW),
            jax.ShapeDtypeStruct((span, LANES), LOW),
        ),
        in_specs=[HBM] * (2 * INNER + 1) + [VMEM] * 3,
        out_specs=(VMEM,) * 4,
        scratch_shapes=[
            pltpu.VMEM((width, width), LOW),
            pltpu.VMEM((span, width), LOW),
            pltpu.VMEM((INNER, span, LANES), LOW),
            pltpu.SemaphoreType.DMA((2, INNER)),
            pltpu.VMEM((span, width), LOW),
            pltpu.SemaphoreType.DMA,
        ],
        compiler_params=room(60),
        cost_estimate=cost(6),
    )(*pieces, *weights, base, params, packed, biases)


def join_cross(pieces, weights, base, base_own, params):
    span, width = base.shape
    return pl.pallas_call(
        functools.partial(join_kernel, 11, 4, None),
        out_shape=(
            jax.ShapeDtypeStruct((span // INNER, width), WIDE),
            jax.ShapeDtypeStruct((span, width), LOW),
        ),
        in_specs=[HBM] * (2 * INNER + 1) + [VMEM] * 2,
        out_specs=(VMEM,) * 2,
        scratch_shapes=[
            pltpu.VMEM((width, width), LOW),
            pltpu.VMEM((span, width), LOW),
            pltpu.VMEM((INNER, span, LANES), LOW),
            pltpu.SemaphoreType.DMA((2, INNER)),
            pltpu.VMEM((span, width), LOW),
            pltpu.SemaphoreType.DMA,
        ],
        compiler_params=room(60),
        cost_estimate=cost(5),
    )(*pieces, *weights, base, base_own, params)


def load_rows(packed, start, target, marks):
    shares = packed.shape[0]
    rows = target.shape[0] // shares
    copies = []
    for n in range(shares):
        source = packed.at[n, pl.ds(start, rows), :]
        aim = target.at[pl.ds(n * rows, rows), :]
        copies.append(pltpu.make_async_copy(source, aim, marks.at[n]))
    for copy in copies:
        copy.start()
    return copies


def feed_kernel(h, bias, packed, *refs):
    pieces = refs[:INNER]
    act, slope, give, keep, bias_grad, up, first, second, marks, weight_marks = refs[INNER:]
    span, width = up.shape
    hidden = second.shape[0]
    loads = load_rows(packed, 0, first, weight_marks.at[0])
    copies = load_rows(packed, width // packed.shape[0], second, weight_marks.at[1])
    copies += pull(pieces, 0, up, marks)
    finish(loads)
    step = 256
    inner = (2.0 / 3.141592653589793) ** 0.5
    for n in range(hidden // step):
        at = slice(n * step, (n + 1) * step)
        pre = dot_n(h[...], first[:, at]) + bias[:, at]
        square = pre * pre
        bend = jnp.tanh(pre * (inner + (inner * 0.044715) * square))
        half = 0.5 * bend + 0.5
        act[:, at] = (pre * half).astype(LOW)
        if n == 0:
            finish(copies)
        rise = half + 0.5 * pre * (1.0 - bend * bend) * (inner + (3 * inner * 0.044715) * square)
        low = (dot_t(up[...], second[at, :]) * rise).astype(LOW)
        slope[:, at] = low
        bias_grad[:, at] = jnp.sum(low.astype(WIDE), axis=0, keepdims=True)
    give[...] = dot_t(slope[span // 2 :, :], first[...]).astype(LOW)
    keep[...] = dot_t(slope[: span // 2, :], first[...])


def feed(h, bias, packed, pieces):
    span, width = h.shape
    hidden = bias.shape[1]
    shares = packed.shape[0]
    return pl.pallas_call(
        feed_kernel,
        out_shape=(
            jax.ShapeDtypeStruct((span, hidden), LOW),
            jax.ShapeDtypeStruct((span, hidden), LOW),
            jax.ShapeDtypeStruct((span // 2, width), LOW),
            jax.ShapeDtypeStruct((span // 2, width), WIDE),
            jax.ShapeDtypeStruct((1, hidden), WIDE),
            jax.ShapeDtypeStruct((span, width), LOW),
        ),
        in_specs=[VMEM] * 2 + [HBM] * (1 + INNER),
        out_specs=(VMEM,) * 6,
        scratch_shapes=[
            pltpu.VMEM((width, hidden), LOW),
            pltpu.VMEM((hidden, width), LOW),
            pltpu.SemaphoreType.DMA((INNER,)),
            pltpu.SemaphoreType.DMA((2, shares)),
        ],
        compiler_params=room(44),
        cost_estimate=cost(13),
    )(h, bias, packed, *pieces)


def side_kernel(act, packed, dk, dv, pair_weight, give, keep, second, marks):
    copies = load_rows(packed, second.shape[1] // packed.shape[0], second, marks)
    half, width = keep.shape[0], second.shape[1]
    weight = pair_weight[:, : 2 * LANES]
    spans = ((half, give), (0, keep))
    for at, out in spans:
        left = jnp.concatenate([dk[at : at + half, :], dv[at : at + half, :]], axis=1)
        out[:, width:] = dot_t(left, weight).astype(out.dtype)
    finish(copies)
    for at, out in spans:
        out[:, :width] = dot_n(act[at : at + half, :], second[...]).astype(out.dtype)


def side_out(act, packed, dk, dv, pair_weight):
    span, hidden = act.shape
    shares, _, width = packed.shape
    return pl.pallas_call(
        side_kernel,
        out_shape=(
            jax.ShapeDtypeStruct((span // 2, 2 * width), LOW),
            jax.ShapeDtypeStruct((span // 2, 2 * width), WIDE),
        ),
        in_specs=[VMEM, HBM] + [VMEM] * 3,
        out_specs=(VMEM,) * 2,
        scratch_shapes=[
            pltpu.VMEM((hidden, width), LOW),
            pltpu.SemaphoreType.DMA((shares,)),
        ],
        compiler_params=room(24),
        cost_estimate=cost(4),
    )(act, packed, dk, dv, pair_weight)


def side_sum_kernel(own, one, two, three, y, params, layer, source):
    total = own[...] + one[...].astype(WIDE) + two[...].astype(WIDE) + three[...].astype(WIDE)
    width = y.shape[1]
    layer[...] = (y[...] + total[:, :width] + params[12:13, :]).astype(LOW)
    source[...] = total[:, width:].astype(LOW)


def side_sum(own, parts, y, params):
    out = jax.ShapeDtypeStruct(y.shape, LOW)
    return pl.pallas_call(
        side_sum_kernel,
        out_shape=(out, out),
        in_specs=[VMEM] * 6,
        out_specs=(VMEM,) * 2,
        compiler_params=room(60),
        cost_estimate=cost(1),
    )(own, *parts, y, params)


def feed_grad_kernel(act, slope, h, up, out):
    width = up.shape[1]
    step = 256
    for n in range(width // step):
        at = slice(n * step, (n + 1) * step)
        out[at, width:] = dot_c(h[:, at], slope[...]).astype(LOW)
    for n in range(act.shape[1] // step):
        at = slice(n * step, (n + 1) * step)
        out[at, :width] = dot_c(act[:, at], up[...]).astype(LOW)


def feed_grad(act, slope, h, up):
    width = h.shape[1]
    hidden = act.shape[1]
    return pl.pallas_call(
        feed_grad_kernel,
        out_shape=jax.ShapeDtypeStruct((width, width + hidden), LOW),
        in_specs=[VMEM] * 4,
        out_specs=VMEM,
        compiler_params=room(40),
        cost_estimate=cost(6),
    )(act, slope, h, up)


def fold_kernel(keep, took, own, one, two, three):
    rows = own.shape[0]
    own[...] = keep[:rows, :] + took[:rows, :].astype(WIDE)
    for n, part in enumerate((one, two, three), 1):
        at = slice(n * rows, (n + 1) * rows)
        part[...] = (keep[at, :] + took[at, :].astype(WIDE)).astype(LOW)


def fold(keep, took):
    half, width = keep.shape
    part = jax.ShapeDtypeStruct((half // 4, width), LOW)
    return pl.pallas_call(
        fold_kernel,
        out_shape=(jax.ShapeDtypeStruct((half // 4, width), WIDE), part, part, part),
        in_specs=[VMEM] * 2,
        out_specs=(VMEM,) * 4,
        compiler_params=room(16),
        cost_estimate=cost(1),
    )(keep, took)


def norm_back_kernel(first, own, one, two, three, value, base, params, grad, low, sums):
    slope = own[...] + one[...].astype(WIDE) + two[...].astype(WIDE) + three[...].astype(WIDE)
    centred, inverse = centre(value[...].astype(WIDE))
    unit = centred * inverse
    lean = slope * params[first : first + 1, :]
    flat = jnp.mean(lean, axis=-1, keepdims=True)
    tilt = jnp.mean(lean * unit, axis=-1, keepdims=True)
    total = base[...].astype(WIDE) + inverse * (lean - flat - unit * tilt)
    grad[...] = total
    cut = total.astype(LOW)
    low[...] = cut
    sums[0:1, :] = jnp.sum(slope * unit, axis=0, keepdims=True)
    sums[1:2, :] = jnp.sum(slope, axis=0, keepdims=True)
    sums[2:3, :] = jnp.sum(cut.astype(WIDE), axis=0, keepdims=True)
    sums[3:4, :] = jnp.sum(base[...].astype(WIDE), axis=0, keepdims=True)


def norm_back(first, own, parts, value, base, params):
    rows, width = own.shape
    return pl.pallas_call(
        functools.partial(norm_back_kernel, first),
        out_shape=(
            jax.ShapeDtypeStruct((rows, width), WIDE),
            jax.ShapeDtypeStruct((rows, width), LOW),
            jax.ShapeDtypeStruct((4, width), WIDE),
        ),
        in_specs=[VMEM] * 7,
        out_specs=(VMEM,) * 3,
        compiler_params=room(16),
        cost_estimate=cost(2),
    )(own, *parts, value, base, params)


def pair_kernel(biases, far, *refs):
    pieces, (states, k, v, packed, marks, mark) = refs[:INNER], refs[INNER:]
    load = pltpu.make_async_copy(far.at[:, pl.ds(0, packed.shape[1])], packed, mark)
    load.start()
    finish(pull(pieces, 0, states, marks) + [load])
    made = dot_n(states[...], packed[:, : 2 * LANES])
    k[...] = made[:, :LANES].astype(LOW)
    v[...] = (made[:, LANES:] + biases[10:11, :]).astype(LOW)


def pair_heads(rows, pieces, packed, biases):
    width = pieces[0].shape[1]
    span = rows * INNER
    heads = jax.ShapeDtypeStruct((span, LANES), LOW)
    return pl.pallas_call(
        pair_kernel,
        out_shape=(
            jax.ShapeDtypeStruct((span, width), LOW),
            heads,
            heads,
            jax.ShapeDtypeStruct((width, 3 * LANES), LOW),
        ),
        in_specs=[VMEM] + [HBM] * (1 + INNER),
        out_specs=(VMEM,) * 4,
        scratch_shapes=[pltpu.SemaphoreType.DMA((INNER,)), pltpu.SemaphoreType.DMA],
        compiler_params=room(60),
        cost_estimate=cost(3),
    )(biases, packed, *pieces)


def spread_self_kernel(dq, dk, dv, packed, x_all, give, keep, sums):
    half = x_all.shape[0] // 2
    weight = packed[:, : 3 * LANES]
    first = second = None
    for part, out in ((1, give), (0, keep)):
        at = slice(part * half, (part + 1) * half)
        left = jnp.concatenate([dq[at, :], dk[at, :], dv[at, :]], axis=1)
        slope = dot_t(left, weight)
        out[...] = slope.astype(out.dtype)
        centred, inverse = centre(x_all[at, :].astype(WIDE))
        gain = jnp.sum(slope * (centred * inverse), axis=0, keepdims=True)
        shift = jnp.sum(slope, axis=0, keepdims=True)
        first = gain if first is None else first + gain
        second = shift if second is None else second + shift
    sums[0:1, :] = first
    sums[1:2, :] = second


def spread_self(dq, dk, dv, packed, x_all):
    span, width = x_all.shape
    return pl.pallas_call(
        spread_self_kernel,
        out_shape=(
            jax.ShapeDtypeStruct((span // 2, width), LOW),
            jax.ShapeDtypeStruct((span // 2, width), WIDE),
            jax.ShapeDtypeStruct((2, width), WIDE),
        ),
        in_specs=[VMEM] * 5,
        out_specs=(VMEM,) * 3,
        compiler_params=room(32),
        cost_estimate=cost(4),
    )(dq, dk, dv, packed, x_all)


def spread_columns(got, kinds, out):
    size = LANES // 2
    for kind in range(kinds):
        heads = {}
        for place in range(INNER):
            for n in (0, 1):
                at = kind * LANES + n * size
                number = (2 * (place & 1) + n) * (INNER // 2) + (place >> 1)
                heads[number] = got[place][:, at : at + size].astype(WIDE)
        for number in range(0, 2 * INNER, 2):
            at = kind * INNER * LANES + number * size
            both = jnp.concatenate([heads[number], heads[number + 1]], axis=1)
            out[:, at : at + LANES] = both


def spread_rows(packed, start, out):
    share = out.shape[0]
    for place in range(INNER):
        block = packed[place * share : (place + 1) * share, start : start + LANES]
        out[:, place * LANES : (place + 1) * LANES] = block.astype(WIDE)


def home_kernel(kinds, got, packed, columns, rows):
    spread_columns(got, kinds, columns)
    spread_rows(packed, kinds * LANES, rows)


def home(got, packed):
    share, lanes = got.shape[1:]
    return pl.pallas_call(
        functools.partial(home_kernel, lanes // LANES),
        out_shape=(
            jax.ShapeDtypeStruct((share, lanes * INNER), WIDE),
            jax.ShapeDtypeStruct((share, LANES * INNER), WIDE),
        ),
        in_specs=[VMEM] * 2,
        out_specs=(VMEM,) * 2,
        compiler_params=room(16),
        cost_estimate=cost(2),
    )(got, packed)


def home_feed_kernel(kinds, hidden, got, packed, feed_sum, *outs):
    columns, rows, first, second = outs
    spread_columns(got, kinds, columns)
    spread_rows(packed, kinds * LANES, rows)
    width = second.shape[1]
    second[...] = feed_sum[:, :width].astype(WIDE)
    lanes = got.shape[2] - kinds * LANES
    for n in range(lanes // hidden):
        for place in range(INNER):
            at = (n * INNER + place) * hidden
            start = kinds * LANES + n * hidden
            first[:, at : at + hidden] = got[place, :, start : start + hidden].astype(WIDE)


def home_feed(kinds, hidden, got, packed, feed_sum):
    share, lanes = got.shape[1:]
    rows = jax.ShapeDtypeStruct((share, LANES * INNER), WIDE)
    return pl.pallas_call(
        functools.partial(home_feed_kernel, kinds, hidden),
        out_shape=(
            jax.ShapeDtypeStruct((share, kinds * LANES * INNER), WIDE),
            rows,
            jax.ShapeDtypeStruct((share, (lanes - kinds * LANES) * INNER), WIDE),
            jax.ShapeDtypeStruct((feed_sum.shape[0], LANES * INNER), WIDE),
        ),
        in_specs=[VMEM] * 3,
        out_specs=(VMEM,) * 4,
        compiler_params=room(24),
        cost_estimate=cost(3),
    )(got, packed, feed_sum)


def column_part_kernel(kinds, *refs):
    count = len(kinds)
    lefts, rights, column = refs[:count], refs[count:-1], refs[-1]
    at = first = 0
    for left, kind in zip(lefts, kinds):
        right = [value[...] for value in rights[first : first + kind]]
        right = right[0] if kind == 1 else jnp.concatenate(right, axis=1)
        lanes = kind * LANES
        column[:, at : at + lanes] = dot_c(left[...], right).astype(LOW)
        at, first = at + lanes, first + kind


def column_part(*pairs):
    width = pairs[0][0].shape[1]
    kinds = tuple(len(rights) for _, rights in pairs)
    lefts = [left for left, _ in pairs]
    rights = [value for _, values in pairs for value in values]
    return pl.pallas_call(
        functools.partial(column_part_kernel, kinds),
        out_shape=jax.ShapeDtypeStruct((width, LANES * sum(kinds)), LOW),
        in_specs=[VMEM] * (len(lefts) + len(rights)),
        out_specs=VMEM,
        compiler_params=room(24),
        cost_estimate=cost(3),
    )(*lefts, *rights)


def head_lanes(source, start, device):
    size = LANES // 2
    at = [start + ((2 * (device & 1) + n) * (INNER // 2) + (device >> 1)) * size for n in (0, 1)]
    return jnp.concatenate([source[:, a : a + size] for a in at], axis=1)


def cut_self_kernel(raw, out):
    width = INNER * LANES
    for device in range(INNER):
        for kind in range(3):
            at = slice(kind * LANES, (kind + 1) * LANES)
            out[device, :, at] = head_lanes(raw, kind * width, device)
        out[device, :, 3 * LANES :] = raw[:, 4 * width :]


def cut_self(raw):
    rows = raw.shape[0]
    return pl.pallas_call(
        cut_self_kernel,
        out_shape=jax.ShapeDtypeStruct((INNER, rows, 4 * LANES), LOW),
        in_specs=[VMEM],
        out_specs=VMEM,
        compiler_params=room(16),
        cost_estimate=cost(2),
    )(raw)


def cut_other_kernel(hidden, pair_weight, query, first, out):
    width = INNER * LANES
    groups = first.shape[1] // (INNER * hidden)
    for device in range(INNER):
        for kind, source in enumerate((pair_weight, pair_weight, query)):
            at = slice(kind * LANES, (kind + 1) * LANES)
            out[device, :, at] = head_lanes(source, (kind % 2) * width, device)
        for n in range(groups):
            at = (n * INNER + device) * hidden
            start = 3 * LANES + n * hidden
            out[device, :, start : start + hidden] = first[:, at : at + hidden]


def cut_other(pair_weight, query, first, hidden):
    rows = query.shape[0]
    lanes = 3 * LANES + first.shape[1] // INNER
    return pl.pallas_call(
        functools.partial(cut_other_kernel, hidden),
        out_shape=jax.ShapeDtypeStruct((INNER, rows, lanes), LOW),
        in_specs=[VMEM] * 3,
        out_specs=VMEM,
        compiler_params=room(16),
        cost_estimate=cost(1),
    )(pair_weight, query, first)


def pick_rows_kernel(start, table, raw, own, give, marks):
    width = own.shape[2]
    copies = []
    for n, out in enumerate((own, give)):
        source = raw.at[pl.ds(table[n], 2), :, pl.ds(start, width)]
        copies.append(pltpu.make_async_copy(source, out, marks.at[n]))
    for copy in copies:
        copy.start()
    finish(copies)


def pick_rows(table, start, raw, width):
    part = jax.ShapeDtypeStruct((2, raw.shape[1], width), LOW)
    return pl.pallas_call(
        functools.partial(pick_rows_kernel, start),
        out_shape=(part, part),
        in_specs=[SMEM, HBM],
        out_specs=(VMEM,) * 2,
        scratch_shapes=[pltpu.SemaphoreType.DMA((2,))],
        compiler_params=room(16),
        cost_estimate=cost(1),
    )(table, raw)


def pick_kernel(table, packed, own, give):
    share = own.shape[1]
    for first, out in ((table[0], own), (table[1], give)):
        for n in range(2):
            for place in range(INNER):
                at = pl.multiple_of(((first + n) * INNER + place) * share, share)
                out[n, :, place * LANES : (place + 1) * LANES] = packed[pl.ds(at, share), :]


def pick(table, packed):
    width = packed.shape[0]
    part = jax.ShapeDtypeStruct((2, width // (4 * INNER), width), LOW)
    return pl.pallas_call(
        pick_kernel,
        out_shape=(part, part),
        in_specs=[SMEM, VMEM],
        out_specs=(VMEM,) * 2,
        compiler_params=room(16),
        cost_estimate=cost(1),
    )(table, packed)


def merge_kernel(table, own, took, out):
    share = own.shape[1]
    for n in range(2):
        for core, value in ((table[2], own), (table[3], took)):
            first = pl.multiple_of((2 * n + core) * share, share)
            out[pl.ds(first, share), :] = value[n]


def merge(table, own, took):
    _, rows, width = own.shape
    return pl.pallas_call(
        merge_kernel,
        out_shape=jax.ShapeDtypeStruct((4 * rows, width), LOW),
        in_specs=[SMEM, VMEM, VMEM],
        out_specs=VMEM,
        compiler_params=room(16),
        cost_estimate=cost(1),
    )(table, own, took)


def pack_kernel(table, columns, *refs):
    rows, out = refs[:-1], refs[-1]
    lanes = columns.shape[1]
    out[:, :lanes] = columns[...]
    share = rows[0].shape[1]
    for kind in range(len(rows) // 2):
        for first, value in ((table[0], rows[2 * kind]), (table[1], rows[2 * kind + 1])):
            for n in range(2):
                for place in range(INNER):
                    at = pl.multiple_of(((first + n) * INNER + place) * share, share)
                    start = lanes + kind * LANES
                    block = value[n, :, place * LANES : (place + 1) * LANES]
                    out[pl.ds(at, share), start : start + LANES] = block


def pack(table, columns, *rows):
    width, lanes = columns.shape
    lanes += LANES * len(rows) // 2
    return pl.pallas_call(
        pack_kernel,
        out_shape=jax.ShapeDtypeStruct((width, lanes), LOW),
        in_specs=[SMEM] + [VMEM] * (1 + len(rows)),
        out_specs=VMEM,
        compiler_params=room(16),
        cost_estimate=cost(2),
    )(table, columns, *rows)


def hop(value, distance):
    route = [(n, n ^ distance) for n in range(INNER)]
    return lax.ppermute(value, "inner", route)


def after(value, *others):
    return lax.optimization_barrier((value,) + others)[0]


def gather_places(own, *filler):
    near = [own] + [hop(own, offset_of(place)) for place in (1, 2, 3)]
    if filler:
        near, filler = lax.optimization_barrier((near, filler))
    pieces = near + [hop(piece, 1) for piece in near]
    return (pieces, *filler) if filler else pieces


def scatter_start(give, keep):
    return fold(keep, hop(give, 1))


def scatter_finish(parts):
    return [hop(part, offset_of(place)) for place, part in enumerate(parts, 1)]


def scatter_places(give, keep):
    own, *parts = scatter_start(give, keep)
    return own, scatter_finish(parts)


def dot(a, b):
    return jnp.dot(a, b, preferred_element_type=WIDE)


def under(a, b):
    return lax.dot_general(a, b, (((0,), (0,)), ((), ())), preferred_element_type=WIDE)


def per_device(
    target,
    source,
    cotangent,
    target_lengths,
    source_lengths,
    self_in,
    self_out,
    cross_query,
    cross_kv,
    cross_out,
    mlp_in,
    mlp_out,
    vectors,
    hidden_bias,
):
    rows, width = target.shape[1:]
    here = lax.axis_index("inner")
    core, chip = here & 1, here >> 1
    stream = lax.axis_index("ulys")
    group = lax.axis_index("outer")
    groups = lax.axis_size("outer")
    shares = lax.axis_size("ulys") * groups
    devices = shares * INNER
    span = rows * INNER
    pair = width // INNER
    size = pair // 2
    share = width // devices
    hidden = hidden_bias.shape[0]
    count = vectors.shape[0]
    chips = INNER // 2
    matched = shares * chips == HEADS and 2 * share == size
    target_ends = jnp.cumsum(target_lengths[stream])
    source_ends = jnp.cumsum(source_lengths[stream])
    start = jnp.stack([here, group * span]).astype(jnp.int32)
    cores = jnp.stack([core, 1 - core])
    self_table = jnp.concatenate([start, target_ends, target_ends, cores]).astype(jnp.int32)
    cross_table = jnp.concatenate([start, target_ends, source_ends, cores]).astype(jnp.int32)
    if matched:
        head_at = [(2 * core + n) * (width // shares) + chip * size for n in (0, 1)]
    else:
        head_at = [here * pair + n * size for n in (0, 1)]
    head_table = jnp.stack(head_at).astype(jnp.int32)

    def by_device(value):
        lead = value.shape[:-1]
        if matched:
            split = value.reshape(lead + (2, 2, chips, size))
            value = jnp.moveaxis(split, -2, -4)
        return value.reshape(lead + (INNER, pair))

    def by_column(value):
        lead = value.shape[:-2]
        if matched:
            split = value.reshape(lead + (chips, 2, 2, size))
            value = jnp.moveaxis(split, -4, -2)
        return value.reshape(lead + (width,))

    def cut_columns(*weights):
        whole = jnp.concatenate([w.reshape(share, -1, width) for w in weights], axis=1)
        cut = jnp.transpose(by_device(whole), (2, 0, 1, 3))
        return cut.reshape(INNER, share, -1)

    def exchange(value):
        return lax.all_to_all(value, "inner", 0, 0)

    order = here ^ jnp.array([offset_of(n) for n in range(INNER)], jnp.int32)

    core_table = jnp.stack([2 * core, 2 - 2 * core, core, 1 - core]).astype(jnp.int32)

    def head_rows(weight, found):
        if not matched:
            whole = lax.all_gather(weight, ALL, axis=0, tiled=True)
            return lax.dynamic_slice_in_dim(whole, here * pair, pair, axis=0)
        own, give = found()
        return merge(core_table, own, hop(give, 1))

    def shard_features(pieces):
        whole = jnp.stack(
            [
                piece.reshape(INNER, rows, pair)[jnp.array([n ^ place for n in range(INNER)])]
                for place, piece in enumerate(pieces)
            ]
        ).reshape(INNER, span, pair)
        whole = jnp.transpose(whole, (1, 0, 2)).reshape(span, width)
        cut = []
        for n in range(shares):
            first = (n * INNER + here) * share
            mixed = (first // pair) ^ here
            place = ((mixed >> 1) & 3) | ((mixed & 1) << 2)
            cut.append(
                lax.dynamic_slice_in_dim(whole, place * pair + first % pair, share, axis=1)
            )
        return jnp.concatenate(cut, axis=1)

    def row_grads(parts, pieces, branch):
        if not matched:
            grad = under(shard_features(pieces), jnp.concatenate(branch, axis=0))
            return [grad.astype(LOW).reshape(shares, share, width)]
        return [parts[0], hop(parts[1], 1)]

    def pack_grads(columns, *rows):
        if matched:
            return pack(core_table, columns, *[part for parts in rows for part in parts])
        lined = [
            jnp.transpose(parts[0].reshape(shares, share, INNER, LANES), (0, 2, 1, 3))
            for parts in rows
        ]
        return jnp.concatenate([columns] + [r.reshape(width, LANES) for r in lined], axis=1)

    def lanes_to_columns(got):
        kinds = got.shape[2] // pair
        got = got.reshape(INNER, share, kinds, pair).astype(WIDE)
        return jnp.transpose(got, (1, 2, 0, 3)).reshape(share, kinds * width)

    def lanes_to_rows(packed, start):
        rows = packed[:, start : start + LANES].reshape(INNER, share, LANES).astype(WIDE)
        return jnp.transpose(rows, (1, 0, 2)).reshape(share, width)

    small = jnp.concatenate([jnp.transpose(vectors), hidden_bias.reshape(share, -1)], axis=1)
    extras = small.shape[1]
    small = jnp.pad(small, ((0, 0), (0, LANES - extras)))
    def over(value):
        return lax.all_gather(value, OUTER, axis=0)

    def row_lanes(weight):
        return jnp.transpose(weight.reshape(-1, INNER, LANES), (1, 0, 2))

    raw = over(jnp.concatenate([self_in, self_out, small], axis=1))
    if matched:
        other = exchange(cut_other(cross_kv, cross_query, mlp_in, hidden))
    else:
        first_cut = jnp.transpose(mlp_in.reshape(share, shares, INNER, hidden), (2, 0, 1, 3))
        first_cut = first_cut.reshape(INNER, share, shares * hidden)
        other = [cut_columns(cross_kv, cross_query), first_cut]
        other = exchange(jnp.concatenate(other, axis=2))
    pieces = gather_places(after(target[0], other))
    cross_far = jnp.concatenate([other[:, :, : 3 * pair], row_lanes(cross_out)], axis=2)
    cross_far = over(after(cross_far, raw, *pieces[1:4])).reshape(width, -1)
    first_mine = other[:, :, 3 * pair :].reshape(INNER * share, -1)
    feed_mine = jnp.concatenate([first_mine, mlp_out], axis=0)

    raw = after(raw, *pieces[1:4])
    if matched:
        self_far = exchange(cut_self(raw.reshape(shares * share, -1)))
        self_far = self_far.reshape(INNER, shares, share, -1)
    else:
        cut = by_device(raw[:, :, : 3 * width].reshape(shares, share, 3, width))
        cut = jnp.transpose(cut, (3, 0, 1, 2, 4)).reshape(INNER, shares, share, 3 * pair)
        extra = jnp.broadcast_to(raw[None, :, :, 4 * width :], (INNER, shares, share, LANES))
        self_far = exchange(jnp.concatenate([cut, extra], axis=3))
        self_far = jnp.transpose(self_far, (1, 0, 2, 3)).reshape(1, 1, width, -1)
    q, k, v, h1, params, biases, self_packed, x_all = enter(head_table, rows, pieces, self_far)
    states, q = gather_places(after(source[0], self_far), q)
    raw = after(raw, q)
    feed_packed = over(after(feed_mine, cross_far, q))
    sout_mine = head_rows(self_out, lambda: pick_rows(core_table, 3 * width, raw, width))
    q = after(q, sout_mine)
    h_bias = self_packed.reshape(shares, INNER, share, -1)
    h_bias = h_bias[..., 3 * pair + count : 3 * pair + extras]
    h_bias = lax.dynamic_index_in_dim(h_bias, here, 1, False).reshape(1, -1).astype(WIDE)

    def stream_keys(own):
        return lax.all_gather(own, "outer", axis=0, tiled=True) if groups > 1 else own

    def own_keys(partial):
        if groups == 1:
            return partial
        return lax.psum_scatter(partial, "outer", scatter_dimension=0, tiled=True)

    k, v = stream_keys(k), stream_keys(v)
    att, self_total = attend(self_table, q, k, v, rows, True)
    w_sout, att = gather_places(sout_mine, att)
    cross_far = after(cross_far, att)
    cout_mine = head_rows(cross_out, lambda: pick(core_table, cross_far[:, 3 * pair :]))
    states, ck, cv, cross_packed = pair_heads(rows, states, cross_far, biases)
    att, cout_mine, states, ck, cv, cross_packed = gather_places(
        att, cout_mine, states, ck, cv, cross_packed
    )
    ck, cv = stream_keys(ck), stream_keys(cv)
    y1, h2, y1_all, cq = join_self(att, w_sout, x_all, params, cross_packed, biases)
    w_cout, y1, h2, y1_all, cq = gather_places(
        after(cout_mine, *att[1:4]), y1, h2, y1_all, cq
    )
    catt, cross_total = attend(cross_table, cq, ck, cv, rows, False)
    catt = gather_places(catt)
    y2, h3 = join_cross(catt, w_cout, y1_all, y1, params)
    pull_up, y2, h3 = gather_places(after(cotangent[0], *catt[1:4]), y2, h3)
    active, before_grad, give, keep, h_bias_grad, up = feed(h3, h_bias, feed_packed, pull_up)
    third_own, third_parts = scatter_places(give, keep)
    mlp_grad = feed_grad(active, before_grad, after(h3, third_own), up)
    third_parts, mlp_grad = lax.optimization_barrier((third_parts, mlp_grad))
    mlp_home = lax.psum_scatter(mlp_grad, OUTER, scatter_dimension=0, tiled=True)
    late_grad, cross_branch, late_sums = norm_back(
        4, third_own, third_parts, y2, cotangent[0], params
    )
    cross_all = gather_places(cross_branch)
    give, keep, dcq, dck, dcv, cross_sums, *cross_rows = attend_back(
        cross_table,
        cq,
        ck,
        cv,
        cross_total,
        cout_mine,
        catt[0],
        cross_all,
        rows,
        False,
        (2, cross_packed),
    )
    dck, dcv = own_keys(dck), own_keys(dcv)
    second_own, second_parts = scatter_places(give, keep)
    cross_grad = column_part((after(states, second_own), (dck, dcv)), (h2, (dcq,)))
    side_give, side_keep = side_out(
        after(active, second_own), feed_packed, dck, dcv, cross_packed
    )
    second_parts, cross_grad, side_give, side_keep = lax.optimization_barrier(
        (second_parts, cross_grad, side_give, side_keep)
    )
    cross_rows = row_grads(cross_rows, catt, cross_all)
    middle_grad, self_branch, middle_sums = norm_back(
        2, second_own, second_parts, y1, late_grad, params
    )
    packed_grad = pack_grads(cross_grad, cross_rows)
    side_own, *side_parts = scatter_start(after(side_give, self_branch), side_keep)
    self_all, packed_grad, side_own, side_parts = gather_places(
        self_branch, packed_grad, side_own, side_parts
    )
    self_all, packed_grad, side_parts = lax.optimization_barrier(
        (self_all, packed_grad, side_parts)
    )
    side_parts = scatter_finish(side_parts)
    cross_sum = lax.psum_scatter(packed_grad, OUTER, scatter_dimension=0, tiled=True)
    made = attend_back(
        self_table,
        q,
        k,
        v,
        self_total,
        sout_mine,
        att[0],
        self_all,
        rows,
        True,
        (0, self_packed, x_all) if groups == 1 else None,
    )
    dq, dk, dv, self_sums, *self_rows = made[-6:]
    dk, dv = own_keys(dk), own_keys(dv)
    if groups == 1:
        give, keep, target_sums = made[:3]
    else:
        give, keep, target_sums = spread_self(dq, dk, dv, self_packed, x_all)
    head_sums = jnp.concatenate([self_sums, cross_sums])[:, None]
    head_sums = lax.dynamic_update_slice_in_dim(
        jnp.zeros((4, INNER, pair), WIDE), head_sums, here, 1
    )
    vector_grad = jnp.concatenate(
        [
            target_sums[:2],
            middle_sums[:2],
            late_sums[:2],
            by_column(head_sums)[:2],
            middle_sums[2:3],
            by_column(head_sums)[2:],
            late_sums[2:],
        ]
    )
    vector_part = jnp.transpose(vector_grad.reshape(count, devices, share), (1, 0, 2))
    bias_part = lax.dynamic_update_slice_in_dim(
        jnp.zeros((shares, INNER, hidden), WIDE), h_bias_grad.reshape(shares, 1, hidden), here, 1
    ).reshape(devices, hidden)
    tiny = jnp.concatenate([vector_part.reshape(devices, -1), bias_part], axis=1)
    give, side_parts, mlp_home = lax.optimization_barrier((give, side_parts, mlp_home))
    first_own, *first_parts = scatter_start(give, keep)
    first_parts = scatter_finish(first_parts)
    self_grad = column_part((after(h1, first_own), (dq, dk, dv)))
    self_rows = row_grads((self_rows[0], after(self_rows[1], first_own)), att, self_all)
    packed_grad = pack_grads(self_grad, self_rows)
    self_sum = lax.psum_scatter(packed_grad, OUTER, scatter_dimension=0, tiled=True)
    tiny = lax.all_to_all(after(tiny, packed_grad), ALL, 0, 0, tiled=True)
    first_parts, tiny = lax.optimization_barrier((first_parts, tiny))
    tiny = jnp.sum(tiny, axis=0)
    target_grad, target_low, _ = norm_back(
        0, first_own, first_parts, target[0], middle_grad, params
    )
    side_own, mlp_home, cross_sum = lax.optimization_barrier(
        (side_own, mlp_home, cross_sum, first_parts)
    )[:3]
    layer_out, source_grad = side_sum(side_own, side_parts, y2, params)
    cross_lanes = cross_sum[:, : 3 * pair].reshape(INNER, share, -1)
    first_lanes = mlp_home[:, width:].reshape(INNER, share, -1)
    cross_got = exchange(jnp.concatenate([cross_lanes, first_lanes], axis=2))
    self_got = exchange(self_sum[:, : 3 * pair].reshape(INNER, share, -1))
    if matched:
        cross_home, cout_home, first_home, second_home = home_feed(
            3, hidden, cross_got, cross_sum, mlp_home
        )
        self_home, sout_home = home(self_got, self_sum)
    else:
        cross_home = lanes_to_columns(cross_got[:, :, : 3 * pair])
        first_home = cross_got[:, :, 3 * pair :].reshape(INNER, share, shares, hidden)
        first_home = jnp.transpose(first_home, (1, 2, 0, 3)).reshape(share, -1).astype(WIDE)
        second_home = mlp_home[:, :width].astype(WIDE)
        cout_home = lanes_to_rows(cross_sum, 3 * pair)
        sout_home = lanes_to_rows(self_sum, 3 * pair)
        self_home = lanes_to_columns(self_got)

    return (
        layer_out[None],
        target_low[None],
        source_grad[None],
        self_home,
        sout_home,
        cross_home[:, 2 * width :],
        cross_home[:, : 2 * width],
        cout_home,
        first_home,
        second_home,
        tiny[: count * share].reshape(count, share),
        tiny[count * share :],
    )


def solution(mesh):
    streams, blocks = mesh.devices.shape
    grid = mesh.devices.reshape(streams, blocks // INNER, INNER)
    inner_mesh = Mesh(grid, ALL)
    rows = P("ulys", ("outer", "inner"), None)
    matrix = P(ALL, None)
    row_vectors = P(None, ALL)
    in_specs = (rows,) * 3 + (P(), P()) + (matrix,) * 7 + (row_vectors, P(ALL))
    out_specs = (rows,) * 3 + (matrix,) * 7 + (row_vectors, P(ALL))
    return jax.shard_map(
        per_device, mesh=inner_mesh, in_specs=in_specs, out_specs=out_specs, check_vma=False
    )
```
